128 devices in a mesh: dp: 32 (over x, z, core), fsdp: 4 (over y).
Axes of the slice: x: 4, y: 4, z: 4, core: 2. Of those that a mesh axis runs over, the one named last changes fastest.
Arguments:
- tokens: bfloat16 [16384, 1024], P(('dp', 'fsdp')), may hold values from -6 to 6
- seq_lengths: int32 [256], replicated, may hold values from 1 to 127, as said below
- seq_owner: int32 [256], replicated, may hold values from 0 to 127, as said below
- input_norm: bfloat16 [1, 1024], P(None, ('dp', 'fsdp')), may hold values from 0.5 to 1.5
- gate_proj: bfloat16 [1, 1024, 1536], P(None, ('dp', 'fsdp')), may hold values from -0.1875 to 0.1875
- inner_proj: bfloat16 [1, 1024, 1792], P(None, ('dp', 'fsdp')), may hold values from -0.1875 to 0.1875
- step_proj: bfloat16 [1, 1024, 24], P(None, ('dp', 'fsdp')), may hold values from -0.1875 to 0.1875
- conv_weight: bfloat16 [1, 4, 1792], P(None, None, ('dp', 'fsdp')), may hold values from -0.5 to 0.5
- conv_bias: bfloat16 [1, 1792], P(None, ('dp', 'fsdp')), may hold values from -0.5 to 0.5
- step_bias: bfloat16 [1, 24], replicated, may hold values from -5 to -1
- decay_log: bfloat16 [1, 24], replicated, may hold values from 0 to 2.765625
- skip_gain: bfloat16 [1, 24], replicated, may hold values from 0.5 to 1.5
- mixer_norm: bfloat16 [1, 1536], P(None, ('dp', 'fsdp')), may hold values from 0.5 to 1.5
- mixer_out: bfloat16 [1, 1536, 1024], P(None, None, ('dp', 'fsdp')), may hold values from -0.15625 to 0.15625
- query_proj: bfloat16 [1, 1024, 512], P(None, ('dp', 'fsdp')), may hold values from -0.1875 to 0.1875
- keyval_proj: bfloat16 [1, 1024, 256], P(None, ('dp', 'fsdp')), may hold values from -0.1875 to 0.1875
- attn_out: bfloat16 [1, 512, 1024], P(None, None, ('dp', 'fsdp')), may hold values from -1.5 to 1.5
- ffn_norm: bfloat16 [1, 1024], P(None, ('dp', 'fsdp')), may hold values from 0.5 to 1.5
- gateup_proj: bfloat16 [1, 1024, 4096], P(None, ('dp', 'fsdp')), may hold values from -0.1875 to 0.1875
- down_proj: bfloat16 [1, 2048, 1024], P(None, None, ('dp', 'fsdp')), may hold values from -0.125 to 0.125
- out_grad: bfloat16 [16384, 1024], P(('dp', 'fsdp')), may hold values from -6 to 6
Outputs:
- result: bfloat16 [16384, 1024], P(('dp', 'fsdp'))
- tokens_grad: float32 [16384, 1024], P(('dp', 'fsdp'))
- input_norm_grad: float32 [1, 1024], P(None, ('dp', 'fsdp'))
- gate_proj_grad: float32 [1, 1024, 1536], P(None, ('dp', 'fsdp'))
- inner_proj_grad: float32 [1, 1024, 1792], P(None, ('dp', 'fsdp'))
- step_proj_grad: float32 [1, 1024, 24], P(None, ('dp', 'fsdp'))
- conv_weight_grad: float32 [1, 4, 1792], P(None, None, ('dp', 'fsdp'))
- conv_bias_grad: float32 [1, 1792], P(None, ('dp', 'fsdp'))
- step_bias_grad: float32 [1, 24], replicated
- decay_log_grad: float32 [1, 24], replicated
- skip_gain_grad: float32 [1, 24], replicated
- mixer_norm_grad: float32 [1, 1536], P(None, ('dp', 'fsdp'))
- mixer_out_grad: float32 [1, 1536, 1024], P(None, None, ('dp', 'fsdp'))
- query_proj_grad: float32 [1, 1024, 512], P(None, ('dp', 'fsdp'))
- keyval_proj_grad: float32 [1, 1024, 256], P(None, ('dp', 'fsdp'))
- attn_out_grad: float32 [1, 512, 1024], P(None, None, ('dp', 'fsdp'))
- ffn_norm_grad: float32 [1, 1024], P(None, ('dp', 'fsdp'))
- gateup_proj_grad: float32 [1, 1024, 4096], P(None, ('dp', 'fsdp'))
- down_proj_grad: float32 [1, 2048, 1024], P(None, None, ('dp', 'fsdp'))
The draws below stay inside these ranges and needn't reach their ends.
Inputs may be any that keep to these rules, and one draw needn't show every extreme that they name: `seq_lengths`: the two sequences of a device hold at least 64 and at most 128 tokens together; some device holds exactly 128. `seq_owner`: every device owns exactly two sequences.
All inputs are finite; a program needn't handle non-finite values.
Results may differ from the reference program's by a relative error of at most 0.012.
Values may be sent and summed in bfloat16 or wider, within the bound.
A program may use at most 192 MiB of HBM per device.

```python
import math
import jax
import jax.numpy as jnp
from jax import lax

D = 1024
HEADS = 24
CONV = 4
QH = 8
KVH = 2
FF = 2048
LAYERS = 1
SLOTS = 128
DI = 1536
XBC = 1792
QW = 512
KW = 128
SEQS = 256
TOKENS = 16384


def deal_sequences(key):
    device_count = SEQS // 2
    fill_key, hub_key, cut_key, order_key = jax.random.split(key, 4)
    filled = jax.random.randint(fill_key, (device_count,), SLOTS // 2, SLOTS + 1)
    chosen = jax.random.randint(hub_key, (), 0, device_count)
    device_ids = jnp.arange(device_count)
    filled = jnp.where(device_ids == chosen, SLOTS, filled)
    raw_cut = jax.random.randint(cut_key, (device_count,), 0, 1 << 20)
    first_length = 1 + raw_cut % (filled - 1)
    first_length = jnp.where(device_ids == chosen, SLOTS - 1, first_length)
    paired = jnp.stack([first_length, filled - first_length], axis=1).reshape(SEQS)
    owners = jnp.repeat(device_ids, 2)
    order = jax.random.permutation(order_key, SEQS)
    return (paired[order].astype(jnp.int32), owners[order].astype(jnp.int32))


def draw_seq_lengths(key, part):
    return deal_sequences(key)[0]


def draw_seq_owner(key, part):
    return deal_sequences(key)[1]


def level_of(own_key, extent, cuts, low, top_value):
    level = 1.0
    for axis_at, parts in cuts:
        draws = jax.random.uniform(jax.random.fold_in(jax.random.fold_in(own_key, 6), axis_at), (parts,), jnp.float32, low / len(cuts), top_value / len(cuts))
        level = level * jnp.repeat(jnp.exp(draws), extent[axis_at] // parts).reshape((-1,) + (1,) * (len(extent) - 1 - axis_at))
    return level


def bell_draw(key, dims, deviation, reach, cuts=(), held_as=jnp.bfloat16):
    drawn = jax.random.normal(key, dims, jnp.float32) * deviation
    if len(cuts) > 0:
        drawn = level_of(key, dims, cuts, -0.22, 0.18) * drawn
    return jnp.clip(drawn, min=-reach, max=reach).astype(held_as)


def setup_inputs(seed: int = 0) -> dict:
    key_list = jax.random.split(jax.random.key(seed), 22)
    tokens = bell_draw(key_list[0], (TOKENS, D), 1.0, 6.0, ((0, 128),))
    seq_lengths = draw_seq_lengths(jax.random.fold_in(key_list[21], 71), 0)
    seq_owner = draw_seq_owner(jax.random.fold_in(key_list[21], 71), 0)
    input_norm = jnp.clip(1.0 + 0.1 * jax.random.normal(key_list[3], (LAYERS, D), jnp.float32), 0.5, 1.5).astype(jnp.bfloat16)
    gate_proj = bell_draw(key_list[4], (LAYERS, D, DI), D ** -0.5, 0.1875, ((1, 128),))
    inner_proj = bell_draw(key_list[5], (LAYERS, D, XBC), D ** -0.5, 0.1875, ((1, 128),))
    step_proj = bell_draw(key_list[6], (LAYERS, D, HEADS), D ** -0.5, 0.1875, ((1, 128),))
    conv_weight = jnp.clip(jax.random.uniform(key_list[7], (LAYERS, CONV, XBC), jnp.float32, -0.5, 0.5) * level_of(key_list[7], (LAYERS, CONV, XBC), ((2, 128),), -0.4, 0.0), -0.5, 0.5).astype(jnp.bfloat16)
    conv_bias = jnp.clip(jax.random.uniform(key_list[8], (LAYERS, XBC), jnp.float32, -0.5, 0.5) * level_of(key_list[8], (LAYERS, XBC), ((1, 128),), -0.4, 0.0), -0.5, 0.5).astype(jnp.bfloat16)
    step_bias = jnp.clip(jax.random.uniform(key_list[9], (LAYERS, HEADS), jnp.float32, -5.0, -1.0), -5.0, -1.0).astype(jnp.bfloat16)
    decay_log = jnp.clip(jax.random.uniform(key_list[10], (LAYERS, HEADS), jnp.float32, 0.0, 2.765625), 0.0, 2.765625).astype(jnp.bfloat16)
    skip_gain = jnp.clip(jax.random.uniform(key_list[11], (LAYERS, HEADS), jnp.float32, 0.5, 1.5), 0.5, 1.5).astype(jnp.bfloat16)
    mixer_norm = jnp.clip(1.0 + 0.1 * jax.random.normal(key_list[12], (LAYERS, DI), jnp.float32), 0.5, 1.5).astype(jnp.bfloat16)
    mixer_out = bell_draw(key_list[13], (LAYERS, DI, D), DI ** -0.5, 0.15625, ((2, 128),))
    query_proj = bell_draw(key_list[14], (LAYERS, D, QW), D ** -0.5, 0.1875, ((1, 128),))
    keyval_proj = bell_draw(key_list[15], (LAYERS, D, 2 * KW), D ** -0.5, 0.1875, ((1, 128),))
    attn_out = bell_draw(key_list[16], (LAYERS, QW, D), (QW // 32) ** -0.5, 1.5, ((2, 128),))
    ffn_norm = jnp.clip(1.0 + 0.1 * jax.random.normal(key_list[17], (LAYERS, D), jnp.float32), 0.5, 1.5).astype(jnp.bfloat16)
    gateup_proj = bell_draw(key_list[18], (LAYERS, D, 2 * FF), D ** -0.5, 0.1875, ((1, 128),))
    down_proj = bell_draw(key_list[19], (LAYERS, FF, D), FF ** -0.5, 0.125, ((2, 128),))
    out_grad = bell_draw(key_list[20], (TOKENS, D), 1.0, 6.0, ((0, 128),))
    return dict(tokens=tokens, seq_lengths=seq_lengths, seq_owner=seq_owner, input_norm=input_norm, gate_proj=gate_proj, inner_proj=inner_proj, step_proj=step_proj, conv_weight=conv_weight, conv_bias=conv_bias, step_bias=step_bias, decay_log=decay_log, skip_gain=skip_gain, mixer_norm=mixer_norm, mixer_out=mixer_out, query_proj=query_proj, keyval_proj=keyval_proj, attn_out=attn_out, ffn_norm=ffn_norm, gateup_proj=gateup_proj, down_proj=down_proj, out_grad=out_grad)


@jax.custom_vjp
def low(v):
    return lax.optimization_barrier(v.astype(jnp.bfloat16)).astype(jnp.float32)

@jax.custom_vjp
def low_back(v):
    return v

def low_keep(v):
    return (low(v), None)

def low_pass(kept, grad):
    return (grad,)

def back_keep(v):
    return (v, None)

def back_low(kept, grad):
    return (low(grad),)
low.defvjp(low_keep, low_pass)
low_back.defvjp(back_keep, back_low)
EPSILON = 1e-05
ROPE_BASE = 100000000000.0

def matmul_high(left_side, right_side):
    return jnp.dot(left_side, right_side, preferred_element_type=jnp.float32, precision=lax.Precision.HIGHEST)

def rms_scale(values, gain):
    return values * lax.rsqrt(lax.optimization_barrier(jnp.mean(values * values, axis=-1, keepdims=True)) + EPSILON) * gain

def layout(device, seq_lengths, seq_owner, slot_count):
    owned = seq_owner == device
    own_lengths = jnp.where(owned, seq_lengths, 0).astype(jnp.int32)
    finish = jnp.cumsum(own_lengths, dtype=jnp.int32)
    slot_ids = jnp.arange(slot_count, dtype=jnp.int32)
    closed = owned[None, :] & (finish[None, :] <= slot_ids[:, None])
    segment = lax.optimization_barrier(jnp.sum(closed.astype(jnp.int32), axis=1, dtype=jnp.int32))
    begins = lax.optimization_barrier(jnp.max(jnp.where(closed, finish[None, :], 0), axis=1)).astype(jnp.int32)
    active = slot_ids < jnp.sum(own_lengths, dtype=jnp.int32)
    return (segment, slot_ids - begins, active)

def rotate(values, position, head_count):
    row_count = values.shape[0]
    model_width = values.shape[1] // head_count
    half_width = model_width // 2
    ladder = jnp.arange(half_width, dtype=jnp.float32) * (2.0 / model_width)
    speeds = jnp.exp(-math.log(ROPE_BASE) * ladder)
    angles = position.astype(jnp.float32)[:, None] * speeds[None, :]
    cosine = jnp.cos(angles)[:, None, :]
    sine_part = jnp.sin(angles)[:, None, :]
    pieces = values.reshape(row_count, head_count, model_width)
    former = pieces[..., :half_width]
    latter = pieces[..., half_width:]
    turned = jnp.concatenate([former * cosine - latter * sine_part, latter * cosine + former * sine_part], axis=-1)
    return turned.reshape(row_count, head_count * model_width)

def attend(queries, keys, values, segment):
    row_count = queries.shape[0]
    group_size = QH // KVH
    model_width = keys.shape[1] // KVH
    query_rank_four = queries.reshape(row_count, KVH, group_size, model_width)
    key_rank_three = keys.reshape(row_count, KVH, model_width)
    value_rank_three = values.reshape(row_count, KVH, model_width)
    attention_scores = jnp.einsum('owhp,xwp->whox', query_rank_four, key_rank_three, precision=lax.Precision.HIGHEST) * (1.0 / math.sqrt(model_width))
    slot_ids = jnp.arange(row_count)
    allowed = (segment[:, None] == segment[None, :]) & (slot_ids[:, None] >= slot_ids[None, :])
    attention_scores = jnp.where(allowed, attention_scores, -1e+30)
    highest = lax.optimization_barrier(jnp.max(attention_scores, axis=-1, keepdims=True))
    attention_weights = jnp.exp(attention_scores - highest)
    attention_weights = attention_weights / lax.optimization_barrier(jnp.sum(attention_weights, axis=-1, keepdims=True))
    mixed_values = jnp.einsum('qmaz,zqc->aqmc', attention_weights, value_rank_three, precision=lax.Precision.HIGHEST)
    return mixed_values.reshape(row_count, KVH * group_size * model_width)

def mamba_core(gate_in, conv_in, step_in, conv_taps, conv_shift, step_shift, decay_logs, skip_coef, gain, segment, position):
    row_count = conv_in.shape[0]
    inner = gate_in.shape[1]
    head_count = step_in.shape[1]
    state_size = (conv_in.shape[1] - inner) // 2
    kernel = conv_taps.shape[0]
    summed = conv_in * conv_taps[kernel - 1]
    for offset in range(1, kernel):
        moved = jnp.pad(conv_in, ((offset, 0), (0, 0)))[:row_count]
        summed = summed + jnp.where((position >= offset)[:, None], moved, 0.0) * conv_taps[kernel - 1 - offset]
    convolved = jax.nn.silu(summed + conv_shift)
    inputs_heads = convolved[:, :inner].reshape(row_count, head_count, inner // head_count)
    b_matrix = convolved[:, inner:inner + state_size]
    c_matrix = convolved[:, inner + state_size:]
    delta = jax.nn.softplus(step_in + step_shift)
    level = jnp.cumsum(delta * -jnp.exp(decay_logs), axis=0)
    slot_ids = jnp.arange(row_count)
    allowed = ((segment[:, None] == segment[None, :]) & (slot_ids[:, None] >= slot_ids[None, :]))[None]
    spread = level.T[:, :, None] - level.T[:, None, :]
    decay = jnp.where(allowed, jnp.exp(jnp.where(allowed, spread, 0.0)), 0.0)
    intersection = matmul_high(c_matrix, b_matrix.T)
    mixing = decay * intersection[None] * delta.T[:, None, :]
    heads_out = jnp.einsum('hts,shp->thp', mixing, inputs_heads, precision=lax.Precision.HIGHEST)
    heads_out = heads_out + skip_coef[None, :, None] * inputs_heads
    gated = heads_out.reshape(row_count, inner) * jax.nn.silu(gate_in)
    return rms_scale(gated, gain)

def swiglu(joined):
    half_width = joined.shape[1] // 2
    return jax.nn.silu(joined[:, :half_width]) * joined[:, half_width:]

def layer_step(stream, params, segment, position):
    in_gain, gate_w, inner_w, step_w, conv_taps, conv_shift, step_shift, decay_logs, skip_coef, mix_gain, mix_out_w, query_w, keyval_w, attn_w, ffn_gain, gateup_w, down_w = params
    normed = low(rms_scale(stream, in_gain))
    gate_val = low_back(matmul_high(normed, gate_w))
    conv_val = low_back(matmul_high(normed, inner_w))
    step_val = low_back(matmul_high(normed, step_w))
    mixer_normed = low(mamba_core(gate_val, conv_val, step_val, conv_taps, conv_shift, step_shift, decay_logs, skip_coef, mix_gain, segment, position))
    mixer_branch = low_back(matmul_high(mixer_normed, mix_out_w))
    queries = low_back(matmul_high(normed, query_w))
    keyvals = low_back(matmul_high(normed, keyval_w))
    key_width = keyvals.shape[1] // 2
    query_turned = low(rotate(queries, position, QH))
    key_turned = low(rotate(keyvals[:, :key_width], position, KVH))
    value_low = low(keyvals[:, key_width:])
    attended = low(attend(query_turned, key_turned, value_low, segment))
    attn_branch = low_back(matmul_high(attended, attn_w))
    middle = stream + mixer_branch + attn_branch
    ffn_in = low(rms_scale(middle, ffn_gain))
    gateup = low_back(matmul_high(ffn_in, gateup_w))
    activated = low(swiglu(gateup))
    return middle + low_back(matmul_high(activated, down_w))

def reference(tokens, seq_lengths, seq_owner, input_norm, gate_proj, inner_proj, step_proj, conv_weight, conv_bias, step_bias, decay_log, skip_gain, mixer_norm, mixer_out, query_proj, keyval_proj, attn_out, ffn_norm, gateup_proj, down_proj, out_grad):
    block_count = TOKENS // SLOTS
    attention_weights = tuple((member.astype(jnp.float32) for member in (input_norm, gate_proj, inner_proj, step_proj, conv_weight, conv_bias, step_bias, decay_log, skip_gain, mixer_norm, mixer_out, query_proj, keyval_proj, attn_out, ffn_norm, gateup_proj, down_proj)))
    token_blocks = tokens.astype(jnp.float32).reshape(block_count, SLOTS, D)
    grad_blocks = out_grad.astype(jnp.float32).reshape(block_count, SLOTS, D)

    def scan_step(totals, entry):
        device, block_in, block_grad = entry
        segment, position, active = layout(device, seq_lengths, seq_owner, SLOTS)

        def whole(stream, params):
            for layer in range(LAYERS):
                stream = layer_step(stream, tuple((member[layer] for member in params)), segment, position)
            return stream
        outcome, pullback = jax.vjp(whole, block_in, attention_weights)
        input_grad, weight_grads = pullback(block_grad * active[:, None].astype(jnp.float32))
        totals = jax.tree.map(jnp.add, totals, weight_grads)
        return (totals, (outcome.astype(jnp.bfloat16), input_grad))
    zeros = jax.tree.map(jnp.zeros_like, attention_weights)
    totals, (outcomes, input_grads) = lax.scan(scan_step, zeros, (jnp.arange(block_count, dtype=jnp.int32), token_blocks, grad_blocks))
    return (outcomes.reshape(TOKENS, D), input_grads.reshape(TOKENS, D), totals[0], totals[1], totals[2], totals[3], totals[4], totals[5], totals[6], totals[7], totals[8], totals[9], totals[10], totals[11], totals[12], totals[13], totals[14], totals[15], totals[16])
```

```python
import functools
import math

import jax
import jax.numpy as jnp
from jax import lax
from jax.experimental import pallas as pl
from jax.experimental.pallas import tpu as pltpu
from jax.sharding import Mesh
from jax.sharding import PartitionSpec as P

EPSILON = 1e-05
ROPE_BASE = 100000000000.0
DP_FSDP = ("dp_0", "dp_1", "dp_2", "fsdp")
AX, AZ, AC, AY = "dp_0", "dp_1", "dp_2", "fsdp"
ORDERS = ((AX, AY, AZ), (AY, AZ, AX), (AZ, AX, AY))
MESH = pl.DeviceIdType.MESH


def places():
    return {a: lax.axis_index(a) for a in (AX, AZ, AC, AY)}


def greet(at):
    barrier = pltpu.get_barrier_semaphore()
    for a in (AX, AZ, AY):
        for d in (1, 3):
            pl.semaphore_signal(barrier, inc=1, device_id={a: lax.rem(at[a] + d, 4)}, device_id_type=MESH)
    pl.semaphore_signal(barrier, inc=1, device_id={AC: 1 - at[AC]}, device_id_type=MESH)
    pl.semaphore_wait(barrier, 7)


def cut3(cols, start=0):
    tiles = cols // 128
    sizes = [tiles // 3 + (1 if k < tiles % 3 else 0) for k in range(3)]
    parts, at = [], start
    for n in sizes:
        lo = (n + 1) // 2 * 128
        parts.append((at, lo, n * 128 - lo))
        at += n * 128
    return parts


def gather_kernel(parts, shard, out, send, recv, sib_send, sib_recv, own_sem):
    at = places()
    greet(at)
    whole = slice(None)
    core = at[AC]

    def block(sel, c0, n):
        return out.at[sel[AX], sel[AZ], core, sel[AY], :, pl.ds(c0, n)]

    own = pltpu.make_async_copy(shard, out.at[at[AX], at[AZ], core, at[AY]], own_sem)
    own.start()
    pending_sib, sent = [], []

    def to_sibling(part, k, sel, c0, n):
        ref = block(sel, c0, n)
        c = pltpu.make_async_remote_copy(ref, ref, sib_send.at[part, k], sib_recv.at[part, k],
                                         device_id={AC: 1 - core}, device_id_type=MESH)
        c.start()
        pending_sib.append(c)

    for phase in range(3):
        state = []
        for part, (c0, lo, hi) in enumerate(parts):
            order = ORDERS[part]
            a = order[phase]
            p = at[a]
            nxt, prv, opp = lax.rem(p + 1, 4), lax.rem(p + 3, 4), lax.rem(p + 2, 4)
            base = {b: at[b] for b in (AX, AZ, AY)}
            for b in order[:phase]:
                base[b] = whole

            def mk(kind, q, cc, n, to, part=part, a=a, base=base):
                dst = block({**base, a: q}, cc, n)
                src = shard.at[:, pl.ds(cc, n)] if (phase == 0 and kind < 4) else dst
                return pltpu.make_async_remote_copy(src, dst, send.at[part, phase, kind], recv.at[part, phase, kind],
                                                    device_id={a: to}, device_id_type=MESH)
            r_lo, l_hi = mk(0, p, c0, lo, nxt), mk(1, p, c0 + lo, hi, prv)
            r_hi, l_lo = mk(2, p, c0 + lo, hi, nxt), mk(3, p, c0, lo, prv)
            for c in (r_lo, l_hi, r_hi, l_lo):
                c.start()
            sent += [r_lo, l_hi, r_hi, l_lo]
            if phase == 2:
                to_sibling(part, 0, {**base}, c0, lo + hi)
            state.append((r_lo, l_hi, r_hi, l_lo, mk, nxt, prv, opp, base, a, c0, lo, hi))
        fwd = []
        for s in state:
            r_lo, l_hi, r_hi, l_lo, mk, nxt, prv, opp, base, a, c0, lo, hi = s
            r_lo.wait_recv()
            fr = mk(4, prv, c0, lo, nxt)
            fr.start()
            l_hi.wait_recv()
            fl = mk(5, nxt, c0 + lo, hi, prv)
            fl.start()
            fwd.append((fr, fl))
            sent += [fr, fl]
        for part, s in enumerate(state):
            r_lo, l_hi, r_hi, l_lo, mk, nxt, prv, opp, base, a, c0, lo, hi = s
            r_hi.wait_recv()
            if phase == 2:
                to_sibling(part, 1, {**base, a: prv}, c0, lo + hi)
            l_lo.wait_recv()
            if phase == 2:
                to_sibling(part, 2, {**base, a: nxt}, c0, lo + hi)
        for part, s in enumerate(state):
            r_lo, l_hi, r_hi, l_lo, mk, nxt, prv, opp, base, a, c0, lo, hi = s
            fr, fl = fwd[part]
            fr.wait_recv()
            if phase == 2:
                to_sibling(part, 3, {**base, a: opp}, c0, lo)
            fl.wait_recv()
            if phase == 2:
                to_sibling(part, 4, {**base, a: opp}, c0 + lo, hi)
        if phase == 0:
            own.wait()
    for c in sent:
        c.wait_send()
    for c in pending_sib:
        c.wait()


def gather(shard, space=pl.ANY, cid=0):
    cols = shard.shape[1]
    parts = cut3(cols)
    return pl.pallas_call(
        functools.partial(gather_kernel, parts),
        out_shape=jax.ShapeDtypeStruct((4, 4, 2, 4, 8, cols), jnp.bfloat16),
        in_specs=[pl.BlockSpec(memory_space=pltpu.VMEM)],
        out_specs=pl.BlockSpec(memory_space=space),
        scratch_shapes=[
            pltpu.SemaphoreType.DMA((3, 3, 6)), pltpu.SemaphoreType.DMA((3, 3, 6)),
            pltpu.SemaphoreType.DMA((3, 5)), pltpu.SemaphoreType.DMA((3, 5)), pltpu.SemaphoreType.DMA,
        ],
        compiler_params=pltpu.CompilerParams(collective_id=cid, has_side_effects=True, vmem_limit_bytes=60 << 20),
        name="gather",
    )(shard)


def shapes_of(phase, cols):
    return (4,) * (2 - phase) + (8, cols)


OFF = dict(gate=(0, 1536), inner=(1536, 1792), query=(3328, 512), keyval=(3840, 256), step=(4096, 128),
           mix=(4224, 1536), attn=(5760, 512), gateup=(6272, 4096), down=(10368, 2048))
COLS = 12416
FIRST = 4224
F32, BF16 = jnp.float32, jnp.bfloat16
HIGH = lax.Precision.HIGHEST


def nn(a, b, precision=None):
    return lax.dot_general(a, b, (((1,), (0,)), ((), ())), preferred_element_type=F32, precision=precision)


def nt(a, b, precision=None):
    return lax.dot_general(a, b, (((1,), (1,)), ((), ())), preferred_element_type=F32, precision=precision)


def tn(a, b, precision=None):
    return lax.dot_general(a, b, (((0,), (0,)), ((), ())), preferred_element_type=F32, precision=precision)


def sigmoid(v):
    return 1.0 / (1.0 + jnp.exp(-v))


def cols_of(i, n, start=0):
    return pl.ds(pl.multiple_of(start + i * n, 128), n)


def rms_back(values, scale, gain, grad):
    inner = grad * gain
    mean = jnp.mean(values * inner, axis=-1, keepdims=True)
    return scale * inner - values * (scale * scale * scale * mean), jnp.sum(grad * values * scale, axis=0, keepdims=True)


def row_scale(values):
    return lax.rsqrt(jnp.mean(values * values, axis=-1, keepdims=True) + EPSILON)


def layer_kernel(x_ref, og_ref, segc, segr, pos, act, cos, sin, w_hbm, gin, gffn, gmix, taps, cbias, sbias, dlog, skipx,
                 result, dx, rt, z, gin_g, gffn_g, gmix_g, taps_g, cbias_g, head_g, skip_g,
                 wv, proj, csum, conv, yfull, dec, soft, qr, x1_s, df_s, dm_s, do_s, dconv, ddt_s, wsem):
    groups = ((0, FIRST), (4224, 2048), (6272, 4096), (10368, 2048))
    loads = []
    for k, (c0, n) in enumerate(groups):
        c = pltpu.make_async_copy(w_hbm.at[:, pl.ds(c0, n)], wv.at[:, pl.ds(c0, n)], wsem.at[k])
        c.start()
        loads.append(c)

    lane = lax.broadcasted_iota(jnp.int32, (128, 128), 1)
    sub = lax.broadcasted_iota(jnp.int32, (128, 128), 0)
    low_lanes = lane < 64
    allowed = (segc[...] == segr[...]) & (sub >= lane)
    position = pos[...]

    def halves(v):
        return jnp.where(low_lanes, v, 0.0), jnp.where(low_lanes, 0.0, v)

    def stacked(v):
        lo, hi = halves(v)
        return jnp.concatenate([lo, hi], axis=0).astype(BF16)

    x = x_ref[...].astype(F32)
    h = (x * row_scale(x) * gin[...]).astype(BF16)
    rt[0:1024, :] = h.T
    g0 = og_ref[...].astype(F32) * act[...]
    glow = g0.astype(BF16)
    rt[3072:4096, :] = glow.T
    z_h = h
    loads[0].wait()

    def project(i, carry):
        proj[:, cols_of(i, 384)] = nn(z_h, wv[:, cols_of(i, 384)])
        return carry
    lax.fori_loop(0, 11, project, 0)

    def convolve(i, carry):
        cs = cols_of(i, 128)
        p = proj[:, cols_of(i, 128, 1536)]
        total = p * taps[3:4, cs]
        for j in (1, 2, 3):
            moved = jnp.where(position >= j, pltpu.roll(p, j, axis=0), 0.0)
            total = total + moved * taps[3 - j:4 - j, cs]
        total = total + cbias[:, cs]
        csum[:, cs] = total
        conv[:, cs] = total * sigmoid(total)
        return carry
    lax.fori_loop(0, 14, convolve, 0)

    step = proj[:, 4096:4224] + sbias[...]
    dt = jnp.maximum(step, 0.0) + jnp.log(1.0 + jnp.exp(-jnp.abs(step)))
    rate = -jnp.exp(dlog[...])
    lower = (sub >= lane).astype(F32)
    level = nn(lower, dt * rate, HIGH)
    dt_t = dt.T
    level_t = level.T
    b_mat = conv[:, 1536:1664]
    c_mat = conv[:, 1664:1792]
    inter = nt(c_mat, b_mat, HIGH)

    square = jnp.zeros((128, 1), F32)
    for t in range(12):
        cs = slice(128 * t, 128 * t + 128)
        mixes = []
        for n in (2 * t, 2 * t + 1):
            spread = jnp.where(allowed, level[:, n:n + 1] - level_t[n:n + 1, :], -1e30)
            decay = jnp.exp(spread)
            dec[n] = decay
            mixes.append((decay * inter * dt_t[n:n + 1, :]).astype(BF16))
        xs = conv[:, cs]
        y = nn(jnp.concatenate(mixes, axis=1), stacked(xs)) + skipx[:, cs] * xs
        yfull[:, cs] = y
        gate = proj[:, cs]
        gy = y * (gate * sigmoid(gate))
        square = square + jnp.sum(gy * gy, axis=1, keepdims=True)
    rmix = lax.rsqrt(square * (1.0 / 1536) + EPSILON)

    def mixer_norm(i, carry):
        cs = cols_of(i, 128)
        gate = proj[:, cs]
        gy = yfull[:, cs] * (gate * sigmoid(gate))
        z[:, cols_of(i, 128, 4224)] = (gy * rmix * gmix[:, cs]).astype(BF16)
        return carry
    lax.fori_loop(0, 12, mixer_norm, 0)

    cosine, sine = cos[...], sin[...]
    first = (lane % 64) < 32

    def turn(v, sign):
        side = jnp.where(first, -pltpu.roll(v, 96, axis=1), pltpu.roll(v, 32, axis=1))
        return v * cosine + sign * side * sine

    def dup(v, j):
        other = pltpu.roll(v, 64, axis=1)
        return jnp.where(low_lanes, v, other) if j == 0 else jnp.where(low_lanes, other, v)
    key_t = turn(proj[:, 3840:3968], 1.0).astype(BF16).astype(F32)
    val = proj[:, 3968:4096].astype(BF16).astype(F32)
    keys = [dup(key_t, j) for j in (0, 1)]
    vals = [dup(val, j) for j in (0, 1)]
    for t in range(4):
        cs = slice(128 * t, 128 * t + 128)
        q = turn(proj[:, 3328 + 128 * t:3456 + 128 * t], 1.0).astype(BF16).astype(F32)
        qr[:, cs] = q
        scores = nt(stacked(q), keys[t // 2].astype(BF16)) * 0.125
        weights = []
        for e in (0, 1):
            s = jnp.where(allowed, scores[128 * e:128 * e + 128], -1e30)
            w = jnp.exp(s - jnp.max(s, axis=1, keepdims=True))
            w = w / jnp.sum(w, axis=1, keepdims=True)
            soft[2 * t + e] = w
            weights.append(w.astype(BF16))
        z[:, 5760 + 128 * t:5888 + 128 * t] = nn(jnp.concatenate(weights, axis=1), stacked(vals[t // 2])).astype(BF16)

    loads[1].wait()
    for i in range(4):
        rows = slice(256 * i, 256 * i + 256)
        x1_s[:, rows] = x_ref[:, rows].astype(F32) + nt(z[:, 4224:6272], wv[rows, 4224:6272])
    x1 = x1_s[...]
    r1 = row_scale(x1)
    f = (x1 * r1 * gffn[...]).astype(BF16)
    rt[2048:3072, :] = f.T

    loads[2].wait()
    loads[3].wait()

    def feed(i, carry):
        g = nn(f, wv[:, cols_of(i, 256, 6272)])
        u = nn(f, wv[:, cols_of(i, 256, 8320)])
        da = nn(glow, wv[:, cols_of(i, 256, 10368)])
        s = sigmoid(g)
        gs = g * s
        z[:, cols_of(i, 256, 10368)] = (gs * u).astype(BF16)
        z[:, cols_of(i, 256, 6272)] = (da * u * (s + gs * (1.0 - s))).astype(BF16)
        z[:, cols_of(i, 256, 8320)] = (da * gs).astype(BF16)
        return carry
    lax.fori_loop(0, 8, feed, 0)
    for i in range(4):
        rows = slice(256 * i, 256 * i + 256)
        result[:, rows] = (x1_s[:, rows] + nt(z[:, 10368:12416], wv[rows, 10368:12416])).astype(BF16)
        df_s[:, rows] = nt(z[:, 6272:10368], wv[rows, 6272:10368])
    part, gain_grad = rms_back(x1, r1, gffn[...], df_s[...])
    gffn_g[...] = gain_grad
    dx1 = g0 + part
    x1_s[...] = dx1
    blow = dx1.astype(BF16)
    rt[1024:2048, :] = blow.T

    def back_branch(i, carry):
        dm_s[:, cols_of(i, 512)] = nn(blow, wv[:, cols_of(i, 512, 4224)])
        return carry
    lax.fori_loop(0, 3, back_branch, 0)
    do_s[...] = nn(blow, wv[:, 5760:6272])

    dks, dvs = [], []
    for t in range(4):
        cs = slice(128 * t, 128 * t + 128)
        do2 = stacked(do_s[:, cs])
        dp = nt(do2, vals[t // 2].astype(BF16))
        ds, ws = [], []
        for e in (0, 1):
            w = soft[2 * t + e]
            d = dp[128 * e:128 * e + 128]
            ds.append((w * (d - jnp.sum(d * w, axis=1, keepdims=True)) * 0.125).astype(BF16))
            ws.append(w.astype(BF16))
        dq = nn(jnp.concatenate(ds, axis=1), stacked(keys[t // 2]))
        z[:, 3328 + 128 * t:3456 + 128 * t] = turn(dq, -1.0).astype(BF16)
        dks.append(tn(jnp.concatenate(ds, axis=0), stacked(qr[:, cs])))
        dvs.append(tn(jnp.concatenate(ws, axis=0), do2))

    def fold(parts):
        a, b = parts[0] + parts[1], parts[2] + parts[3]
        return jnp.where(low_lanes, a + pltpu.roll(a, 64, axis=1), b + pltpu.roll(b, 64, axis=1))
    z[:, 3840:3968] = turn(fold(dks), -1.0).astype(BF16)
    z[:, 3968:4096] = fold(dvs).astype(BF16)

    dots = jnp.zeros((128, 1), F32)
    for t in range(12):
        cs = slice(128 * t, 128 * t + 128)
        gate = proj[:, cs]
        gy = yfull[:, cs] * (gate * sigmoid(gate))
        dm = dm_s[:, cs]
        gmix_g[:, cs] = jnp.sum(dm * gy * rmix, axis=0, keepdims=True)
        dots = dots + jnp.sum(gy * dm * gmix[:, cs], axis=1, keepdims=True)
    pull = rmix * rmix * rmix * dots * (1.0 / 1536)
    ddt_s[...] = jnp.zeros((128, 128), F32)
    dlevel = jnp.zeros((128, 128), F32)
    dinter = jnp.zeros((128, 128), F32)
    for t in range(12):
        cs = slice(128 * t, 128 * t + 128)
        gate = proj[:, cs]
        s = sigmoid(gate)
        gs = gate * s
        y = yfull[:, cs]
        dgy = rmix * (gmix[:, cs] * dm_s[:, cs]) - y * gs * pull
        z[:, cs] = (dgy * y * (s + gs * (1.0 - s))).astype(BF16)
        dy = dgy * gs
        xs = conv[:, cs]
        skip_g[:, cs] = jnp.sum(dy * xs, axis=0, keepdims=True)
        dy2 = stacked(dy)
        dmix = nt(dy2, xs.astype(BF16))
        mixes = []
        for e in (0, 1):
            n = 2 * t + e
            dt_row = dt_t[n:n + 1, :]
            decay = dec[n]
            mixed = decay * inter
            dm = dmix[128 * e:128 * e + 128]
            mixes.append((mixed * dt_row).astype(BF16))
            dd = dm * dt_row
            dinter = dinter + dd * decay
            ddt_s[n:n + 1, :] = jnp.sum(dm * mixed, axis=0, keepdims=True)
            dlevel = dlevel + jnp.where(lane == n, jnp.sum(dd * mixed, axis=1, keepdims=True), 0.0)
        dconv[:, cs] = tn(jnp.concatenate(mixes, axis=0), dy2) + skipx[:, cs] * dy
    dconv[:, 1536:1664] = tn(dinter, c_mat, HIGH)
    dconv[:, 1664:1792] = nn(dinter, b_mat, HIGH)
    ddt = ddt_s[...].T
    dlevel = dlevel - ddt * dt
    upper = (sub <= lane).astype(F32)
    drate = nn(upper, dlevel, HIGH)
    dstep = jnp.where(lane < 24, (ddt + drate * rate) * sigmoid(step), 0.0)
    z[:, 4096:4224] = dstep.astype(BF16)
    head_g[0:1, :] = jnp.sum(dstep, axis=0, keepdims=True)
    head_g[1:2, :] = jnp.sum(drate * dt * rate, axis=0, keepdims=True)

    def unconvolve(i, carry):
        cs = cols_of(i, 128)
        total = csum[:, cs]
        s = sigmoid(total)
        d = dconv[:, cs] * (s + total * s * (1.0 - s))
        p = proj[:, cols_of(i, 128, 1536)]
        cbias_g[:, cs] = jnp.sum(d, axis=0, keepdims=True)
        taps_g[3:4, cs] = jnp.sum(d * p, axis=0, keepdims=True)
        back = d * taps[3:4, cs]
        for j in (1, 2, 3):
            masked = jnp.where(position >= j, d, 0.0)
            taps_g[3 - j:4 - j, cs] = jnp.sum(masked * pltpu.roll(p, j, axis=0), axis=0, keepdims=True)
            back = back + pltpu.roll(masked, 128 - j, axis=0) * taps[3 - j:4 - j, cs]
        z[:, cols_of(i, 128, 1536)] = back.astype(BF16)
        return carry
    lax.fori_loop(0, 14, unconvolve, 0)

    for i in range(4):
        rows = slice(256 * i, 256 * i + 256)
        df_s[:, rows] = nt(z[:, 0:FIRST], wv[rows, 0:FIRST])
    x = x_ref[...].astype(F32)
    part, gain_grad = rms_back(x, row_scale(x), gin[...], df_s[...])
    gin_g[...] = gain_grad
    dx[...] = x1_s[...] + part


def layer_call(*args):
    def of(*s, t=F32):
        return jax.ShapeDtypeStruct(s, t)
    vm = pl.BlockSpec(memory_space=pltpu.VMEM)
    specs = [vm] * 17
    specs[8] = pl.BlockSpec(memory_space=pl.ANY)
    return pl.pallas_call(
        layer_kernel,
        out_shape=(of(128, 1024, t=BF16), of(128, 1024), of(4096, 128, t=BF16), of(128, COLS, t=BF16), of(1, 1024),
                   of(1, 1024), of(1, 1536), of(4, 1792), of(1, 1792), of(8, 128), of(1, 1536)),
        in_specs=specs,
        out_specs=[vm] * 11,
        scratch_shapes=[
            pltpu.VMEM((1024, COLS), BF16), pltpu.VMEM((128, FIRST), F32), pltpu.VMEM((128, 1792), F32),
            pltpu.VMEM((128, 1792), F32), pltpu.VMEM((128, 1536), F32), pltpu.VMEM((24, 128, 128), F32),
            pltpu.VMEM((8, 128, 128), F32), pltpu.VMEM((128, 512), F32), pltpu.VMEM((128, 1024), F32),
            pltpu.VMEM((128, 1024), F32), pltpu.VMEM((128, 1536), F32), pltpu.VMEM((128, 512), F32),
            pltpu.VMEM((128, 1792), F32), pltpu.VMEM((128, 128), F32), pltpu.SemaphoreType.DMA((4,)),
        ],
        compiler_params=pltpu.CompilerParams(vmem_limit_bytes=60 << 20),
        cost_estimate=pl.CostEstimate(flops=6_500_000_000, bytes_accessed=30_000_000, transcendentals=3_000_000),
        name="layer",
    )(*args)


def layout(device, seq_lengths, seq_owner, slot_count):
    owned = seq_owner == device
    own_lengths = jnp.where(owned, seq_lengths, 0)
    finish = jnp.cumsum(own_lengths, dtype=jnp.int32)
    slot_ids = jnp.arange(slot_count, dtype=jnp.int32)
    closed = owned[None, :] & (finish[None, :] <= slot_ids[:, None])
    segment = jnp.sum(closed.astype(jnp.int32), axis=1, dtype=jnp.int32)
    begins = jnp.max(jnp.where(closed, finish[None, :], 0), axis=1)
    active = slot_ids < jnp.sum(own_lengths, dtype=jnp.int32)
    return (segment, slot_ids - begins, active)


def turn_tables(position):
    ladder = jnp.arange(32, dtype=jnp.float32) * (2.0 / 64)
    speeds = jnp.exp(-math.log(ROPE_BASE) * ladder)
    angles = position.astype(jnp.float32)[:, None] * jnp.tile(speeds, 4)[None, :]
    return jnp.cos(angles), jnp.sin(angles)


def pack_smalls(mixer, taps, bias):
    k = mixer.shape[0]
    flat = jnp.concatenate([mixer, taps.reshape(k, 56), bias, jnp.zeros((k, 6), mixer.dtype)], axis=1)
    return flat.reshape(k * 8, 11)


def unpack_smalls(table):
    k = table.shape[0] // 8
    flat = table.reshape(k, 88)
    return flat[:, :12], flat[:, 12:68].reshape(k, 4, 14), flat[:, 68:82]


def row_of(values, width=128):
    return jnp.pad(values.astype(F32), ((0, 0), (0, width - values.shape[1])))


def layer_inputs(tokens, out_grad, segment, position, active, weights, step_bias, decay_log, skip_gain):
    smalls = weights[:, 4120:4133].astype(F32)
    mixer, taps, bias = unpack_smalls(smalls[:, 2:])
    cosine, sine = turn_tables(position)
    return (tokens, out_grad, segment[:, None], segment[None, :], position[:, None], active[:, None].astype(F32),
            cosine, sine, weights, smalls[:, 0][None], smalls[:, 1][None], mixer.reshape(1, 1536),
            jnp.moveaxis(taps, 1, 0).reshape(4, 1792), bias.reshape(1, 1792), row_of(step_bias), row_of(decay_log),
            jnp.repeat(skip_gain.astype(F32), 64, axis=1))


def small_table(gin_g, gffn_g, gmix_g, taps_g, cbias_g):
    smalls = pack_smalls(gmix_g.reshape(128, 12), jnp.moveaxis(taps_g.reshape(4, 128, 14), 0, 1), cbias_g.reshape(128, 14))
    return jnp.concatenate([jnp.zeros((1024, 24), F32), gin_g.reshape(1024, 1), gffn_g.reshape(1024, 1), smalls,
                            jnp.zeros((1024, 91), F32)], axis=1)


PIECES = (((0, 0, 4224, 384),), ((1, 4224, 2048, 256), (2, 6272, 2048, 256)), ((2, 8320, 2048, 256), (3, 10368, 2048, 256)))


def reduce_kernel(parts, rt, z, small, out, grad, z_sib, rt_sib, small_sib, *scratch):
    bufs, (send, recv, x_send, x_recv) = scratch[:-4], scratch[-4:]
    at = places()
    greet(at)
    whole = slice(None)
    core = at[AC]
    swaps = []

    def swap(k, src, dst):
        c = pltpu.make_async_remote_copy(src, dst, x_send.at[k], x_recv.at[k], device_id={AC: 1 - core}, device_id_type=MESH)
        c.start()
        swaps.append(c)
    swap(0, rt.at[:, :, 1 - core], rt_sib)
    for part, (c0, lo, hi) in enumerate(parts):
        swap(1 + part, z.at[:, pl.ds(c0, lo + hi)], z_sib.at[:, pl.ds(c0, lo + hi)])
        if part == 0:
            swap(4, small.at[:, 1 - core], small_sib)

    def products(part):
        for g, c0, n, width in PIECES[part]:
            left = jnp.concatenate([rt[g, :, core].reshape(512, 128), rt_sib[g].reshape(512, 128)], axis=1)

            def one(i, carry, c0=c0, width=width, left=left):
                cs = pl.ds(pl.multiple_of(c0 + i * width, 128), width)
                right = jnp.concatenate([z[:, cs], z_sib[:, cs]], axis=0)
                v = lax.dot_general(left, right, (((1,), (0,)), ((), ())), preferred_element_type=F32)
                grad[:, :, :, :, cs] = v.reshape(4, 4, 4, 8, width).astype(BF16)
                return carry
            lax.fori_loop(0, n // width, one, 0)

    sent = []
    for phase in range(3):
        state = []
        for part, (c0, lo, hi) in enumerate(parts):
            order = ORDERS[part][::-1]
            a = order[phase]
            p = at[a]
            nxt, prv, opp = lax.rem(p + 1, 4), lax.rem(p + 3, 4), lax.rem(p + 2, 4)
            base = {b: at[b] for b in (AX, AZ, AY)}
            for b in order[phase + 1:]:
                base[b] = whole
            el, er, fr, fl = bufs[(part * 3 + phase) * 4:(part * 3 + phase) * 4 + 4]

            def ref(q, cc, n, base=base, a=a):
                sel = {**base, a: q}
                return grad.at[sel[AX], sel[AZ], sel[AY], :, pl.ds(cc, n)]

            def mk(kind, q, cc, n, dst, to, part=part, a=a, ref=ref):
                return pltpu.make_async_remote_copy(ref(q, cc, n), dst, send.at[part, phase, kind],
                                                    recv.at[part, phase, kind], device_id={a: to}, device_id_type=MESH)
            if phase == 0:
                if part == 0:
                    swaps[0].wait_recv()
                    swaps[1].wait_recv()
                    swaps[2].wait_recv()
                else:
                    swaps[2 + part].wait_recv()
                products(part)
                if part == 0:
                    tile = grad.at[:, :, :, :, pl.ds(4096, 128)]
                    extra = small[:, core] + small_sib[...]
                    tile[...] = (tile[...].astype(F32) + extra.reshape(4, 4, 4, 8, 128)).astype(BF16)
            lead = (whole,) * (2 - phase) + (whole,)
            fr_lo, fr_hi = fr.at[lead + (pl.ds(0, lo),)], fr.at[lead + (pl.ds(lo, hi),)]
            fl_lo, fl_hi = fl.at[lead + (pl.ds(0, lo),)], fl.at[lead + (pl.ds(lo, hi),)]
            e_l = mk(0, opp, c0, lo, el, prv)
            e_r = mk(1, opp, c0 + lo, hi, er, nxt)
            d_l_hi = mk(2, prv, c0 + lo, hi, fr_hi, prv)
            d_r_lo = mk(3, nxt, c0, lo, fl_lo, nxt)
            for c in (e_l, e_r, d_l_hi, d_r_lo):
                c.start()
            d_l_lo = mk(4, prv, c0, lo, fr_lo, prv)
            d_r_hi = mk(5, nxt, c0 + lo, hi, fl_hi, nxt)
            sent += [e_l, e_r, d_l_hi, d_r_lo, d_l_lo, d_r_hi]
            state.append((e_l, e_r, d_l_hi, d_r_lo, d_l_lo, d_r_hi, ref, nxt, prv, p, c0, lo, hi, el, er, fr, fl))

        def each(fn):
            n = 2 - phase
            if n == 2:
                def outer(k, carry):
                    fn((k // 4, k % 4))
                    return carry
                lax.fori_loop(0, 16, outer, 0)
            elif n == 1:
                def outer(k, carry):
                    fn((k,))
                    return carry
                lax.fori_loop(0, 4, outer, 0)
            else:
                fn(())

        for s in state:
            e_l, e_r, d_l_hi, d_r_lo, d_l_lo, d_r_hi, ref, nxt, prv, p, c0, lo, hi, el, er, fr, fl = s
            e_l.wait_recv()

            def add_lo(ix, t=ref(prv, c0, lo), e=el):
                ix = ix + (whole, whole)
                t[ix] = t[ix] + e[ix]
            each(add_lo)
            d_l_lo.start()
            e_r.wait_recv()

            def add_hi(ix, t=ref(nxt, c0 + lo, hi), e=er):
                ix = ix + (whole, whole)
                t[ix] = t[ix] + e[ix]
            each(add_hi)
            d_r_hi.start()
        for part, s in enumerate(state):
            e_l, e_r, d_l_hi, d_r_lo, d_l_lo, d_r_hi, ref, nxt, prv, p, c0, lo, hi, el, er, fr, fl = s
            for c in (d_l_hi, d_r_lo, d_l_lo, d_r_hi):
                c.wait_recv()

            def total(ix, t=ref(p, c0, lo + hi), l=fl, r=fr):
                ix = ix + (whole, whole)
                v = t[ix].astype(F32) + l[ix].astype(F32) + r[ix].astype(F32)
                if phase == 2:
                    out[:, pl.ds(c0, lo + hi)] = v
                else:
                    t[ix] = v.astype(BF16)
            each(total)
    for c in sent:
        c.wait_send()
    for c in swaps:
        c.wait_send()


def shapes_of(phase, cols):
    return (4,) * (2 - phase) + (8, cols)


def reduce_call(rt, z, small):
    parts = cut3(COLS)
    bufs = []
    for c0, lo, hi in parts:
        for phase in range(3):
            for n in (lo, hi, lo + hi, lo + hi):
                bufs.append(pltpu.VMEM(shapes_of(phase, n), BF16))
    vm = pl.BlockSpec(memory_space=pltpu.VMEM)
    return pl.pallas_call(
        functools.partial(reduce_kernel, parts),
        out_shape=jax.ShapeDtypeStruct((8, COLS), F32),
        in_specs=[vm] * 3,
        out_specs=vm,
        scratch_shapes=[pltpu.VMEM((4, 4, 4, 8, COLS), BF16), pltpu.VMEM((128, COLS), BF16),
                        pltpu.VMEM((4, 16, 32, 128), BF16), pltpu.VMEM((16, 32, 128), F32)] + bufs + [
            pltpu.SemaphoreType.DMA((3, 3, 6)), pltpu.SemaphoreType.DMA((3, 3, 6)),
            pltpu.SemaphoreType.DMA((5,)), pltpu.SemaphoreType.DMA((5,))],
        compiler_params=pltpu.CompilerParams(collective_id=1, has_side_effects=True, vmem_limit_bytes=60 << 20),
        name="reduce",
    )(rt, z, small)


def body(tokens, seq_lengths, seq_owner, input_norm, gate_proj, inner_proj, step_proj, conv_weight, conv_bias, step_bias,
         decay_log, skip_gain, mixer_norm, mixer_out, query_proj, keyval_proj, attn_out, ffn_norm, gateup_proj, down_proj,
         out_grad):
    device = lax.axis_index(DP_FSDP)
    segment, position, active = layout(device, seq_lengths, seq_owner, tokens.shape[0])
    smalls = pack_smalls(mixer_norm, conv_weight, conv_bias)
    shard = jnp.concatenate(
        [gate_proj[0], inner_proj[0], query_proj[0], keyval_proj[0], step_proj[0], input_norm.reshape(8, 1),
         ffn_norm.reshape(8, 1), smalls, jnp.zeros((8, 91), BF16), mixer_out[0].T, attn_out[0].T, gateup_proj[0],
         down_proj[0].T], axis=1)
    weights = gather(shard).reshape(1024, COLS)
    inputs = layer_inputs(tokens, out_grad, segment, position, active, weights, step_bias, decay_log, skip_gain)
    result, dx, rt, z, gin_g, gffn_g, gmix_g, taps_g, cbias_g, head_g, skip_g = layer_call(*inputs)
    table = small_table(gin_g, gffn_g, gmix_g, taps_g, cbias_g)
    heads = jnp.concatenate([head_g[0, :24], head_g[1, :24], jnp.sum(skip_g.reshape(24, 64), axis=1)])
    heads = lax.psum(heads, DP_FSDP).reshape(3, 1, 24)
    grads = reduce_call(rt.reshape(4, 16, 2, 32, 128), z, table.reshape(16, 2, 32, 128))
    mixer_g, conv_g, bias_g = unpack_smalls(grads[:, 4122:4133])

    def cols(name):
        start, n = OFF[name]
        return grads[:, start:start + n]
    return (
        result, dx, grads[:, 4120].reshape(1, 8), cols("gate")[None], cols("inner")[None], grads[None, :, 4096:4120],
        conv_g, bias_g, heads[0], heads[1], heads[2], mixer_g, cols("mix").T[None], cols("query")[None],
        cols("keyval")[None], cols("attn").T[None], grads[:, 4121].reshape(1, 8), cols("gateup")[None],
        cols("down").T[None],
    )


def solution(mesh):
    split = Mesh(mesh.devices.reshape(4, 4, 2, mesh.shape["fsdp"]), DP_FSDP)
    rows, flat = P(DP_FSDP, None), P(None, DP_FSDP)
    weight, turned = P(None, DP_FSDP, None), P(None, None, DP_FSDP)
    in_specs = (rows, P(), P(), flat, weight, weight, weight, turned, flat, P(), P(), P(), flat, turned, weight, weight,
                turned, flat, weight, turned, rows)
    out_specs = (rows, rows, flat, weight, weight, weight, turned, flat, P(), P(), P(), flat, turned, weight, weight,
                 turned, flat, weight, turned)
    return jax.shard_map(body, mesh=split, in_specs=in_specs, out_specs=out_specs, check_vma=False)
```

```python
import functools
import math

import jax
import jax.numpy as jnp
from jax import lax
from jax.experimental import pallas as pl
from jax.experimental.pallas import tpu as pltpu
from jax.sharding import Mesh
from jax.sharding import PartitionSpec as P

EPSILON = 1e-05
ROPE_BASE = 100000000000.0
DP_FSDP = ("dp_0", "dp_1", "dp_2", "fsdp")
OFF = dict(gate=(0, 1536), inner=(1536, 1792), query=(3328, 512), keyval=(3840, 256), step=(4096, 128),
           mix=(4224, 1536), attn=(5760, 512), gateup=(6272, 4096), down=(10368, 2048))
COLS = 12416
FIRST = 4224
F32, BF16 = jnp.float32, jnp.bfloat16
HIGH = lax.Precision.HIGHEST
AT_IN, AT_FFN, AT_MIX, AT_BIAS, AT_TAPS = 24, 32, 40, 52, 66
SMALLS = ((AT_IN, 8, 1024), (AT_FFN, 8, 1024), (AT_MIX, 12, 1536), (AT_BIAS, 14, 1792))
INVERSE = {8: 8192, 12: 5462, 14: 4682}


AX, AZ, AC, AY = "dp_0", "dp_1", "dp_2", "fsdp"
ORDERS = ((AX, AY, AZ), (AY, AZ, AX), (AZ, AX, AY))
MESH = pl.DeviceIdType.MESH


def places():
    return {a: lax.axis_index(a) for a in (AX, AZ, AC, AY)}


def greet(at):
    barrier = pltpu.get_barrier_semaphore()
    for a in (AX, AZ, AY):
        for d in (1, 2, 3):
            pl.semaphore_signal(barrier, inc=1, device_id={a: lax.rem(at[a] + d, 4)}, device_id_type=MESH)
    pl.semaphore_signal(barrier, inc=1, device_id={AC: 1 - at[AC]}, device_id_type=MESH)
    pl.semaphore_wait(barrier, 10)


def cut3(cols, start=0):
    tiles = cols // 128
    sizes = [tiles // 3 + (1 if k < tiles % 3 else 0) for k in range(3)]
    parts, at = [], start
    for n in sizes:
        lo = (n + 1) // 2 * 128
        parts.append((at, lo, n * 128 - lo))
        at += n * 128
    return parts


def assemble(pieces, shard, tile):
    gate, inner, step, taps, cbias, mixer, mix, query, keyval, attn, gin, gffn, gateup, down = pieces
    for ref, (c0, n) in ((gate, OFF["gate"]), (inner, OFF["inner"]), (query, OFF["query"]), (keyval, OFF["keyval"]),
                         (mix, OFF["mix"]), (attn, OFF["attn"]), (gateup, OFF["gateup"]), (down, OFF["down"])):
        shard[:, c0:c0 + n] = ref[...]
    tile[...] = jnp.zeros((8, 128), F32)
    tile[:, 0:24] = step[...].astype(F32)
    tile[0:1, AT_IN:AT_IN + 8] = gin[...].astype(F32)
    tile[0:1, AT_FFN:AT_FFN + 8] = gffn[...].astype(F32)
    tile[0:1, AT_MIX:AT_MIX + 12] = mixer[...].astype(F32)
    tile[0:1, AT_BIAS:AT_BIAS + 14] = cbias[...].astype(F32)
    tile[0:4, AT_TAPS:AT_TAPS + 14] = taps[...].astype(F32)
    shard[:, 4096:4224] = tile[...].astype(BF16)


def gather_kernel(parts, *refs):
    pieces, out, (shard, tile, send, recv, sib_send, sib_recv, own_sem) = refs[:14], refs[14], refs[15:]
    at = places()
    assemble(pieces, shard, tile)
    greet(at)
    whole = slice(None)
    core = at[AC]

    def block(sel, c0, n):
        return out.at[sel[AX], sel[AZ], core, sel[AY], :, pl.ds(c0, n)]

    own = pltpu.make_async_copy(shard, out.at[at[AX], at[AZ], core, at[AY]], own_sem)
    own.start()
    pending_sib, sent = [], []

    def to_sibling(part, k, sel, c0, n):
        ref = block(sel, c0, n)
        c = pltpu.make_async_remote_copy(ref, ref, sib_send.at[part, k], sib_recv.at[part, k],
                                         device_id={AC: 1 - core}, device_id_type=MESH)
        c.start()
        pending_sib.append(c)

    for phase in range(3):
        state = []
        for part, (c0, lo, hi) in enumerate(parts):
            order = ORDERS[part]
            a = order[phase]
            p = at[a]
            nxt, prv, opp = lax.rem(p + 1, 4), lax.rem(p + 3, 4), lax.rem(p + 2, 4)
            base = {b: at[b] for b in (AX, AZ, AY)}
            for b in order[:phase]:
                base[b] = whole

            def mk(kind, q, cc, n, to, part=part, a=a, base=base):
                dst = block({**base, a: q}, cc, n)
                src = shard.at[:, pl.ds(cc, n)] if (phase == 0 and kind < 4) else dst
                return pltpu.make_async_remote_copy(src, dst, send.at[part, phase, kind], recv.at[part, phase, kind],
                                                    device_id={a: to}, device_id_type=MESH)
            r_lo, l_hi = mk(0, p, c0, lo, nxt), mk(1, p, c0 + lo, hi, prv)
            r_hi, l_lo = mk(2, p, c0 + lo, hi, nxt), mk(3, p, c0, lo, prv)
            for c in (r_lo, l_hi, r_hi, l_lo):
                c.start()
            sent += [r_lo, l_hi, r_hi, l_lo]
            if phase == 2:
                to_sibling(part, 0, {**base}, c0, lo + hi)
            state.append((r_lo, l_hi, r_hi, l_lo, mk, nxt, prv, opp, base, a, c0, lo, hi))
        fwd = []
        for s in state:
            r_lo, l_hi, r_hi, l_lo, mk, nxt, prv, opp, base, a, c0, lo, hi = s
            r_lo.wait_recv()
            fr = mk(4, prv, c0, lo, nxt)
            fr.start()
            l_hi.wait_recv()
            fl = mk(5, nxt, c0 + lo, hi, prv)
            fl.start()
            fwd.append((fr, fl))
            sent += [fr, fl]
        for part, s in enumerate(state):
            r_lo, l_hi, r_hi, l_lo, mk, nxt, prv, opp, base, a, c0, lo, hi = s
            r_hi.wait_recv()
            if phase == 2:
                to_sibling(part, 1, {**base, a: prv}, c0, lo + hi)
            l_lo.wait_recv()
            if phase == 2:
                to_sibling(part, 2, {**base, a: nxt}, c0, lo + hi)
        for part, s in enumerate(state):
            r_lo, l_hi, r_hi, l_lo, mk, nxt, prv, opp, base, a, c0, lo, hi = s
            fr, fl = fwd[part]
            fr.wait_recv()
            if phase == 2:
                to_sibling(part, 3, {**base, a: opp}, c0, lo)
            fl.wait_recv()
            if phase == 2:
                to_sibling(part, 4, {**base, a: opp}, c0 + lo, hi)
        if phase == 0:
            own.wait()
    for c in sent:
        c.wait_send()
    for c in pending_sib:
        c.wait()


def gather(*pieces):
    parts = cut3(COLS)
    vm = pl.BlockSpec(memory_space=pltpu.VMEM)
    return pl.pallas_call(
        functools.partial(gather_kernel, parts),
        out_shape=jax.ShapeDtypeStruct((4, 4, 2, 4, 8, COLS), BF16),
        in_specs=[vm] * 14,
        out_specs=pl.BlockSpec(memory_space=pl.ANY),
        scratch_shapes=[
            pltpu.VMEM((8, COLS), BF16), pltpu.VMEM((8, 128), F32),
            pltpu.SemaphoreType.DMA((3, 3, 6)), pltpu.SemaphoreType.DMA((3, 3, 6)),
            pltpu.SemaphoreType.DMA((3, 5)), pltpu.SemaphoreType.DMA((3, 5)), pltpu.SemaphoreType.DMA,
        ],
        compiler_params=pltpu.CompilerParams(collective_id=0, has_side_effects=True, vmem_limit_bytes=60 << 20),
        name="gather",
    )(*pieces)


def nn(a, b, precision=None):
    return lax.dot_general(a, b, (((1,), (0,)), ((), ())), preferred_element_type=F32, precision=precision)


def nt(a, b, precision=None):
    return lax.dot_general(a, b, (((1,), (1,)), ((), ())), preferred_element_type=F32, precision=precision)


def tn(a, b, precision=None):
    return lax.dot_general(a, b, (((0,), (0,)), ((), ())), preferred_element_type=F32, precision=precision)


def sigmoid(v):
    return 1.0 / (1.0 + jnp.exp(-v))


def cols_of(i, n, start=0):
    return pl.ds(pl.multiple_of(start + i * n, 128), n)


def rms_back(values, scale, gain, grad):
    inner = grad * gain
    mean = jnp.mean(values * inner, axis=-1, keepdims=True)
    return scale * inner - values * (scale * scale * scale * mean), jnp.sum(grad * values * scale, axis=0, keepdims=True)


def row_scale(values):
    return lax.rsqrt(jnp.mean(values * values, axis=-1, keepdims=True) + EPSILON)


def selectors(i, start, n):
    d = lax.broadcasted_iota(jnp.int32, (128, 128), 1) + 128 * i
    row = lax.broadcasted_iota(jnp.int32, (128, 128), 0)
    owner = lax.shift_right_logical(d * INVERSE[n], 16)
    return row == owner, row == start + d - n * owner


def spread_row(table, start, n, width, dst, row=0):
    for i in range(width // 128):
        owned, lane = selectors(i, start, n)
        v = nn(table, lane.astype(F32).astype(BF16))
        dst[row:row + 1, 128 * i:128 * i + 128] = jnp.sum(jnp.where(owned, v, 0.0), axis=0, keepdims=True)


def unspread_row(src, start, n, width, row=0):
    total = jnp.zeros((128, 128), F32)
    for i in range(width // 128):
        owned, lane = selectors(i, start, n)
        held = jnp.where(owned, src[row:row + 1, 128 * i:128 * i + 128], 0.0)
        total = total + nt(held.astype(BF16), lane.astype(F32).astype(BF16))
    return total


def layer_kernel(x_ref, og_ref, lengths, owners, w_hbm, sbias_ref, dlog_ref, skip_ref,
                 result, dx, rt, z, small, head_g,
                 wv, proj, csum, conv, yfull, dec, soft, qr, x1_s, df_s, dm_s, do_s, dconv, ddt_s, wsem,
                 gin, gffn, gmix, taps, cbias, skipx, rows_s, gin_g, gffn_g, gmix_g, taps_g, cbias_g, table):
    groups = ((0, FIRST), (4224, 2048), (6272, 4096), (10368, 2048))
    loads = []
    for k, (c0, n) in enumerate(groups):
        c = pltpu.make_async_copy(w_hbm.at[:, pl.ds(c0, n)], wv.at[:, pl.ds(c0, n)], wsem.at[k])
        c.start()
        loads.append(c)

    lane = lax.broadcasted_iota(jnp.int32, (128, 128), 1)
    sub = lax.broadcasted_iota(jnp.int32, (128, 128), 0)
    low_lanes = lane < 64

    at = places()
    me = ((at[AX] * 4 + at[AZ]) * 2 + at[AC]) * 4 + at[AY]
    owned = owners[...] == me
    held = jnp.where(owned, lengths[...], 0).astype(F32)
    before = lax.broadcasted_iota(jnp.int32, (256, 256), 0) <= lax.broadcasted_iota(jnp.int32, (256, 256), 1)
    ends = nn(jnp.broadcast_to(held, (8, 256)).astype(BF16), before.astype(F32).astype(BF16))[0:1, :]
    slot = lax.broadcasted_iota(jnp.int32, (128, 256), 0).astype(F32)
    closed = jnp.broadcast_to(owned.astype(F32), (128, 256)) * (jnp.broadcast_to(ends, (128, 256)) <= slot).astype(F32)
    segment = jnp.sum(closed, axis=1, keepdims=True)
    begins = jnp.max(closed * ends, axis=1, keepdims=True)
    used = jnp.max(ends, axis=1, keepdims=True)
    slots = sub.astype(F32)
    position = jnp.broadcast_to(slots[:, 0:1] - begins, (128, 128))
    active = (slots[:, 0:1] < used).astype(F32)
    segments = jnp.broadcast_to(segment, (128, 128))
    allowed = (segments == segments.T) & (sub >= lane)
    speeds = jnp.exp((lane % 32).astype(F32) * (-math.log(ROPE_BASE) * 2.0 / 64))
    angles = position * speeds
    cosine, sine = jnp.cos(angles), jnp.sin(angles)

    rows_s[...] = jnp.zeros((8, 128), F32)
    rows_s[0:1, 0:24] = sbias_ref[...].astype(F32)
    rows_s[1:2, 0:24] = dlog_ref[...].astype(F32)
    rows_s[2:3, 0:24] = skip_ref[...].astype(F32)
    sbias, dlog = rows_s[0:1, :], rows_s[1:2, :]
    heads_low = rows_s[...].astype(BF16)
    for i in range(12):
        of_head = (sub == 2 * i + lax.shift_right_logical(lane, 6)).astype(F32).astype(BF16)
        skipx[:, 128 * i:128 * i + 128] = nn(heads_low, of_head)[2:3, :]

    def halves(v):
        return jnp.where(low_lanes, v, 0.0), jnp.where(low_lanes, 0.0, v)

    def stacked(v):
        lo, hi = halves(v)
        return jnp.concatenate([lo, hi], axis=0).astype(BF16)

    loads[0].wait()
    table[...] = wv[:, 4096:4224].astype(F32)
    tables = [table[pl.ds(r, 128, stride=8), :].astype(BF16) for r in range(4)]
    for dst, (start, n, width) in zip((gin, gffn, gmix, cbias), SMALLS):
        spread_row(tables[0], start, n, width, dst)
    for r in range(4):
        spread_row(tables[r], AT_TAPS, 14, 1792, taps, r)

    x = x_ref[...].astype(F32)
    h = (x * row_scale(x) * gin[...]).astype(BF16)
    rt[0:1024, :] = h.T
    g0 = og_ref[...].astype(F32) * active
    glow = g0.astype(BF16)
    rt[3072:4096, :] = glow.T
    z_h = h

    def project(i, carry):
        proj[:, cols_of(i, 384)] = nn(z_h, wv[:, cols_of(i, 384)])
        return carry
    lax.fori_loop(0, 11, project, 0)

    def convolve(i, carry):
        cs = cols_of(i, 128)
        p = proj[:, cols_of(i, 128, 1536)]
        total = p * taps[3:4, cs]
        for j in (1, 2, 3):
            moved = jnp.where(position >= float(j), pltpu.roll(p, j, axis=0), 0.0)
            total = total + moved * taps[3 - j:4 - j, cs]
        total = total + cbias[:, cs]
        csum[:, cs] = total
        conv[:, cs] = total * sigmoid(total)
        return carry
    lax.fori_loop(0, 14, convolve, 0)

    step = proj[:, 4096:4224] + sbias
    dt = jnp.maximum(step, 0.0) + jnp.log(1.0 + jnp.exp(-jnp.abs(step)))
    rate = -jnp.exp(dlog)
    lower = (sub >= lane).astype(F32)
    level = nn(lower, dt * rate, HIGH)
    dt_t = dt.T
    level_t = level.T
    b_mat = conv[:, 1536:1664]
    c_mat = conv[:, 1664:1792]
    inter = nt(c_mat, b_mat, HIGH)

    square = jnp.zeros((128, 1), F32)
    for t in range(12):
        cs = slice(128 * t, 128 * t + 128)
        mixes = []
        for n in (2 * t, 2 * t + 1):
            spread = jnp.where(allowed, level[:, n:n + 1] - level_t[n:n + 1, :], -1e30)
            decay = jnp.exp(spread)
            dec[n] = decay
            mixes.append((decay * inter * dt_t[n:n + 1, :]).astype(BF16))
        xs = conv[:, cs]
        y = nn(jnp.concatenate(mixes, axis=1), stacked(xs)) + skipx[:, cs] * xs
        yfull[:, cs] = y
        gate = proj[:, cs]
        gy = y * (gate * sigmoid(gate))
        square = square + jnp.sum(gy * gy, axis=1, keepdims=True)
    rmix = lax.rsqrt(square * (1.0 / 1536) + EPSILON)

    def mixer_norm(i, carry):
        cs = cols_of(i, 128)
        gate = proj[:, cs]
        gy = yfull[:, cs] * (gate * sigmoid(gate))
        z[:, cols_of(i, 128, 4224)] = (gy * rmix * gmix[:, cs]).astype(BF16)
        return carry
    lax.fori_loop(0, 12, mixer_norm, 0)

    first = (lane % 64) < 32

    def turn(v, sign):
        side = jnp.where(first, -pltpu.roll(v, 96, axis=1), pltpu.roll(v, 32, axis=1))
        return v * cosine + sign * side * sine

    def dup(v, j):
        other = pltpu.roll(v, 64, axis=1)
        return jnp.where(low_lanes, v, other) if j == 0 else jnp.where(low_lanes, other, v)
    key_t = turn(proj[:, 3840:3968], 1.0).astype(BF16).astype(F32)
    val = proj[:, 3968:4096].astype(BF16).astype(F32)
    keys = [dup(key_t, j) for j in (0, 1)]
    vals = [dup(val, j) for j in (0, 1)]
    for t in range(4):
        cs = slice(128 * t, 128 * t + 128)
        q = turn(proj[:, 3328 + 128 * t:3456 + 128 * t], 1.0).astype(BF16).astype(F32)
        qr[:, cs] = q
        scores = nt(stacked(q), keys[t // 2].astype(BF16)) * 0.125
        weights = []
        for e in (0, 1):
            s = jnp.where(allowed, scores[128 * e:128 * e + 128], -1e30)
            w = jnp.exp(s - jnp.max(s, axis=1, keepdims=True))
            w = w / jnp.sum(w, axis=1, keepdims=True)
            soft[2 * t + e] = w
            weights.append(w.astype(BF16))
        z[:, 5760 + 128 * t:5888 + 128 * t] = nn(jnp.concatenate(weights, axis=1), stacked(vals[t // 2])).astype(BF16)

    loads[1].wait()
    for i in range(4):
        rows = slice(256 * i, 256 * i + 256)
        x1_s[:, rows] = x_ref[:, rows].astype(F32) + nt(z[:, 4224:6272], wv[rows, 4224:6272])
    x1 = x1_s[...]
    r1 = row_scale(x1)
    f = (x1 * r1 * gffn[...]).astype(BF16)
    rt[2048:3072, :] = f.T

    loads[2].wait()
    loads[3].wait()

    def feed(i, carry):
        g = nn(f, wv[:, cols_of(i, 256, 6272)])
        u = nn(f, wv[:, cols_of(i, 256, 8320)])
        da = nn(glow, wv[:, cols_of(i, 256, 10368)])
        s = sigmoid(g)
        gs = g * s
        z[:, cols_of(i, 256, 10368)] = (gs * u).astype(BF16)
        z[:, cols_of(i, 256, 6272)] = (da * u * (s + gs * (1.0 - s))).astype(BF16)
        z[:, cols_of(i, 256, 8320)] = (da * gs).astype(BF16)
        return carry
    lax.fori_loop(0, 8, feed, 0)
    for i in range(4):
        rows = slice(256 * i, 256 * i + 256)
        result[:, rows] = (x1_s[:, rows] + nt(z[:, 10368:12416], wv[rows, 10368:12416])).astype(BF16)
        df_s[:, rows] = nt(z[:, 6272:10368], wv[rows, 6272:10368])
    part, gain_grad = rms_back(x1, r1, gffn[...], df_s[...])
    gffn_g[...] = gain_grad
    dx1 = g0 + part
    x1_s[...] = dx1
    blow = dx1.astype(BF16)
    rt[1024:2048, :] = blow.T

    def back_branch(i, carry):
        dm_s[:, cols_of(i, 512)] = nn(blow, wv[:, cols_of(i, 512, 4224)])
        return carry
    lax.fori_loop(0, 3, back_branch, 0)
    do_s[...] = nn(blow, wv[:, 5760:6272])

    dks, dvs = [], []
    for t in range(4):
        cs = slice(128 * t, 128 * t + 128)
        do2 = stacked(do_s[:, cs])
        dp = nt(do2, vals[t // 2].astype(BF16))
        ds, ws = [], []
        for e in (0, 1):
            w = soft[2 * t + e]
            d = dp[128 * e:128 * e + 128]
            ds.append((w * (d - jnp.sum(d * w, axis=1, keepdims=True)) * 0.125).astype(BF16))
            ws.append(w.astype(BF16))
        dq = nn(jnp.concatenate(ds, axis=1), stacked(keys[t // 2]))
        z[:, 3328 + 128 * t:3456 + 128 * t] = turn(dq, -1.0).astype(BF16)
        dks.append(tn(jnp.concatenate(ds, axis=0), stacked(qr[:, cs])))
        dvs.append(tn(jnp.concatenate(ws, axis=0), do2))

    def fold(parts):
        a, b = parts[0] + parts[1], parts[2] + parts[3]
        return jnp.where(low_lanes, a + pltpu.roll(a, 64, axis=1), b + pltpu.roll(b, 64, axis=1))
    z[:, 3840:3968] = turn(fold(dks), -1.0).astype(BF16)
    z[:, 3968:4096] = fold(dvs).astype(BF16)

    dots = jnp.zeros((128, 1), F32)
    for t in range(12):
        cs = slice(128 * t, 128 * t + 128)
        gate = proj[:, cs]
        gy = yfull[:, cs] * (gate * sigmoid(gate))
        dm = dm_s[:, cs]
        gmix_g[:, cs] = jnp.sum(dm * gy * rmix, axis=0, keepdims=True)
        dots = dots + jnp.sum(gy * dm * gmix[:, cs], axis=1, keepdims=True)
    pull = rmix * rmix * rmix * dots * (1.0 / 1536)
    ddt_s[...] = jnp.zeros((128, 128), F32)
    dlevel = jnp.zeros((128, 128), F32)
    dskip = jnp.zeros((1, 128), F32)
    lane_row = lane[0:1, :]
    dinter = jnp.zeros((128, 128), F32)
    for t in range(12):
        cs = slice(128 * t, 128 * t + 128)
        gate = proj[:, cs]
        s = sigmoid(gate)
        gs = gate * s
        y = yfull[:, cs]
        dgy = rmix * (gmix[:, cs] * dm_s[:, cs]) - y * gs * pull
        z[:, cs] = (dgy * y * (s + gs * (1.0 - s))).astype(BF16)
        dy = dgy * gs
        xs = conv[:, cs]
        skipped = jnp.sum(dy * xs, axis=0, keepdims=True)
        for e in (0, 1):
            in_head = (lane_row < 64) if e == 0 else (lane_row >= 64)
            dskip = dskip + jnp.where(lane_row == 2 * t + e,
                                      jnp.sum(jnp.where(in_head, skipped, 0.0), axis=1, keepdims=True), 0.0)
        dy2 = stacked(dy)
        dmix = nt(dy2, xs.astype(BF16))
        mixes = []
        for e in (0, 1):
            n = 2 * t + e
            dt_row = dt_t[n:n + 1, :]
            decay = dec[n]
            mixed = decay * inter
            dm = dmix[128 * e:128 * e + 128]
            mixes.append((mixed * dt_row).astype(BF16))
            dd = dm * dt_row
            dinter = dinter + dd * decay
            ddt_s[n:n + 1, :] = jnp.sum(dm * mixed, axis=0, keepdims=True)
            dlevel = dlevel + jnp.where(lane == n, jnp.sum(dd * mixed, axis=1, keepdims=True), 0.0)
        dconv[:, cs] = tn(jnp.concatenate(mixes, axis=0), dy2) + skipx[:, cs] * dy
    dconv[:, 1536:1664] = tn(dinter, c_mat, HIGH)
    dconv[:, 1664:1792] = nn(dinter, b_mat, HIGH)
    ddt = ddt_s[...].T
    dlevel = dlevel - ddt * dt
    upper = (sub <= lane).astype(F32)
    drate = nn(upper, dlevel, HIGH)
    dstep = jnp.where(lane < 24, (ddt + drate * rate) * sigmoid(step), 0.0)
    z[:, 4096:4224] = dstep.astype(BF16)
    head_g[...] = jnp.zeros((8, 128), F32)
    head_g[2:3, :] = dskip
    head_g[0:1, :] = jnp.sum(dstep, axis=0, keepdims=True)
    head_g[1:2, :] = jnp.sum(drate * dt * rate, axis=0, keepdims=True)

    def unconvolve(i, carry):
        cs = cols_of(i, 128)
        total = csum[:, cs]
        s = sigmoid(total)
        d = dconv[:, cs] * (s + total * s * (1.0 - s))
        p = proj[:, cols_of(i, 128, 1536)]
        cbias_g[:, cs] = jnp.sum(d, axis=0, keepdims=True)
        taps_g[3:4, cs] = jnp.sum(d * p, axis=0, keepdims=True)
        back = d * taps[3:4, cs]
        for j in (1, 2, 3):
            masked = jnp.where(position >= float(j), d, 0.0)
            taps_g[3 - j:4 - j, cs] = jnp.sum(masked * pltpu.roll(p, j, axis=0), axis=0, keepdims=True)
            back = back + pltpu.roll(masked, 128 - j, axis=0) * taps[3 - j:4 - j, cs]
        z[:, cols_of(i, 128, 1536)] = back.astype(BF16)
        return carry
    lax.fori_loop(0, 14, unconvolve, 0)

    for i in range(4):
        rows = slice(256 * i, 256 * i + 256)
        df_s[:, rows] = nt(z[:, 0:FIRST], wv[rows, 0:FIRST])
    x = x_ref[...].astype(F32)
    part, gain_grad = rms_back(x, row_scale(x), gin[...], df_s[...])
    gin_g[...] = gain_grad
    dx[...] = x1_s[...] + part

    small[...] = jnp.zeros((1024, 128), F32)
    for r in range(4):
        total = unspread_row(taps_g, AT_TAPS, 14, 1792, r)
        if r == 0:
            for src, (start, n, width) in zip((gin_g, gffn_g, gmix_g, cbias_g), SMALLS):
                total = total + unspread_row(src, start, n, width)
        small[pl.ds(r, 128, stride=8), :] = total


def layer_call(*args):
    def of(*s, t=F32):
        return jax.ShapeDtypeStruct(s, t)
    vm = pl.BlockSpec(memory_space=pltpu.VMEM)
    specs = [vm] * 8
    specs[4] = pl.BlockSpec(memory_space=pl.ANY)
    return pl.pallas_call(
        layer_kernel,
        out_shape=(of(128, 1024, t=BF16), of(128, 1024), of(4096, 128, t=BF16), of(128, COLS, t=BF16), of(1024, 128),
                   of(8, 128)),
        in_specs=specs,
        out_specs=[vm] * 6,
        scratch_shapes=[
            pltpu.VMEM((1024, COLS), BF16), pltpu.VMEM((128, FIRST), F32), pltpu.VMEM((128, 1792), F32),
            pltpu.VMEM((128, 1792), F32), pltpu.VMEM((128, 1536), F32), pltpu.VMEM((24, 128, 128), F32),
            pltpu.VMEM((8, 128, 128), F32), pltpu.VMEM((128, 512), F32), pltpu.VMEM((128, 1024), F32),
            pltpu.VMEM((128, 1024), F32), pltpu.VMEM((128, 1536), F32), pltpu.VMEM((128, 512), F32),
            pltpu.VMEM((128, 1792), F32), pltpu.VMEM((128, 128), F32), pltpu.SemaphoreType.DMA((4,)),
            pltpu.VMEM((1, 1024), F32), pltpu.VMEM((1, 1024), F32), pltpu.VMEM((1, 1536), F32), pltpu.VMEM((4, 1792), F32),
            pltpu.VMEM((1, 1792), F32), pltpu.VMEM((1, 1536), F32), pltpu.VMEM((8, 128), F32),
            pltpu.VMEM((1, 1024), F32), pltpu.VMEM((1, 1024), F32), pltpu.VMEM((1, 1536), F32), pltpu.VMEM((4, 1792), F32),
            pltpu.VMEM((1, 1792), F32), pltpu.VMEM((1024, 128), F32),
        ],
        compiler_params=pltpu.CompilerParams(vmem_limit_bytes=60 << 20),
        cost_estimate=pl.CostEstimate(flops=6_500_000_000, bytes_accessed=30_000_000, transcendentals=3_000_000),
        name="layer",
    )(*args)


PIECES = (((0, 0, 4224, 384),), ((1, 4224, 2048, 256), (2, 6272, 2048, 256)), ((2, 8320, 2048, 256), (3, 10368, 2048, 256)))


def reduce_kernel(parts, rt, z, small, head, out, head_out, grad, z_sib, rt_sib, small_sib, *scratch):
    bufs, (send, recv, x_send, x_recv, hnow, hbuf, h_send, h_recv) = scratch[:-8], scratch[-8:]
    at = places()
    greet(at)
    whole = slice(None)
    core = at[AC]
    swaps = []

    def swap(k, src, dst):
        c = pltpu.make_async_remote_copy(src, dst, x_send.at[k], x_recv.at[k], device_id={AC: 1 - core}, device_id_type=MESH)
        c.start()
        swaps.append(c)
    swap(0, rt.at[:, :, 1 - core], rt_sib)
    for part, (c0, lo, hi) in enumerate(parts):
        swap(1 + part, z.at[:, pl.ds(c0, lo + hi)], z_sib.at[:, pl.ds(c0, lo + hi)])
        if part == 0:
            swap(4, small.at[:, 1 - core], small_sib)
            swap(5, head, hnow.at[4])

    def products(part):
        for g, c0, n, width in PIECES[part]:
            left = jnp.concatenate([rt[g, :, core].reshape(512, 128), rt_sib[g].reshape(512, 128)], axis=1)

            def one(i, carry, c0=c0, width=width, left=left):
                cs = pl.ds(pl.multiple_of(c0 + i * width, 128), width)
                right = jnp.concatenate([z[:, cs], z_sib[:, cs]], axis=0)
                v = lax.dot_general(left, right, (((1,), (0,)), ((), ())), preferred_element_type=F32)
                grad[:, :, :, :, cs] = v.reshape(4, 4, 4, 8, width).astype(BF16)
                return carry
            lax.fori_loop(0, n // width, one, 0)

    sent = []
    axes = (AX, AZ, AY)

    def heads_out(k):
        a = axes[k]
        p = at[a]
        hbuf[k, p] = hnow[k]
        copies = []
        for d in (1, 2, 3):
            c = pltpu.make_async_remote_copy(hnow.at[k], hbuf.at[k, p], h_send.at[k, d - 1], h_recv.at[k, d - 1],
                                             device_id={a: lax.rem(p + d, 4)}, device_id_type=MESH)
            c.start()
            copies.append(c)
        sent.extend(copies)
        return copies

    def heads_in(k, copies):
        for c in copies:
            c.wait_recv()
        return ((hbuf[k, 0] + hbuf[k, 1]) + hbuf[k, 2]) + hbuf[k, 3]
    moving = None
    for phase in range(3):
        state = []
        for part, (c0, lo, hi) in enumerate(parts):
            order = ORDERS[part][::-1]
            a = order[phase]
            p = at[a]
            nxt, prv, opp = lax.rem(p + 1, 4), lax.rem(p + 3, 4), lax.rem(p + 2, 4)
            base = {b: at[b] for b in (AX, AZ, AY)}
            for b in order[phase + 1:]:
                base[b] = whole
            el, er, fr, fl = bufs[(part * 3 + phase) * 4:(part * 3 + phase) * 4 + 4]

            def ref(q, cc, n, base=base, a=a):
                sel = {**base, a: q}
                return grad.at[sel[AX], sel[AZ], sel[AY], :, pl.ds(cc, n)]

            def mk(kind, q, cc, n, dst, to, part=part, a=a, ref=ref):
                return pltpu.make_async_remote_copy(ref(q, cc, n), dst, send.at[part, phase, kind],
                                                    recv.at[part, phase, kind], device_id={a: to}, device_id_type=MESH)
            if phase == 0:
                if part == 0:
                    swaps[0].wait_recv()
                    swaps[1].wait_recv()
                    swaps[2].wait_recv()
                else:
                    swaps[3 + part].wait_recv()
                products(part)
                if part == 0:
                    tile = grad.at[:, :, :, :, pl.ds(4096, 128)]
                    extra = small[:, core] + small_sib[...]
                    tile[...] = (tile[...].astype(F32) + extra.reshape(4, 4, 4, 8, 128)).astype(BF16)
            lead = (whole,) * (2 - phase) + (whole,)
            fr_lo, fr_hi = fr.at[lead + (pl.ds(0, lo),)], fr.at[lead + (pl.ds(lo, hi),)]
            fl_lo, fl_hi = fl.at[lead + (pl.ds(0, lo),)], fl.at[lead + (pl.ds(lo, hi),)]
            e_l = mk(0, opp, c0, lo, el, prv)
            e_r = mk(1, opp, c0 + lo, hi, er, nxt)
            d_l_hi = mk(2, prv, c0 + lo, hi, fr_hi, prv)
            d_r_lo = mk(3, nxt, c0, lo, fl_lo, nxt)
            for c in (e_l, e_r, d_l_hi, d_r_lo):
                c.start()
            d_l_lo = mk(4, prv, c0, lo, fr_lo, prv)
            d_r_hi = mk(5, nxt, c0 + lo, hi, fl_hi, nxt)
            sent += [e_l, e_r, d_l_hi, d_r_lo, d_l_lo, d_r_hi]
            state.append((e_l, e_r, d_l_hi, d_r_lo, d_l_lo, d_r_hi, ref, nxt, prv, p, c0, lo, hi, el, er, fr, fl))

        if phase == 0:
            swaps[3].wait_recv()
            hnow[0] = head[...] + hnow[4]
        else:
            hnow[phase] = heads_in(phase - 1, moving)
        moving = heads_out(phase)

        def each(fn):
            n = 2 - phase
            if n == 2:
                def outer(k, carry):
                    fn((k // 4, k % 4))
                    return carry
                lax.fori_loop(0, 16, outer, 0)
            elif n == 1:
                def outer(k, carry):
                    fn((k,))
                    return carry
                lax.fori_loop(0, 4, outer, 0)
            else:
                fn(())

        for s in state:
            e_l, e_r, d_l_hi, d_r_lo, d_l_lo, d_r_hi, ref, nxt, prv, p, c0, lo, hi, el, er, fr, fl = s
            e_l.wait_recv()

            def add_lo(ix, t=ref(prv, c0, lo), e=el):
                ix = ix + (whole, whole)
                t[ix] = t[ix] + e[ix]
            each(add_lo)
            d_l_lo.start()
            e_r.wait_recv()

            def add_hi(ix, t=ref(nxt, c0 + lo, hi), e=er):
                ix = ix + (whole, whole)
                t[ix] = t[ix] + e[ix]
            each(add_hi)
            d_r_hi.start()
        for part, s in enumerate(state):
            e_l, e_r, d_l_hi, d_r_lo, d_l_lo, d_r_hi, ref, nxt, prv, p, c0, lo, hi, el, er, fr, fl = s
            for c in (d_l_hi, d_r_lo, d_l_lo, d_r_hi):
                c.wait_recv()

            def total(ix, t=ref(p, c0, lo + hi), l=fl, r=fr):
                ix = ix + (whole, whole)
                v = t[ix].astype(F32) + l[ix].astype(F32) + r[ix].astype(F32)
                if phase == 2:
                    out[:, pl.ds(c0, lo + hi)] = v
                else:
                    t[ix] = v.astype(BF16)
            each(total)
    head_out[...] = heads_in(2, moving)
    for c in sent:
        c.wait_send()
    for c in swaps:
        c.wait_send()


def shapes_of(phase, cols):
    return (4,) * (2 - phase) + (8, cols)


def reduce_call(rt, z, small, head):
    parts = cut3(COLS)
    bufs = []
    for c0, lo, hi in parts:
        for phase in range(3):
            for n in (lo, hi, lo + hi, lo + hi):
                bufs.append(pltpu.VMEM(shapes_of(phase, n), BF16))
    vm = pl.BlockSpec(memory_space=pltpu.VMEM)
    return pl.pallas_call(
        functools.partial(reduce_kernel, parts),
        out_shape=(jax.ShapeDtypeStruct((8, COLS), F32), jax.ShapeDtypeStruct((8, 128), F32)),
        in_specs=[vm] * 4,
        out_specs=[vm] * 2,
        scratch_shapes=[pltpu.VMEM((4, 4, 4, 8, COLS), BF16), pltpu.VMEM((128, COLS), BF16),
                        pltpu.VMEM((4, 16, 32, 128), BF16), pltpu.VMEM((16, 32, 128), F32)] + bufs + [
            pltpu.SemaphoreType.DMA((3, 3, 6)), pltpu.SemaphoreType.DMA((3, 3, 6)),
            pltpu.SemaphoreType.DMA((6,)), pltpu.SemaphoreType.DMA((6,)),
            pltpu.VMEM((5, 8, 128), F32), pltpu.VMEM((3, 4, 8, 128), F32),
            pltpu.SemaphoreType.DMA((3, 3)), pltpu.SemaphoreType.DMA((3, 3))],
        compiler_params=pltpu.CompilerParams(collective_id=1, has_side_effects=True, vmem_limit_bytes=60 << 20),
        name="reduce",
    )(rt, z, small, head)


SPLIT = ("gate", "inner", "query", "keyval", "mix", "attn", "gateup", "down")


def split_kernel(grads, head, *outs):
    for name, dst in zip(SPLIT, outs[:8]):
        start, n = OFF[name]
        dst[...] = grads[:, start:start + n]
    step, gin, gffn, gmix, cbias, taps, bias, decay, skip = outs[8:]
    tile = grads[:, 4096:4224]
    step[...] = tile[:, 0:24]
    gin[...] = tile[0:1, AT_IN:AT_IN + 8]
    gffn[...] = tile[0:1, AT_FFN:AT_FFN + 8]
    gmix[...] = tile[0:1, AT_MIX:AT_MIX + 12]
    cbias[...] = tile[0:1, AT_BIAS:AT_BIAS + 14]
    taps[...] = tile[0:4, AT_TAPS:AT_TAPS + 14]
    for r, dst in enumerate((bias, decay, skip)):
        dst[...] = head[r:r + 1, 0:24]


def split_call(grads, head):
    def of(*s):
        return jax.ShapeDtypeStruct(s, F32)
    vm = pl.BlockSpec(memory_space=pltpu.VMEM)
    return pl.pallas_call(
        split_kernel,
        out_shape=[of(8, OFF[k][1]) for k in SPLIT] + [of(8, 24), of(1, 8), of(1, 8), of(1, 12), of(1, 14), of(4, 14),
                                                       of(1, 24), of(1, 24), of(1, 24)],
        in_specs=[vm] * 2,
        out_specs=[vm] * 17,
        name="split",
    )(grads, head)


def body(tokens, seq_lengths, seq_owner, input_norm, gate_proj, inner_proj, step_proj, conv_weight, conv_bias, step_bias,
         decay_log, skip_gain, mixer_norm, mixer_out, query_proj, keyval_proj, attn_out, ffn_norm, gateup_proj, down_proj,
         out_grad):
    weights = gather(gate_proj[0], inner_proj[0], step_proj[0], conv_weight[0], conv_bias, mixer_norm, mixer_out[0].T,
                     query_proj[0], keyval_proj[0], attn_out[0].T, input_norm, ffn_norm, gateup_proj[0],
                     down_proj[0].T).reshape(1024, COLS)
    result, dx, rt, z, small, head = layer_call(tokens, out_grad, seq_lengths.reshape(1, 256), seq_owner.reshape(1, 256),
                                                weights, step_bias, decay_log, skip_gain)
    grads, heads = reduce_call(rt.reshape(4, 16, 2, 32, 128), z, small.reshape(16, 2, 32, 128), head)
    (gate, inner, query, keyval, mix, attn, gateup, down, step, gin, gffn, gmix, cbias, taps, bias, decay,
     skip) = split_call(grads, heads)
    return (result, dx, gin, gate[None], inner[None], step[None], taps[None], cbias, bias, decay, skip, gmix, mix.T[None],
            query[None], keyval[None], attn.T[None], gffn, gateup[None], down.T[None])


def solution(mesh):
    split = Mesh(mesh.devices.reshape(4, 4, 2, mesh.shape["fsdp"]), DP_FSDP)
    rows, flat = P(DP_FSDP, None), P(None, DP_FSDP)
    weight, turned = P(None, DP_FSDP, None), P(None, None, DP_FSDP)
    in_specs = (rows, P(), P(), flat, weight, weight, weight, turned, flat, P(), P(), P(), flat, turned, weight, weight,
                turned, flat, weight, turned, rows)
    out_specs = (rows, rows, flat, weight, weight, weight, turned, flat, P(), P(), P(), flat, turned, weight, weight,
                 turned, flat, weight, turned)
    return jax.shard_map(body, mesh=split, in_specs=in_specs, out_specs=out_specs, check_vma=False)
```

```python
import functools
import math

import jax
import jax.numpy as jnp
from jax import lax
from jax.experimental import pallas as pl
from jax.experimental.pallas import tpu as pltpu
from jax.sharding import Mesh
from jax.sharding import PartitionSpec as P

EPSILON = 1e-05
ROPE_BASE = 100000000000.0
DP_FSDP = ("dp_0", "dp_1", "dp_2", "fsdp")
OFF = dict(gate=(0, 1536), inner=(1536, 1792), query=(3328, 512), keyval=(3840, 256), step=(4096, 128),
           mix=(4224, 1536), attn=(5760, 512), gateup=(6272, 4096), down=(10368, 2048))
COLS = 12416
FIRST = 4224
F32, BF16 = jnp.float32, jnp.bfloat16
HIGH = lax.Precision.HIGHEST
AT_IN, AT_FFN, AT_MIX, AT_BIAS, AT_TAPS = 24, 32, 40, 52, 66
SMALLS = ((AT_IN, 8, 1024), (AT_FFN, 8, 1024), (AT_MIX, 12, 1536), (AT_BIAS, 14, 1792))
INVERSE = {8: 8192, 12: 5462, 14: 4682}


AX, AZ, AC, AY = "dp_0", "dp_1", "dp_2", "fsdp"
ORDERS = ((AX, AY, AZ), (AY, AZ, AX), (AZ, AX, AY))
MESH = pl.DeviceIdType.MESH
WHOLE = slice(None)


def places():
    return {a: lax.axis_index(a) for a in (AX, AZ, AC, AY)}


def greet(at):
    barrier = pltpu.get_barrier_semaphore()
    for a in (AX, AZ, AY):
        for d in (1, 2, 3):
            pl.semaphore_signal(barrier, inc=1, device_id={a: lax.rem(at[a] + d, 4)}, device_id_type=MESH)
    pl.semaphore_signal(barrier, inc=1, device_id={AC: 1 - at[AC]}, device_id_type=MESH)
    pl.semaphore_wait(barrier, 10)


def cut3(cols, start=0):
    tiles = cols // 128
    sizes = [tiles // 3 + (1 if k < tiles % 3 else 0) for k in range(3)]
    parts, at = [], start
    for n in sizes:
        lo = (n + 1) // 2 * 128
        parts.append((at, lo, n * 128 - lo))
        at += n * 128
    return parts


class Gather:
    def __init__(self, at, parts, shard, out, send, recv, sib_send, sib_recv):
        self.at, self.parts, self.shard, self.out = at, parts, shard, out
        self.sems, self.sib_sems = (send, recv), (sib_send, sib_recv)
        self.sent, self.sib, self.state = [], [], {}

    def block(self, sel, c0, n):
        return self.out.at[sel[AX], sel[AZ], self.at[AC], sel[AY], :, pl.ds(c0, n)]

    def to_sibling(self, part, k, sel, c0, n):
        ref = self.block(sel, c0, n)
        send, recv = self.sib_sems
        c = pltpu.make_async_remote_copy(ref, ref, send.at[part, k], recv.at[part, k],
                                         device_id={AC: 1 - self.at[AC]}, device_id_type=MESH)
        c.start()
        self.sib.append(c)

    def start(self, phase):
        send, recv = self.sems
        state = []
        for part, (c0, lo, hi) in enumerate(self.parts):
            order = ORDERS[part]
            a = order[phase]
            p = self.at[a]
            nxt, prv, opp = lax.rem(p + 1, 4), lax.rem(p + 3, 4), lax.rem(p + 2, 4)
            base = {b: self.at[b] for b in (AX, AZ, AY)}
            for b in order[:phase]:
                base[b] = WHOLE

            def mk(kind, q, cc, n, to, part=part, a=a, base=base):
                dst = self.block({**base, a: q}, cc, n)
                src = self.shard.at[:, pl.ds(cc, n)] if (phase == 0 and kind < 4) else dst
                return pltpu.make_async_remote_copy(src, dst, send.at[part, phase, kind], recv.at[part, phase, kind],
                                                    device_id={a: to}, device_id_type=MESH)
            copies = [mk(0, p, c0, lo, nxt), mk(1, p, c0 + lo, hi, prv), mk(2, p, c0 + lo, hi, nxt), mk(3, p, c0, lo, prv)]
            for c in copies:
                c.start()
            self.sent += copies
            if phase == 2:
                self.to_sibling(part, 0, base, c0, lo + hi)
            state.append((copies, mk, nxt, prv, opp, base, a, c0, lo, hi))
        self.state[phase] = state

    def forward(self, phase):
        self.fwd = []
        for part, (copies, mk, nxt, prv, opp, base, a, c0, lo, hi) in enumerate(self.state[phase]):
            copies[0].wait_recv()
            fr = mk(4, prv, c0, lo, nxt)
            fr.start()
            copies[1].wait_recv()
            fl = mk(5, nxt, c0 + lo, hi, prv)
            fl.start()
            if phase == 2:
                self.to_sibling(part, 1, {**base, a: prv}, c0, lo)
                self.to_sibling(part, 2, {**base, a: nxt}, c0 + lo, hi)
            self.fwd.append((fr, fl))
            self.sent += [fr, fl]

    def sides(self, phase):
        for part, (copies, mk, nxt, prv, opp, base, a, c0, lo, hi) in enumerate(self.state[phase]):
            copies[2].wait_recv()
            if phase == 2:
                self.to_sibling(part, 3, {**base, a: prv}, c0 + lo, hi)
            copies[3].wait_recv()
            if phase == 2:
                self.to_sibling(part, 4, {**base, a: nxt}, c0, lo)

    def finish(self, phase):
        for part, (copies, mk, nxt, prv, opp, base, a, c0, lo, hi) in enumerate(self.state[phase]):
            fr, fl = self.fwd[part]
            fr.wait_recv()
            if phase == 2:
                self.to_sibling(part, 5, {**base, a: opp}, c0, lo)
            fl.wait_recv()
            if phase == 2:
                self.to_sibling(part, 6, {**base, a: opp}, c0 + lo, hi)

    def shared(self):
        for c in self.sib:
            c.wait_recv()

    def drain(self):
        for c in self.sent + self.sib:
            c.wait_send()


class Reduce:
    def __init__(self, at, parts, grad, first, out, bufs, send, recv):
        self.at, self.parts, self.grad, self.first, self.out, self.bufs = at, parts, grad, first, out, bufs
        self.sems, self.sent, self.state = (send, recv), [], {0: [], 1: [], 2: []}

    def start(self, phase, part):
        send, recv = self.sems
        c0, lo, hi = self.parts[part]
        order = ORDERS[part][::-1]
        a = order[phase]
        p = self.at[a]
        nxt, prv, opp = lax.rem(p + 1, 4), lax.rem(p + 3, 4), lax.rem(p + 2, 4)
        base = {b: self.at[b] for b in (AX, AZ, AY)}
        for b in order[phase + 1:]:
            base[b] = WHOLE
        el, er, fr, fl = self.bufs[(part * 3 + phase) * 4:(part * 3 + phase) * 4 + 4]

        def ref(q, cc, n):
            sel = {**base, a: q}
            return self.grad.at[sel[AX], sel[AZ], sel[AY], :, pl.ds(cc - self.first, n)]

        def mk(kind, q, cc, n, dst, to):
            return pltpu.make_async_remote_copy(ref(q, cc, n), dst, send.at[part, phase, kind],
                                                recv.at[part, phase, kind], device_id={a: to}, device_id_type=MESH)
        lead = (WHOLE,) * (3 - phase)
        fr_lo, fr_hi = fr.at[lead + (pl.ds(0, lo),)], fr.at[lead + (pl.ds(lo, hi),)]
        fl_lo, fl_hi = fl.at[lead + (pl.ds(0, lo),)], fl.at[lead + (pl.ds(lo, hi),)]
        now = [mk(0, opp, c0, lo, el, prv), mk(1, opp, c0 + lo, hi, er, nxt), mk(2, prv, c0 + lo, hi, fr_hi, prv),
               mk(3, nxt, c0, lo, fl_lo, nxt)]
        for c in now:
            c.start()
        later = [mk(4, prv, c0, lo, fr_lo, prv), mk(5, nxt, c0 + lo, hi, fl_hi, nxt)]
        self.sent += now + later
        self.state[phase].append((now, later, ref(prv, c0, lo), ref(nxt, c0 + lo, hi), ref(p, c0, lo + hi), el, er, fr, fl))

    def each(self, phase, fn):
        if phase == 2:
            fn((WHOLE, WHOLE))
            return

        def one(k, carry):
            fn(((k // 4, k % 4) if phase == 0 else (k,)) + (WHOLE, WHOLE))
            return carry
        lax.fori_loop(0, 16 if phase == 0 else 4, one, 0)

    def middle(self, phase):
        for now, later, left, right, own, el, er, fr, fl in self.state[phase]:
            for c, onward, target, come in ((now[0], later[0], left, el), (now[1], later[1], right, er)):
                c.wait_recv()

                def add(ix, target=target, come=come):
                    target[ix] = target[ix] + come[ix]
                self.each(phase, add)
                onward.start()

    def finish(self, phase, then=None):
        for part, (now, later, left, right, own, el, er, fr, fl) in enumerate(self.state[phase]):
            for c in (now[2], now[3], later[0], later[1]):
                c.wait_recv()
            c0, lo, hi = self.parts[part]

            def total(ix, own=own, fl=fl, fr=fr, c0=c0, n=lo + hi):
                v = own[ix].astype(F32) + fl[ix].astype(F32) + fr[ix].astype(F32)
                if phase == 2:
                    self.out[:, pl.ds(c0, n)] = v
                else:
                    own[ix] = v.astype(BF16)
            self.each(phase, total)
            if phase < 2:
                self.start(phase + 1, part)

    def drain(self):
        for c in self.sent:
            c.wait_send()


def assemble(pieces, shard, tile):
    gate, inner, step, taps, cbias, mixer, mix, query, keyval, attn, gin, gffn, gateup, down = pieces
    for ref, (c0, n) in ((gate, OFF["gate"]), (inner, OFF["inner"]), (query, OFF["query"]), (keyval, OFF["keyval"]),
                         (mix, OFF["mix"]), (attn, OFF["attn"]), (gateup, OFF["gateup"]), (down, OFF["down"])):
        shard[:, c0:c0 + n] = ref[...]
    tile[...] = jnp.zeros((8, 128), F32)
    tile[:, 0:24] = step[...].astype(F32)
    tile[0:1, AT_IN:AT_IN + 8] = gin[...].astype(F32)
    tile[0:1, AT_FFN:AT_FFN + 8] = gffn[...].astype(F32)
    tile[0:1, AT_MIX:AT_MIX + 12] = mixer[...].astype(F32)
    tile[0:1, AT_BIAS:AT_BIAS + 14] = cbias[...].astype(F32)
    tile[0:4, AT_TAPS:AT_TAPS + 14] = taps[...].astype(F32)
    shard[:, 4096:4224] = tile[...].astype(BF16)


def nn(a, b, precision=None):
    return lax.dot_general(a, b, (((1,), (0,)), ((), ())), preferred_element_type=F32, precision=precision)


def nt(a, b, precision=None):
    return lax.dot_general(a, b, (((1,), (1,)), ((), ())), preferred_element_type=F32, precision=precision)


def tn(a, b, precision=None):
    return lax.dot_general(a, b, (((0,), (0,)), ((), ())), preferred_element_type=F32, precision=precision)


def sigmoid(v):
    return 1.0 / (1.0 + jnp.exp(-v))


def cols_of(i, n, start=0):
    return pl.ds(pl.multiple_of(start + i * n, 128), n)


def rms_back(values, scale, gain, grad):
    inner = grad * gain
    mean = jnp.mean(values * inner, axis=-1, keepdims=True)
    return scale * inner - values * (scale * scale * scale * mean), jnp.sum(grad * values * scale, axis=0, keepdims=True)


def row_scale(values):
    return lax.rsqrt(jnp.mean(values * values, axis=-1, keepdims=True) + EPSILON)


def selectors(i, start, n):
    d = lax.broadcasted_iota(jnp.int32, (128, 128), 1) + 128 * i
    row = lax.broadcasted_iota(jnp.int32, (128, 128), 0)
    owner = lax.shift_right_logical(d * INVERSE[n], 16)
    return row == owner, row == start + d - n * owner


def spread_row(table, start, n, width, dst, row=0):
    for i in range(width // 128):
        owned, lane = selectors(i, start, n)
        v = nn(table, lane.astype(F32).astype(BF16))
        dst[row:row + 1, 128 * i:128 * i + 128] = jnp.sum(jnp.where(owned, v, 0.0), axis=0, keepdims=True)


def unspread_row(src, start, n, width, row=0):
    total = jnp.zeros((128, 128), F32)
    for i in range(width // 128):
        owned, lane = selectors(i, start, n)
        held = jnp.where(owned, src[row:row + 1, 128 * i:128 * i + 128], 0.0)
        total = total + nt(held.astype(BF16), lane.astype(F32).astype(BF16))
    return total


SAVED = (("proj", (128, FIRST)), ("csum", (128, 1792)), ("conv", (128, 1792)), ("yfull", (128, 1536)), ("dec", (24, 128, 128)),
         ("soft", (8, 128, 128)), ("qr", (128, 512)), ("misc", (9, 128, 128)))


def forward_kernel(*refs):
    pieces, (x_ref, og_ref, lengths, owners, sbias_ref, dlog_ref, skip_ref) = refs[:14], refs[14:21]
    w, result, rt, zb, x1_s, dm_s, do_s, gffn_g, gin, gmix, taps, skipx, rows_s = refs[21:34]
    kept, (proj, csum, conv, yfull, dec, soft, qr, misc) = refs[34:42], refs[42:50]
    wv, df_s, gffn, cbias, table, shard, tile, wsem, own_sem, keep_sem, a_sems, b_sems, a_sib, b_sib = refs[50:]
    at = places()
    assemble(pieces, shard, tile)
    greet(at)
    own = pltpu.make_async_copy(shard, w.at[at[AX], at[AZ], at[AC], at[AY]], own_sem)
    own.start()
    first_group = Gather(at, cut3(FIRST), shard, w, a_sems.at[0], a_sems.at[1], a_sib.at[0], a_sib.at[1])
    second_group = Gather(at, cut3(COLS - FIRST, FIRST), shard, w, b_sems.at[0], b_sems.at[1], b_sib.at[0], b_sib.at[1])
    first_group.start(0)
    second_group.start(0)
    lane = lax.broadcasted_iota(jnp.int32, (128, 128), 1)
    sub = lax.broadcasted_iota(jnp.int32, (128, 128), 0)
    low_lanes = lane < 64

    me = ((at[AX] * 4 + at[AZ]) * 2 + at[AC]) * 4 + at[AY]
    owned = owners[...] == me
    held = jnp.where(owned, lengths[...], 0).astype(F32)
    before = lax.broadcasted_iota(jnp.int32, (256, 256), 0) <= lax.broadcasted_iota(jnp.int32, (256, 256), 1)
    ends = nn(jnp.broadcast_to(held, (8, 256)).astype(BF16), before.astype(F32).astype(BF16))[0:1, :]
    slot = lax.broadcasted_iota(jnp.int32, (128, 256), 0).astype(F32)
    closed = jnp.broadcast_to(owned.astype(F32), (128, 256)) * (jnp.broadcast_to(ends, (128, 256)) <= slot).astype(F32)
    segment = jnp.sum(closed, axis=1, keepdims=True)
    begins = jnp.max(closed * ends, axis=1, keepdims=True)
    used = jnp.max(ends, axis=1, keepdims=True)
    slots = sub.astype(F32)
    position = jnp.broadcast_to(slots[:, 0:1] - begins, (128, 128))
    active = (slots[:, 0:1] < used).astype(F32)
    segments = jnp.broadcast_to(segment, (128, 128))
    allowed = (segments == segments.T) & (sub >= lane)
    speeds = jnp.exp((lane % 32).astype(F32) * (-math.log(ROPE_BASE) * 2.0 / 64))
    angles = position * speeds
    cosine, sine = jnp.cos(angles), jnp.sin(angles)

    rows_s[...] = jnp.zeros((8, 128), F32)
    rows_s[0:1, 0:24] = sbias_ref[...].astype(F32)
    rows_s[1:2, 0:24] = dlog_ref[...].astype(F32)
    rows_s[2:3, 0:24] = skip_ref[...].astype(F32)
    sbias, dlog = rows_s[0:1, :], rows_s[1:2, :]
    heads_low = rows_s[...].astype(BF16)
    for i in range(12):
        of_head = (sub == 2 * i + lax.shift_right_logical(lane, 6)).astype(F32).astype(BF16)
        skipx[:, 128 * i:128 * i + 128] = nn(heads_low, of_head)[2:3, :]

    def halves(v):
        return jnp.where(low_lanes, v, 0.0), jnp.where(low_lanes, 0.0, v)

    def stacked(v):
        lo, hi = halves(v)
        return jnp.concatenate([lo, hi], axis=0).astype(BF16)

    first_group.forward(0)
    second_group.forward(0)
    first_group.sides(0)
    first_group.finish(0)
    own.wait()
    first_group.start(1)
    second_group.sides(0)
    second_group.finish(0)
    second_group.start(1)
    first_group.forward(1)
    first_group.sides(1)
    second_group.forward(1)
    first_group.finish(1)
    first_group.start(2)
    first_group.forward(2)
    second_group.sides(1)
    second_group.finish(1)
    second_group.start(2)
    first_group.sides(2)
    first_group.finish(2)
    first_group.shared()
    rows_of_w = w.reshape(1024, COLS)

    def load(k, c0, n):
        c = pltpu.make_async_copy(rows_of_w.at[:, pl.ds(c0, n)], wv.at[:, pl.ds(c0, n)], wsem.at[k])
        c.start()
        return c
    load(0, 0, FIRST).wait()
    table[...] = wv[:, 4096:4224].astype(F32)
    tables = [table[pl.ds(r, 128, stride=8), :].astype(BF16) for r in range(4)]
    for dst, (start, n, width) in zip((gin, gffn, gmix, cbias), SMALLS):
        spread_row(tables[0], start, n, width, dst)
    for r in range(4):
        spread_row(tables[r], AT_TAPS, 14, 1792, taps, r)

    x = x_ref[...].astype(F32)
    h = (x * row_scale(x) * gin[...]).astype(BF16)
    rt[0:1024, :] = h.T
    g0 = og_ref[...].astype(F32) * active
    glow = g0.astype(BF16)
    rt[3072:4096, :] = glow.T
    z_h = h

    def project(i, carry):
        proj[:, cols_of(i, 384)] = nn(z_h, wv[:, cols_of(i, 384)])
        return carry
    lax.fori_loop(0, 11, project, 0)

    def convolve(i, carry):
        cs = cols_of(i, 128)
        p = proj[:, cols_of(i, 128, 1536)]
        total = p * taps[3:4, cs]
        for j in (1, 2, 3):
            moved = jnp.where(position >= float(j), pltpu.roll(p, j, axis=0), 0.0)
            total = total + moved * taps[3 - j:4 - j, cs]
        total = total + cbias[:, cs]
        csum[:, cs] = total
        conv[:, cs] = total * sigmoid(total)
        return carry
    lax.fori_loop(0, 14, convolve, 0)

    step = proj[:, 4096:4224] + sbias
    dt = jnp.maximum(step, 0.0) + jnp.log(1.0 + jnp.exp(-jnp.abs(step)))
    rate = -jnp.exp(dlog)
    lower = (sub >= lane).astype(F32)
    level = nn(lower, dt * rate, HIGH)
    dt_t = dt.T
    level_t = level.T
    b_mat = conv[:, 1536:1664]
    c_mat = conv[:, 1664:1792]
    inter = nt(c_mat, b_mat, HIGH)

    second_group.forward(2)
    square = jnp.zeros((128, 1), F32)
    for t in range(12):
        cs = slice(128 * t, 128 * t + 128)
        mixes = []
        for n in (2 * t, 2 * t + 1):
            spread = jnp.where(allowed, level[:, n:n + 1] - level_t[n:n + 1, :], -1e30)
            decay = jnp.exp(spread)
            dec[n] = decay
            mixes.append((decay * inter * dt_t[n:n + 1, :]).astype(BF16))
        xs = conv[:, cs]
        y = nn(jnp.concatenate(mixes, axis=1), stacked(xs)) + skipx[:, cs] * xs
        yfull[:, cs] = y
        gate = proj[:, cs]
        gy = y * (gate * sigmoid(gate))
        square = square + jnp.sum(gy * gy, axis=1, keepdims=True)
    rmix = lax.rsqrt(square * (1.0 / 1536) + EPSILON)

    def mixer_norm(i, carry):
        cs = cols_of(i, 128)
        gate = proj[:, cs]
        gy = yfull[:, cs] * (gate * sigmoid(gate))
        zb[:, cols_of(i, 128)] = (gy * rmix * gmix[:, cs]).astype(BF16)
        return carry
    lax.fori_loop(0, 12, mixer_norm, 0)

    second_group.sides(2)
    first = (lane % 64) < 32

    def turn(v, sign):
        side = jnp.where(first, -pltpu.roll(v, 96, axis=1), pltpu.roll(v, 32, axis=1))
        return v * cosine + sign * side * sine

    def dup(v, j):
        other = pltpu.roll(v, 64, axis=1)
        return jnp.where(low_lanes, v, other) if j == 0 else jnp.where(low_lanes, other, v)
    key_t = turn(proj[:, 3840:3968], 1.0).astype(BF16).astype(F32)
    val = proj[:, 3968:4096].astype(BF16).astype(F32)
    keys = [dup(key_t, j) for j in (0, 1)]
    vals = [dup(val, j) for j in (0, 1)]
    for t in range(4):
        cs = slice(128 * t, 128 * t + 128)
        q = turn(proj[:, 3328 + 128 * t:3456 + 128 * t], 1.0).astype(BF16).astype(F32)
        qr[:, cs] = q
        scores = nt(stacked(q), keys[t // 2].astype(BF16)) * 0.125
        weights = []
        for e in (0, 1):
            s = jnp.where(allowed, scores[128 * e:128 * e + 128], -1e30)
            w = jnp.exp(s - jnp.max(s, axis=1, keepdims=True))
            w = w / jnp.sum(w, axis=1, keepdims=True)
            soft[2 * t + e] = w
            weights.append(w.astype(BF16))
        zb[:, 1536 + 128 * t:1664 + 128 * t] = nn(jnp.concatenate(weights, axis=1), stacked(vals[t // 2])).astype(BF16)

    for k, v in enumerate((key_t, val, dt, step, inter, jnp.broadcast_to(rmix, (128, 128)), position, cosine, sine)):
        misc[k] = v
    keeps = []
    for k, (src, dst) in enumerate(zip((proj, csum, conv, yfull, dec, soft, qr, misc), kept)):
        c = pltpu.make_async_copy(src, dst, keep_sem.at[k])
        c.start()
        keeps.append(c)
    second_group.finish(2)
    second_group.shared()
    loads = [load(1, 4224, 2048), load(2, 6272, 4096), load(3, 10368, 2048)]
    loads[0].wait()
    for i in range(4):
        rows = slice(256 * i, 256 * i + 256)
        x1_s[:, rows] = x_ref[:, rows].astype(F32) + nt(zb[:, 0:2048], wv[rows, 4224:6272])
    x1 = x1_s[...]
    r1 = row_scale(x1)
    f = (x1 * r1 * gffn[...]).astype(BF16)
    rt[2048:3072, :] = f.T

    loads[1].wait()
    loads[2].wait()

    def feed(i, carry):
        g = nn(f, wv[:, cols_of(i, 256, 6272)])
        u = nn(f, wv[:, cols_of(i, 256, 8320)])
        da = nn(glow, wv[:, cols_of(i, 256, 10368)])
        s = sigmoid(g)
        gs = g * s
        zb[:, cols_of(i, 256, 6144)] = (gs * u).astype(BF16)
        zb[:, cols_of(i, 256, 2048)] = (da * u * (s + gs * (1.0 - s))).astype(BF16)
        zb[:, cols_of(i, 256, 4096)] = (da * gs).astype(BF16)
        return carry
    lax.fori_loop(0, 8, feed, 0)
    for i in range(4):
        rows = slice(256 * i, 256 * i + 256)
        result[:, rows] = (x1_s[:, rows] + nt(zb[:, 6144:8192], wv[rows, 10368:12416])).astype(BF16)
        df_s[:, rows] = nt(zb[:, 2048:6144], wv[rows, 6272:10368])
    part, gain_grad = rms_back(x1, r1, gffn[...], df_s[...])
    gffn_g[...] = gain_grad
    dx1 = g0 + part
    x1_s[...] = dx1
    blow = dx1.astype(BF16)
    rt[1024:2048, :] = blow.T

    def back_branch(i, carry):
        dm_s[:, cols_of(i, 512)] = nn(blow, wv[:, cols_of(i, 512, 4224)])
        return carry
    lax.fori_loop(0, 3, back_branch, 0)
    do_s[...] = nn(blow, wv[:, 5760:6272])

    first_group.drain()
    second_group.drain()
    for c in keeps:
        c.wait()


def forward_call(*args):
    def of(*s, t=F32):
        return jax.ShapeDtypeStruct(s, t)
    vm, hbm = pl.BlockSpec(memory_space=pltpu.VMEM), pl.BlockSpec(memory_space=pl.ANY)
    return pl.pallas_call(
        forward_kernel,
        out_shape=[of(4, 4, 2, 4, 8, COLS, t=BF16), of(128, 1024, t=BF16), of(4096, 128, t=BF16),
                   of(128, COLS - FIRST, t=BF16), of(128, 1024), of(128, 1536), of(128, 512), of(1, 1024), of(1, 1024),
                   of(1, 1536), of(4, 1792), of(1, 1536), of(8, 128)] + [of(*s) for _, s in SAVED],
        in_specs=[vm] * 21,
        out_specs=[hbm] + [vm] * 12 + [hbm] * 8,
        scratch_shapes=[pltpu.VMEM(s, F32) for _, s in SAVED] + [
            pltpu.VMEM((1024, COLS), BF16), pltpu.VMEM((128, 1024), F32), pltpu.VMEM((1, 1024), F32),
            pltpu.VMEM((1, 1792), F32), pltpu.VMEM((1024, 128), F32), pltpu.VMEM((8, COLS), BF16), pltpu.VMEM((8, 128), F32),
            pltpu.SemaphoreType.DMA((4,)), pltpu.SemaphoreType.DMA, pltpu.SemaphoreType.DMA((8,)),
            pltpu.SemaphoreType.DMA((2, 3, 3, 6)), pltpu.SemaphoreType.DMA((2, 3, 3, 6)),
            pltpu.SemaphoreType.DMA((2, 3, 7)), pltpu.SemaphoreType.DMA((2, 3, 7)),
        ],
        compiler_params=pltpu.CompilerParams(collective_id=0, has_side_effects=True, vmem_limit_bytes=60 << 20),
        name="forward",
    )(*args)


PIECES_A = (((0, 0, 1280, 256), (0, 1280, 128, 128)), ((0, 1408, 1280, 256), (0, 2688, 128, 128)),
            ((0, 2816, 1280, 256), (0, 4096, 128, 128)))
PIECES_B = (((1, 4224, 2048, 256), (2, 6272, 768, 256)), ((2, 7040, 2688, 384),), ((2, 9728, 640, 128), (3, 10368, 2048, 256)))


def backward_kernel(x_ref, rt, zb, x1_s, dm_s, do_s, gffn_g, gin, gmix, taps, skipx, rows_s, w, *refs):
    kept, (dx, out, head_out), (proj, csum, conv, yfull, dec, soft, qr, misc) = refs[:8], refs[8:11], refs[11:19]
    (wv, z, df_s, dconv, ddt_s, gin_g, gmix_g, taps_g, cbias_g, small, head_g, grad_a, grad_b, zb_sib, za_sib, rt_sib,
     small_sib, wsem, keep_sem, x_send, x_recv, hnow, hbuf, h_send, h_recv, a_sems, b_sems) = refs[19:46]
    bufs_a, bufs_b = refs[46:82], refs[82:118]
    at = places()
    load = pltpu.make_async_copy(w.reshape(1024, COLS).at[:, pl.ds(0, FIRST)], wv, wsem)
    load.start()
    keeps = []
    for k, (src, dst) in enumerate(zip(kept, (proj, csum, conv, yfull, dec, soft, qr, misc))):
        c = pltpu.make_async_copy(src, dst, keep_sem.at[k])
        c.start()
        keeps.append(c)
    greet(at)
    core = at[AC]
    parts_a, parts_b = cut3(FIRST), cut3(COLS - FIRST, FIRST)
    swaps = {}

    def swap(k, src, dst):
        c = pltpu.make_async_remote_copy(src, dst, x_send.at[k], x_recv.at[k], device_id={AC: 1 - core}, device_id_type=MESH)
        c.start()
        swaps[k] = c

    def swap_columns(k, src, dst, part, first):
        c0, lo, hi = part
        cs = pl.ds(c0 - first, lo + hi)
        swap(k, src.at[:, cs], dst.at[:, cs])
    swap(0, rt.at[:, :, 1 - core], rt_sib)
    for part in range(3):
        swap_columns(1 + part, zb, zb_sib, parts_b[part], FIRST)

    def products(pieces, grad, mine, other, first):
        for g, c0, n, width in pieces:
            left = jnp.concatenate([rt[g, :, core].reshape(512, 128), rt_sib[g].reshape(512, 128)], axis=1)

            def one(i, carry, c0=c0, width=width, left=left):
                cs = pl.ds(pl.multiple_of(c0 - first + i * width, 128), width)
                right = jnp.concatenate([mine[:, cs], other[:, cs]], axis=0)
                grad[:, :, :, :, cs] = nn(left, right).reshape(4, 4, 4, 8, width).astype(BF16)
                return carry
            lax.fori_loop(0, n // width, one, 0)

    sum_a = Reduce(at, parts_a, grad_a, 0, out, bufs_a, a_sems.at[0], a_sems.at[1])
    sum_b = Reduce(at, parts_b, grad_b, FIRST, out, bufs_b, b_sems.at[0], b_sems.at[1])
    swaps[0].wait_recv()
    for part in range(3):
        swaps[1 + part].wait_recv()
        products(PIECES_B[part], grad_b, zb, zb_sib, FIRST)
        sum_b.start(0, part)

    axes, head_sent = (AX, AZ, AY), []

    def heads_go(k):
        a = axes[k]
        p = at[a]
        hbuf[k, p] = hnow[k]
        copies = []
        for d in (1, 2, 3):
            c = pltpu.make_async_remote_copy(hnow.at[k], hbuf.at[k, p], h_send.at[k, d - 1], h_recv.at[k, d - 1],
                                             device_id={a: lax.rem(p + d, 4)}, device_id_type=MESH)
            c.start()
            copies.append(c)
        head_sent.extend(copies)
        return copies

    def heads_come(k, copies):
        for c in copies:
            c.wait_recv()
        return ((hbuf[k, 0] + hbuf[k, 1]) + hbuf[k, 2]) + hbuf[k, 3]

    lane = lax.broadcasted_iota(jnp.int32, (128, 128), 1)
    sub = lax.broadcasted_iota(jnp.int32, (128, 128), 0)
    low_lanes = lane < 64
    def halves(v):
        return jnp.where(low_lanes, v, 0.0), jnp.where(low_lanes, 0.0, v)

    def stacked(v):
        lo, hi = halves(v)
        return jnp.concatenate([lo, hi], axis=0).astype(BF16)

    for c in keeps:
        c.wait()
    key_t, val, dt, step, inter, rmix, position, cosine, sine = [misc[k] for k in range(9)]
    rmix = rmix[:, 0:1]
    first = (lane % 64) < 32

    def turn(v, sign):
        side = jnp.where(first, -pltpu.roll(v, 96, axis=1), pltpu.roll(v, 32, axis=1))
        return v * cosine + sign * side * sine

    def dup(v, j):
        other = pltpu.roll(v, 64, axis=1)
        return jnp.where(low_lanes, v, other) if j == 0 else jnp.where(low_lanes, other, v)
    keys = [dup(key_t, j) for j in (0, 1)]
    vals = [dup(val, j) for j in (0, 1)]
    dks, dvs = [], []
    for t in range(4):
        cs = slice(128 * t, 128 * t + 128)
        do2 = stacked(do_s[:, cs])
        dp = nt(do2, vals[t // 2].astype(BF16))
        ds, ws = [], []
        for e in (0, 1):
            w = soft[2 * t + e]
            d = dp[128 * e:128 * e + 128]
            ds.append((w * (d - jnp.sum(d * w, axis=1, keepdims=True)) * 0.125).astype(BF16))
            ws.append(w.astype(BF16))
        dq = nn(jnp.concatenate(ds, axis=1), stacked(keys[t // 2]))
        z[:, 3328 + 128 * t:3456 + 128 * t] = turn(dq, -1.0).astype(BF16)
        dks.append(tn(jnp.concatenate(ds, axis=0), stacked(qr[:, cs])))
        dvs.append(tn(jnp.concatenate(ws, axis=0), do2))

    def fold(parts):
        a, b = parts[0] + parts[1], parts[2] + parts[3]
        return jnp.where(low_lanes, a + pltpu.roll(a, 64, axis=1), b + pltpu.roll(b, 64, axis=1))
    z[:, 3840:3968] = turn(fold(dks), -1.0).astype(BF16)
    z[:, 3968:4096] = fold(dvs).astype(BF16)

    dt_t = dt.T
    rate = -jnp.exp(rows_s[1:2, :])
    b_mat = conv[:, 1536:1664]
    c_mat = conv[:, 1664:1792]
    dots = jnp.zeros((128, 1), F32)
    for t in range(12):
        cs = slice(128 * t, 128 * t + 128)
        gate = proj[:, cs]
        gy = yfull[:, cs] * (gate * sigmoid(gate))
        dm = dm_s[:, cs]
        gmix_g[:, cs] = jnp.sum(dm * gy * rmix, axis=0, keepdims=True)
        dots = dots + jnp.sum(gy * dm * gmix[:, cs], axis=1, keepdims=True)
    pull = rmix * rmix * rmix * dots * (1.0 / 1536)
    ddt_s[...] = jnp.zeros((128, 128), F32)
    dlevel = jnp.zeros((128, 128), F32)
    dskip = jnp.zeros((1, 128), F32)
    lane_row = lane[0:1, :]
    dinter = jnp.zeros((128, 128), F32)
    for t in range(12):
        cs = slice(128 * t, 128 * t + 128)
        gate = proj[:, cs]
        s = sigmoid(gate)
        gs = gate * s
        y = yfull[:, cs]
        dgy = rmix * (gmix[:, cs] * dm_s[:, cs]) - y * gs * pull
        z[:, cs] = (dgy * y * (s + gs * (1.0 - s))).astype(BF16)
        dy = dgy * gs
        xs = conv[:, cs]
        skipped = jnp.sum(dy * xs, axis=0, keepdims=True)
        for e in (0, 1):
            in_head = (lane_row < 64) if e == 0 else (lane_row >= 64)
            dskip = dskip + jnp.where(lane_row == 2 * t + e,
                                      jnp.sum(jnp.where(in_head, skipped, 0.0), axis=1, keepdims=True), 0.0)
        dy2 = stacked(dy)
        dmix = nt(dy2, xs.astype(BF16))
        mixes = []
        for e in (0, 1):
            n = 2 * t + e
            dt_row = dt_t[n:n + 1, :]
            decay = dec[n]
            mixed = decay * inter
            dm = dmix[128 * e:128 * e + 128]
            mixes.append((mixed * dt_row).astype(BF16))
            dd = dm * dt_row
            dinter = dinter + dd * decay
            ddt_s[n:n + 1, :] = jnp.sum(dm * mixed, axis=0, keepdims=True)
            dlevel = dlevel + jnp.where(lane == n, jnp.sum(dd * mixed, axis=1, keepdims=True), 0.0)
        dconv[:, cs] = tn(jnp.concatenate(mixes, axis=0), dy2) + skipx[:, cs] * dy
    sum_b.middle(0)
    dconv[:, 1536:1664] = tn(dinter, c_mat, HIGH)
    dconv[:, 1664:1792] = nn(dinter, b_mat, HIGH)
    ddt = ddt_s[...].T
    dlevel = dlevel - ddt * dt
    upper = (sub <= lane).astype(F32)
    drate = nn(upper, dlevel, HIGH)
    dstep = jnp.where(lane < 24, (ddt + drate * rate) * sigmoid(step), 0.0)
    z[:, 4096:4224] = dstep.astype(BF16)
    head_g[...] = jnp.zeros((8, 128), F32)
    head_g[2:3, :] = dskip
    head_g[0:1, :] = jnp.sum(dstep, axis=0, keepdims=True)
    head_g[1:2, :] = jnp.sum(drate * dt * rate, axis=0, keepdims=True)

    def unconvolve(i, carry):
        cs = cols_of(i, 128)
        total = csum[:, cs]
        s = sigmoid(total)
        d = dconv[:, cs] * (s + total * s * (1.0 - s))
        p = proj[:, cols_of(i, 128, 1536)]
        cbias_g[:, cs] = jnp.sum(d, axis=0, keepdims=True)
        taps_g[3:4, cs] = jnp.sum(d * p, axis=0, keepdims=True)
        back = d * taps[3:4, cs]
        for j in (1, 2, 3):
            masked = jnp.where(position >= float(j), d, 0.0)
            taps_g[3 - j:4 - j, cs] = jnp.sum(masked * pltpu.roll(p, j, axis=0), axis=0, keepdims=True)
            back = back + pltpu.roll(masked, 128 - j, axis=0) * taps[3 - j:4 - j, cs]
        z[:, cols_of(i, 128, 1536)] = back.astype(BF16)
        return carry
    lax.fori_loop(0, 14, unconvolve, 0)

    for part in range(3):
        swap_columns(4 + part, z, za_sib, parts_a[part], 0)
    swap(8, head_g, hnow.at[3])
    load.wait()
    for i in range(4):
        rows = slice(256 * i, 256 * i + 256)
        df_s[:, rows] = nt(z[:, 0:FIRST], wv[rows, 0:FIRST])
    x = x_ref[...].astype(F32)
    part, gain_grad = rms_back(x, row_scale(x), gin[...], df_s[...])
    gin_g[...] = gain_grad
    dx[...] = x1_s[...] + part

    small_rows = small.reshape(1024, 128)
    small_rows[...] = jnp.zeros((1024, 128), F32)
    for r in range(4):
        total = unspread_row(taps_g, AT_TAPS, 14, 1792, r)
        if r == 0:
            for src, (start, n, width) in zip((gin_g, gffn_g, gmix_g, cbias_g), SMALLS):
                total = total + unspread_row(src, start, n, width)
        small_rows[pl.ds(r, 128, stride=8), :] = total


    swap(7, small.at[:, 1 - core], small_sib)
    swaps[8].wait_recv()
    hnow[0] = head_g[...] + hnow[3]
    moving = heads_go(0)
    for part in range(3):
        swaps[4 + part].wait_recv()
        products(PIECES_A[part], grad_a, z, za_sib, 0)
        if part == 2:
            swaps[7].wait_recv()
            tile = grad_a.at[:, :, :, :, pl.ds(4096, 128)]
            extra = small[:, core] + small_sib[...]
            tile[...] = (tile[...].astype(F32) + extra.reshape(4, 4, 4, 8, 128)).astype(BF16)
        sum_a.start(0, part)
    sum_b.finish(0)
    hnow[1] = heads_come(0, moving)
    moving = heads_go(1)
    sum_a.middle(0)
    sum_b.middle(1)
    sum_a.finish(0)
    hnow[2] = heads_come(1, moving)
    moving = heads_go(2)
    sum_b.finish(1)
    sum_a.middle(1)
    sum_b.middle(2)
    sum_a.finish(1)
    sum_b.finish(2)
    head_out[...] = heads_come(2, moving)
    sum_a.middle(2)
    sum_a.finish(2)
    sum_a.drain()
    sum_b.drain()
    for c in list(swaps.values()) + head_sent:
        c.wait_send()


def shapes_of(phase, cols):
    return (4,) * (2 - phase) + (8, cols)


def buffers(parts):
    return [pltpu.VMEM(shapes_of(phase, n), BF16) for c0, lo, hi in parts for phase in range(3)
            for n in (lo, hi, lo + hi, lo + hi)]


def backward_call(*args):
    def of(*s, t=F32):
        return jax.ShapeDtypeStruct(s, t)
    vm, hbm = pl.BlockSpec(memory_space=pltpu.VMEM), pl.BlockSpec(memory_space=pl.ANY)
    second = COLS - FIRST
    return pl.pallas_call(
        backward_kernel,
        out_shape=[of(128, 1024), of(8, COLS), of(8, 128)],
        in_specs=[vm] * 12 + [hbm] * 9,
        out_specs=[vm] * 3,
        scratch_shapes=[pltpu.VMEM(s, F32) for _, s in SAVED] + [
            pltpu.VMEM((1024, FIRST), BF16), pltpu.VMEM((128, FIRST), BF16), pltpu.VMEM((128, 1024), F32),
            pltpu.VMEM((128, 1792), F32), pltpu.VMEM((128, 128), F32), pltpu.VMEM((1, 1024), F32), pltpu.VMEM((1, 1536), F32),
            pltpu.VMEM((4, 1792), F32), pltpu.VMEM((1, 1792), F32), pltpu.VMEM((16, 2, 32, 128), F32),
            pltpu.VMEM((8, 128), F32), pltpu.VMEM((4, 4, 4, 8, FIRST), BF16), pltpu.VMEM((4, 4, 4, 8, second), BF16),
            pltpu.VMEM((128, second), BF16), pltpu.VMEM((128, FIRST), BF16), pltpu.VMEM((4, 16, 32, 128), BF16),
            pltpu.VMEM((16, 32, 128), F32), pltpu.SemaphoreType.DMA, pltpu.SemaphoreType.DMA((8,)),
            pltpu.SemaphoreType.DMA((9,)), pltpu.SemaphoreType.DMA((9,)),
            pltpu.VMEM((4, 8, 128), F32), pltpu.VMEM((3, 4, 8, 128), F32),
            pltpu.SemaphoreType.DMA((3, 3)), pltpu.SemaphoreType.DMA((3, 3)),
            pltpu.SemaphoreType.DMA((2, 3, 3, 6)), pltpu.SemaphoreType.DMA((2, 3, 3, 6)),
        ] + buffers(cut3(FIRST)) + buffers(cut3(second, FIRST)),
        compiler_params=pltpu.CompilerParams(collective_id=1, has_side_effects=True, vmem_limit_bytes=62 << 20),
        name="backward",
    )(*args)


SPLIT = ("gate", "inner", "query", "keyval", "mix", "attn", "gateup", "down")


def split_kernel(grads, head, *outs):
    for name, dst in zip(SPLIT, outs[:8]):
        start, n = OFF[name]
        dst[...] = grads[:, start:start + n]
    step, gin, gffn, gmix, cbias, taps, bias, decay, skip = outs[8:]
    tile = grads[:, 4096:4224]
    step[...] = tile[:, 0:24]
    gin[...] = tile[0:1, AT_IN:AT_IN + 8]
    gffn[...] = tile[0:1, AT_FFN:AT_FFN + 8]
    gmix[...] = tile[0:1, AT_MIX:AT_MIX + 12]
    cbias[...] = tile[0:1, AT_BIAS:AT_BIAS + 14]
    taps[...] = tile[0:4, AT_TAPS:AT_TAPS + 14]
    for r, dst in enumerate((bias, decay, skip)):
        dst[...] = head[r:r + 1, 0:24]


def split_call(grads, head):
    def of(*s):
        return jax.ShapeDtypeStruct(s, F32)
    vm = pl.BlockSpec(memory_space=pltpu.VMEM)
    return pl.pallas_call(
        split_kernel,
        out_shape=[of(8, OFF[k][1]) for k in SPLIT] + [of(8, 24), of(1, 8), of(1, 8), of(1, 12), of(1, 14), of(4, 14),
                                                       of(1, 24), of(1, 24), of(1, 24)],
        in_specs=[vm] * 2,
        out_specs=[vm] * 17,
        name="split",
    )(grads, head)


def body(tokens, seq_lengths, seq_owner, input_norm, gate_proj, inner_proj, step_proj, conv_weight, conv_bias, step_bias,
         decay_log, skip_gain, mixer_norm, mixer_out, query_proj, keyval_proj, attn_out, ffn_norm, gateup_proj, down_proj,
         out_grad):
    made = forward_call(gate_proj[0], inner_proj[0], step_proj[0], conv_weight[0], conv_bias, mixer_norm, mixer_out[0].T,
                        query_proj[0], keyval_proj[0], attn_out[0].T, input_norm, ffn_norm, gateup_proj[0], down_proj[0].T,
                        tokens, out_grad, seq_lengths.reshape(1, 256), seq_owner.reshape(1, 256), step_bias, decay_log,
                        skip_gain)
    weights, result, rt = made[:3]
    dx, grads, heads = backward_call(tokens, rt.reshape(4, 16, 2, 32, 128), *made[3:13], weights, *made[13:])
    (gate, inner, query, keyval, mix, attn, gateup, down, step, gin, gffn, gmix, cbias, taps, bias, decay,
     skip) = split_call(grads, heads)
    return (result, dx, gin, gate[None], inner[None], step[None], taps[None], cbias, bias, decay, skip, gmix, mix.T[None],
            query[None], keyval[None], attn.T[None], gffn, gateup[None], down.T[None])


def solution(mesh):
    split = Mesh(mesh.devices.reshape(4, 4, 2, mesh.shape["fsdp"]), DP_FSDP)
    rows, flat = P(DP_FSDP, None), P(None, DP_FSDP)
    weight, turned = P(None, DP_FSDP, None), P(None, None, DP_FSDP)
    in_specs = (rows, P(), P(), flat, weight, weight, weight, turned, flat, P(), P(), P(), flat, turned, weight, weight,
                turned, flat, weight, turned, rows)
    out_specs = (rows, rows, flat, weight, weight, weight, turned, flat, P(), P(), P(), flat, turned, weight, weight,
                 turned, flat, weight, turned)
    return jax.shard_map(body, mesh=split, in_specs=in_specs, out_specs=out_specs, check_vma=False)
```

```python
import functools
import math

import jax
import jax.numpy as jnp
from jax import lax
from jax.experimental import pallas as pl
from jax.experimental.pallas import tpu as pltpu
from jax.sharding import Mesh
from jax.sharding import PartitionSpec as P

EPSILON = 1e-05
ROPE_BASE = 100000000000.0
DP_FSDP = ("dp_0", "dp_1", "dp_2", "fsdp")
OFF = dict(gate=(0, 1536), inner=(1536, 1792), query=(3328, 512), keyval=(3840, 256), step=(4096, 128),
           mix=(4224, 1536), attn=(5760, 512), down=(6272, 2048), gateup=(8320, 4096))
COLS = 12416
GATEUP = ((0, 8320), (2048, 9344), (1024, 10368), (3072, 11392))
FIRST = 4224
F32, BF16 = jnp.float32, jnp.bfloat16
HIGH = lax.Precision.HIGHEST
AT_IN, AT_FFN, AT_MIX, AT_BIAS, AT_TAPS = 24, 32, 40, 52, 66
SMALLS = ((AT_IN, 8, 1024), (AT_FFN, 8, 1024), (AT_MIX, 12, 1536), (AT_BIAS, 14, 1792))
INVERSE = {8: 8192, 12: 5462, 14: 4682}


AX, AZ, AC, AY = "dp_0", "dp_1", "dp_2", "fsdp"
ORDERS = ((AX, AY, AZ), (AY, AZ, AX), (AZ, AX, AY))
MESH = pl.DeviceIdType.MESH
WHOLE = slice(None)


def places():
    return {a: lax.axis_index(a) for a in (AX, AZ, AC, AY)}


def greet_start(at):
    barrier = pltpu.get_barrier_semaphore()
    for a in (AX, AZ, AY):
        for d in (1, 2, 3):
            pl.semaphore_signal(barrier, inc=1, device_id={a: lax.rem(at[a] + d, 4)}, device_id_type=MESH)
    pl.semaphore_signal(barrier, inc=1, device_id={AC: 1 - at[AC]}, device_id_type=MESH)


def greet_end():
    pl.semaphore_wait(pltpu.get_barrier_semaphore(), 10)


def cut3(cols, start=0):
    tiles = cols // 128
    sizes = [tiles // 3 + (1 if k < tiles % 3 else 0) for k in range(3)]
    parts, at = [], start
    for n in sizes:
        lo = (n + 1) // 2 * 128
        parts.append((at, lo, n * 128 - lo))
        at += n * 128
    return parts


class Gather:
    def __init__(self, at, parts, shard, out, send, recv, sib_send, sib_recv):
        self.at, self.parts, self.shard, self.out = at, parts, shard, out
        self.sems, self.sib_sems = (send, recv), (sib_send, sib_recv)
        self.sent, self.sib, self.state = [], [], {}

    def block(self, sel, c0, n):
        return self.out.at[sel[AX], sel[AZ], self.at[AC], sel[AY], :, pl.ds(c0, n)]

    def to_sibling(self, part, k, sel, c0, n):
        ref = self.block(sel, c0, n)
        send, recv = self.sib_sems
        c = pltpu.make_async_remote_copy(ref, ref, send.at[part, k], recv.at[part, k],
                                         device_id={AC: 1 - self.at[AC]}, device_id_type=MESH)
        c.start()
        self.sib.append(c)

    def start(self, phase):
        send, recv = self.sems
        state = []
        for part, (c0, lo, hi) in enumerate(self.parts):
            order = ORDERS[part]
            a = order[phase]
            p = self.at[a]
            nxt, prv, opp = lax.rem(p + 1, 4), lax.rem(p + 3, 4), lax.rem(p + 2, 4)
            base = {b: self.at[b] for b in (AX, AZ, AY)}
            for b in order[:phase]:
                base[b] = WHOLE

            def mk(kind, q, cc, n, to, part=part, a=a, base=base):
                dst = self.block({**base, a: q}, cc, n)
                src = self.shard.at[:, pl.ds(cc, n)] if (phase == 0 and kind < 4) else dst
                return pltpu.make_async_remote_copy(src, dst, send.at[part, phase, kind], recv.at[part, phase, kind],
                                                    device_id={a: to}, device_id_type=MESH)
            if phase == 0:
                copies = [mk(k, p, c0, lo + hi, to) for k, to in enumerate((nxt, prv, opp))]
                for c in copies:
                    c.start()
                self.sent += copies
                state.append(copies)
                continue
            copies = [mk(0, p, c0, lo, nxt), mk(1, p, c0 + lo, hi, prv), mk(2, p, c0 + lo, hi, nxt), mk(3, p, c0, lo, prv)]
            for c in copies:
                c.start()
            self.sent += copies
            if phase == 2:
                self.to_sibling(part, 0, base, c0, lo + hi)
            state.append((copies, mk, nxt, prv, opp, base, a, c0, lo, hi))
        self.state[phase] = state

    def forward(self, phase):
        self.fwd = []
        for part, (copies, mk, nxt, prv, opp, base, a, c0, lo, hi) in enumerate(self.state[phase]):
            copies[0].wait_recv()
            fr = mk(4, prv, c0, lo, nxt)
            fr.start()
            copies[1].wait_recv()
            fl = mk(5, nxt, c0 + lo, hi, prv)
            fl.start()
            if phase == 2:
                self.to_sibling(part, 1, {**base, a: prv}, c0, lo)
                self.to_sibling(part, 2, {**base, a: nxt}, c0 + lo, hi)
            self.fwd.append((fr, fl))
            self.sent += [fr, fl]

    def sides(self, phase):
        for part, (copies, mk, nxt, prv, opp, base, a, c0, lo, hi) in enumerate(self.state[phase]):
            copies[2].wait_recv()
            if phase == 2:
                self.to_sibling(part, 3, {**base, a: prv}, c0 + lo, hi)
            copies[3].wait_recv()
            if phase == 2:
                self.to_sibling(part, 4, {**base, a: nxt}, c0, lo)

    def finish(self, phase):
        if phase == 0:
            for copies in self.state[0]:
                for c in copies:
                    c.wait_recv()
            return
        for part, (copies, mk, nxt, prv, opp, base, a, c0, lo, hi) in enumerate(self.state[phase]):
            fr, fl = self.fwd[part]
            fr.wait_recv()
            if phase == 2:
                self.to_sibling(part, 5, {**base, a: opp}, c0, lo)
            fl.wait_recv()
            if phase == 2:
                self.to_sibling(part, 6, {**base, a: opp}, c0 + lo, hi)

    def shared(self):
        for c in self.sib:
            c.wait_recv()

    def drain(self):
        for c in self.sent + self.sib:
            c.wait_send()


class Reduce:
    def __init__(self, at, parts, grad, first, out, bufs, send, recv):
        self.at, self.parts, self.grad, self.first, self.out, self.bufs = at, parts, grad, first, out, bufs
        self.sems, self.sent, self.state = (send, recv), [], {0: [], 1: [], 2: []}

    def start(self, phase, part):
        send, recv = self.sems
        c0, lo, hi = self.parts[part]
        order = ORDERS[part][::-1]
        a = order[phase]
        p = self.at[a]
        nxt, prv, opp = lax.rem(p + 1, 4), lax.rem(p + 3, 4), lax.rem(p + 2, 4)
        base = {b: self.at[b] for b in (AX, AZ, AY)}
        for b in order[phase + 1:]:
            base[b] = WHOLE
        el, er, fr, fl = self.bufs[(part * 3 + phase) * 4:(part * 3 + phase) * 4 + 4]

        def ref(q, cc, n):
            sel = {**base, a: q}
            return self.grad.at[sel[AX], sel[AZ], sel[AY], :, pl.ds(cc - self.first, n)]

        def mk(kind, q, cc, n, dst, to):
            return pltpu.make_async_remote_copy(ref(q, cc, n), dst, send.at[part, phase, kind],
                                                recv.at[part, phase, kind], device_id={a: to}, device_id_type=MESH)
        if phase == 2:
            now = [mk(k, q, c0, lo + hi, dst, q) for k, (q, dst) in enumerate(((nxt, el), (prv, er), (opp, fr)))]
            for c in now:
                c.start()
            self.sent += now
            self.state[2].append((now, ref(p, c0, lo + hi), (el, er, fr)))
            return
        lead = (WHOLE,) * (3 - phase)
        fr_lo, fr_hi = fr.at[lead + (pl.ds(0, lo),)], fr.at[lead + (pl.ds(lo, hi),)]
        fl_lo, fl_hi = fl.at[lead + (pl.ds(0, lo),)], fl.at[lead + (pl.ds(lo, hi),)]
        now = [mk(0, opp, c0, lo, el, prv), mk(1, opp, c0 + lo, hi, er, nxt), mk(2, prv, c0 + lo, hi, fr_hi, prv),
               mk(3, nxt, c0, lo, fl_lo, nxt)]
        for c in now:
            c.start()
        later = [mk(4, prv, c0, lo, fr_lo, prv), mk(5, nxt, c0 + lo, hi, fl_hi, nxt)]
        self.sent += now + later
        self.state[phase].append((now, later, ref(prv, c0, lo), ref(nxt, c0 + lo, hi), ref(p, c0, lo + hi), el, er, fr, fl))

    def each(self, phase, fn):
        def one(k, carry):
            fn(((k // 4, k % 4) if phase == 0 else (k,)) + (WHOLE, WHOLE))
            return carry
        lax.fori_loop(0, 16 if phase == 0 else 4, one, 0)

    def middle(self, phase):
        for now, later, left, right, own, el, er, fr, fl in self.state[phase]:
            for c, onward, target, come in ((now[0], later[0], left, el), (now[1], later[1], right, er)):
                c.wait_recv()

                def add(ix, target=target, come=come):
                    target[ix] = target[ix] + come[ix]
                self.each(phase, add)
                onward.start()

    def last(self):
        for (c0, lo, hi), (now, own, come) in zip(self.parts, self.state[2]):
            for c in now:
                c.wait_recv()
            total = own[...].astype(F32)
            for ref in come:
                total = total + ref[...].astype(F32)
            self.out[:, pl.ds(c0, lo + hi)] = total

    def finish(self, phase):
        for part, (now, later, left, right, own, el, er, fr, fl) in enumerate(self.state[phase]):
            for c in (now[2], now[3], later[0], later[1]):
                c.wait_recv()

            def total(ix, own=own, fl=fl, fr=fr):
                v = own[ix].astype(F32) + fl[ix].astype(F32) + fr[ix].astype(F32)
                own[ix] = v.astype(BF16)
            self.each(phase, total)
            self.start(phase + 1, part)

    def drain(self):
        for c in self.sent:
            c.wait_send()


def assemble(pieces, shard, tile):
    gate, inner, step, taps, cbias, mixer, mix, query, keyval, attn, gin, gffn, gateup, down = pieces
    for src, dst in GATEUP:
        shard[:, dst:dst + 1024] = gateup[:, src:src + 1024]
    for ref, (c0, n) in ((gate, OFF["gate"]), (inner, OFF["inner"]), (query, OFF["query"]), (keyval, OFF["keyval"]),
                         (mix, OFF["mix"]), (attn, OFF["attn"]), (down, OFF["down"])):
        shard[:, c0:c0 + n] = ref[...]
    tile[...] = jnp.zeros((8, 128), F32)
    tile[:, 0:24] = step[...].astype(F32)
    tile[0:1, AT_IN:AT_IN + 8] = gin[...].astype(F32)
    tile[0:1, AT_FFN:AT_FFN + 8] = gffn[...].astype(F32)
    tile[0:1, AT_MIX:AT_MIX + 12] = mixer[...].astype(F32)
    tile[0:1, AT_BIAS:AT_BIAS + 14] = cbias[...].astype(F32)
    tile[0:4, AT_TAPS:AT_TAPS + 14] = taps[...].astype(F32)
    shard[:, 4096:4224] = tile[...].astype(BF16)


def nn(a, b, precision=None):
    return lax.dot_general(a, b, (((1,), (0,)), ((), ())), preferred_element_type=F32, precision=precision)


def nt(a, b, precision=None):
    return lax.dot_general(a, b, (((1,), (1,)), ((), ())), preferred_element_type=F32, precision=precision)


def tn(a, b, precision=None):
    return lax.dot_general(a, b, (((0,), (0,)), ((), ())), preferred_element_type=F32, precision=precision)


def sigmoid(v):
    return 1.0 / (1.0 + jnp.exp(-v))


def cols_of(i, n, start=0):
    return pl.ds(pl.multiple_of(start + i * n, 128), n)


def rms_back(values, scale, gain, grad):
    inner = grad * gain
    mean = jnp.mean(values * inner, axis=-1, keepdims=True)
    return scale * inner - values * (scale * scale * scale * mean), jnp.sum(grad * values * scale, axis=0, keepdims=True)


def row_scale(values):
    return lax.rsqrt(jnp.mean(values * values, axis=-1, keepdims=True) + EPSILON)


def selectors(i, start, n):
    d = lax.broadcasted_iota(jnp.int32, (128, 128), 1) + 128 * i
    row = lax.broadcasted_iota(jnp.int32, (128, 128), 0)
    owner = lax.shift_right_logical(d * INVERSE[n], 16)
    return row == owner, row == start + d - n * owner


def spread_row(table, start, n, width, dst, row=0):
    for i in range(width // 128):
        owned, lane = selectors(i, start, n)
        v = nn(table, lane.astype(F32).astype(BF16))
        dst[row:row + 1, 128 * i:128 * i + 128] = jnp.sum(jnp.where(owned, v, 0.0), axis=0, keepdims=True)


def unspread_row(src, start, n, width, row=0):
    total = jnp.zeros((128, 128), F32)
    for i in range(width // 128):
        owned, lane = selectors(i, start, n)
        held = jnp.where(owned, src[row:row + 1, 128 * i:128 * i + 128], 0.0)
        total = total + nt(held.astype(BF16), lane.astype(F32).astype(BF16))
    return total


GROUPS = ((0, FIRST), (FIRST, 4096), (8320, 2048), (10368, 2048))
SAVED = ((128, FIRST), (128, 1792), (128, 1792), (128, 1536), (24, 128, 128), (8, 128, 128), (128, 512), (9, 128, 128),
         (128, 1024), (128, 1024), (128, COLS - FIRST), (4096, 128))
KINDS = (F32,) * 10 + (BF16,) * 2


def forward_kernel(*refs):
    pieces, (x_ref, og_ref, lengths, owners, sbias_ref, dlog_ref, skip_ref) = refs[:14], refs[14:21]
    w, gffn_g, gin, gmix, taps, skipx, rows_s, zb_sib, rt_sib = refs[21:30]
    kept, (proj, csum, conv, yfull, dec, soft, qr, misc, dx1_s, x1_s, zb, rt) = refs[30:42], refs[42:54]
    (wv, df_s, da_s, gffn, cbias, table, shard, tile, wsem, own_sem, keep_sem, sems, sib_sems, x_send, x_recv) = refs[54:]
    at = places()
    greet_start(at)
    assemble(pieces, shard, tile)
    greet_end()
    own = pltpu.make_async_copy(shard, w.at[at[AX], at[AZ], at[AC], at[AY]], own_sem)
    own.start()
    groups = [Gather(at, cut3(n, c0), shard, w, sems.at[0, k], sems.at[1, k], sib_sems.at[0, k], sib_sems.at[1, k])
              for k, (c0, n) in enumerate(GROUPS)]
    one, two, three, four = groups
    for g in groups:
        g.start(0)
    lane = lax.broadcasted_iota(jnp.int32, (128, 128), 1)
    sub = lax.broadcasted_iota(jnp.int32, (128, 128), 0)
    low_lanes = lane < 64

    me = ((at[AX] * 4 + at[AZ]) * 2 + at[AC]) * 4 + at[AY]
    owned = owners[...] == me
    held = jnp.where(owned, lengths[...], 0).astype(F32)
    before = lax.broadcasted_iota(jnp.int32, (256, 256), 0) <= lax.broadcasted_iota(jnp.int32, (256, 256), 1)
    ends = nn(jnp.broadcast_to(held, (8, 256)).astype(BF16), before.astype(F32).astype(BF16))[0:1, :]
    slot = lax.broadcasted_iota(jnp.int32, (128, 256), 0).astype(F32)
    closed = jnp.broadcast_to(owned.astype(F32), (128, 256)) * (jnp.broadcast_to(ends, (128, 256)) <= slot).astype(F32)
    segment = jnp.sum(closed, axis=1, keepdims=True)
    begins = jnp.max(closed * ends, axis=1, keepdims=True)
    used = jnp.max(ends, axis=1, keepdims=True)
    slots = sub.astype(F32)
    position = jnp.broadcast_to(slots[:, 0:1] - begins, (128, 128))
    active = (slots[:, 0:1] < used).astype(F32)
    segments = jnp.broadcast_to(segment, (128, 128))
    allowed = (segments == segments.T) & (sub >= lane)
    speeds = jnp.exp((lane % 32).astype(F32) * (-math.log(ROPE_BASE) * 2.0 / 64))
    angles = position * speeds
    cosine, sine = jnp.cos(angles), jnp.sin(angles)

    rows_s[...] = jnp.zeros((8, 128), F32)
    rows_s[0:1, 0:24] = sbias_ref[...].astype(F32)
    rows_s[1:2, 0:24] = dlog_ref[...].astype(F32)
    rows_s[2:3, 0:24] = skip_ref[...].astype(F32)
    sbias, dlog = rows_s[0:1, :], rows_s[1:2, :]
    heads_low = rows_s[...].astype(BF16)
    for i in range(12):
        of_head = (sub == 2 * i + lax.shift_right_logical(lane, 6)).astype(F32).astype(BF16)
        skipx[:, 128 * i:128 * i + 128] = nn(heads_low, of_head)[2:3, :]

    def halves(v):
        return jnp.where(low_lanes, v, 0.0), jnp.where(low_lanes, 0.0, v)

    def stacked(v):
        lo, hi = halves(v)
        return jnp.concatenate([lo, hi], axis=0).astype(BF16)

    own.wait()
    for g in groups:
        g.finish(0)
        g.start(1)
    for g in groups:
        g.forward(1)
    one.sides(1)
    one.finish(1)
    one.start(2)
    one.forward(2)
    two.sides(1)
    two.finish(1)
    two.start(2)
    one.sides(2)
    one.finish(2)
    two.forward(2)
    for g in (three, four):
        g.sides(1)
        g.finish(1)
        g.start(2)
    one.shared()
    rows_of_w = w.reshape(1024, COLS)

    def load(k, c0, n):
        c = pltpu.make_async_copy(rows_of_w.at[:, pl.ds(c0, n)], wv.at[:, pl.ds(c0, n)], wsem.at[k])
        c.start()
        return c
    swaps = []
    rt5 = rt.reshape(4, 16, 2, 32, 128)

    def swap(k, src, dst):
        c = pltpu.make_async_remote_copy(src, dst, x_send.at[k], x_recv.at[k], device_id={AC: 1 - at[AC]},
                                         device_id_type=MESH)
        c.start()
        swaps.append(c)

    def swap_rows(g):
        swap(g, rt5.at[g, :, 1 - at[AC]], rt_sib.at[g])

    def swap_columns(k, c0):
        swap(k, zb.at[:, pl.ds(c0, 2048)], zb_sib.at[:, pl.ds(c0, 2048)])
    load(0, 0, FIRST).wait()
    table[...] = wv[:, 4096:4224].astype(F32)
    tables = [table[pl.ds(r, 128, stride=8), :].astype(BF16) for r in range(4)]
    for dst, (start, n, width) in zip((gin, gffn, gmix, cbias), SMALLS):
        spread_row(tables[0], start, n, width, dst)
    for r in range(4):
        spread_row(tables[r], AT_TAPS, 14, 1792, taps, r)

    x = x_ref[...].astype(F32)
    h = (x * row_scale(x) * gin[...]).astype(BF16)
    rt[0:1024, :] = h.T
    g0 = og_ref[...].astype(F32) * active
    glow = g0.astype(BF16)
    rt[3072:4096, :] = glow.T
    swap_rows(0)
    swap_rows(3)
    z_h = h

    def project(i, carry):
        proj[:, cols_of(i, 384)] = nn(z_h, wv[:, cols_of(i, 384)])
        return carry
    lax.fori_loop(0, 11, project, 0)

    def convolve(i, carry):
        cs = cols_of(i, 128)
        p = proj[:, cols_of(i, 128, 1536)]
        total = p * taps[3:4, cs]
        for j in (1, 2, 3):
            moved = jnp.where(position >= float(j), pltpu.roll(p, j, axis=0), 0.0)
            total = total + moved * taps[3 - j:4 - j, cs]
        total = total + cbias[:, cs]
        csum[:, cs] = total
        conv[:, cs] = total * sigmoid(total)
        return carry
    lax.fori_loop(0, 14, convolve, 0)

    step = proj[:, 4096:4224] + sbias
    dt = jnp.maximum(step, 0.0) + jnp.log(1.0 + jnp.exp(-jnp.abs(step)))
    rate = -jnp.exp(dlog)
    lower = (sub >= lane).astype(F32)
    level = nn(lower, dt * rate, HIGH)
    dt_t = dt.T
    level_t = level.T
    b_mat = conv[:, 1536:1664]
    c_mat = conv[:, 1664:1792]
    inter = nt(c_mat, b_mat, HIGH)

    square = jnp.zeros((128, 1), F32)
    for t in range(6):
        cs = slice(128 * t, 128 * t + 128)
        mixes = []
        for n in (2 * t, 2 * t + 1):
            spread = jnp.where(allowed, level[:, n:n + 1] - level_t[n:n + 1, :], -1e30)
            decay = jnp.exp(spread)
            dec[n] = decay
            mixes.append((decay * inter * dt_t[n:n + 1, :]).astype(BF16))
        xs = conv[:, cs]
        y = nn(jnp.concatenate(mixes, axis=1), stacked(xs)) + skipx[:, cs] * xs
        yfull[:, cs] = y
        gate = proj[:, cs]
        gy = y * (gate * sigmoid(gate))
        square = square + jnp.sum(gy * gy, axis=1, keepdims=True)
    two.sides(2)
    two.finish(2)
    three.forward(2)
    for t in range(6, 12):
        cs = slice(128 * t, 128 * t + 128)
        mixes = []
        for n in (2 * t, 2 * t + 1):
            spread = jnp.where(allowed, level[:, n:n + 1] - level_t[n:n + 1, :], -1e30)
            decay = jnp.exp(spread)
            dec[n] = decay
            mixes.append((decay * inter * dt_t[n:n + 1, :]).astype(BF16))
        xs = conv[:, cs]
        y = nn(jnp.concatenate(mixes, axis=1), stacked(xs)) + skipx[:, cs] * xs
        yfull[:, cs] = y
        gate = proj[:, cs]
        gy = y * (gate * sigmoid(gate))
        square = square + jnp.sum(gy * gy, axis=1, keepdims=True)
    rmix = lax.rsqrt(square * (1.0 / 1536) + EPSILON)

    def mixer_norm(i, carry):
        cs = cols_of(i, 128)
        gate = proj[:, cs]
        gy = yfull[:, cs] * (gate * sigmoid(gate))
        zb[:, cols_of(i, 128)] = (gy * rmix * gmix[:, cs]).astype(BF16)
        return carry
    lax.fori_loop(0, 12, mixer_norm, 0)

    four.forward(2)
    first = (lane % 64) < 32

    def turn(v, sign):
        side = jnp.where(first, -pltpu.roll(v, 96, axis=1), pltpu.roll(v, 32, axis=1))
        return v * cosine + sign * side * sine

    def dup(v, j):
        other = pltpu.roll(v, 64, axis=1)
        return jnp.where(low_lanes, v, other) if j == 0 else jnp.where(low_lanes, other, v)
    key_t = turn(proj[:, 3840:3968], 1.0).astype(BF16).astype(F32)
    val = proj[:, 3968:4096].astype(BF16).astype(F32)
    keys = [dup(key_t, j) for j in (0, 1)]
    vals = [dup(val, j) for j in (0, 1)]
    for t in range(4):
        cs = slice(128 * t, 128 * t + 128)
        q = turn(proj[:, 3328 + 128 * t:3456 + 128 * t], 1.0).astype(BF16).astype(F32)
        qr[:, cs] = q
        scores = nt(stacked(q), keys[t // 2].astype(BF16)) * 0.125
        weights = []
        for e in (0, 1):
            s = jnp.where(allowed, scores[128 * e:128 * e + 128], -1e30)
            w = jnp.exp(s - jnp.max(s, axis=1, keepdims=True))
            w = w / jnp.sum(w, axis=1, keepdims=True)
            soft[2 * t + e] = w
            weights.append(w.astype(BF16))
        zb[:, 1536 + 128 * t:1664 + 128 * t] = nn(jnp.concatenate(weights, axis=1), stacked(vals[t // 2])).astype(BF16)

    for k, v in enumerate((key_t, val, dt, step, inter, jnp.broadcast_to(rmix, (128, 128)), position, cosine, sine)):
        misc[k] = v
    keeps = []

    def keep(*which):
        for k in which:
            c = pltpu.make_async_copy(refs[42 + k], kept[k], keep_sem.at[k])
            c.start()
            keeps.append(c)
    keep(0, 1, 2, 3, 4, 5, 6, 7)
    swap_columns(4, 0)
    two.shared()
    loads = [load(1, 4224, 4096)]
    three.sides(2)
    four.sides(2)
    loads[0].wait()
    for i in range(4):
        rows = slice(256 * i, 256 * i + 256)
        x1_s[:, rows] = x_ref[:, rows].astype(F32) + nt(zb[:, 0:2048], wv[rows, 4224:6272])
    x1 = x1_s[...]
    r1 = row_scale(x1)
    f = (x1 * r1 * gffn[...]).astype(BF16)
    rt[2048:3072, :] = f.T
    swap_rows(2)
    three.finish(2)

    def back_down(i, carry):
        da_s[:, cols_of(i, 512)] = nn(glow, wv[:, cols_of(i, 512, 6272)])
        return carry
    lax.fori_loop(0, 4, back_down, 0)

    four.finish(2)

    for k, g in enumerate((three, four)):
        base = 8320 + 2048 * k
        g.shared()
        load(2 + k, base, 2048).wait()
        for i in range(4):
            gate = nn(f, wv[:, base + 256 * i:base + 256 * i + 256])
            up = nn(f, wv[:, base + 1024 + 256 * i:base + 1280 + 256 * i])
            da = da_s[:, 1024 * k + 256 * i:1024 * k + 256 * i + 256]
            s = sigmoid(gate)
            gs = gate * s
            at_a, at_g = 2048 + 1024 * k + 256 * i, 4096 + 2048 * k + 256 * i
            zb[:, at_a:at_a + 256] = (gs * up).astype(BF16)
            zb[:, at_g:at_g + 256] = (da * up * (s + gs * (1.0 - s))).astype(BF16)
            zb[:, at_g + 1024:at_g + 1280] = (da * gs).astype(BF16)
        swap_columns(5 + k, 4096 + 2048 * k)
        if k == 1:
            swap_columns(7, 2048)
            keep(9, 10)
        for i in range(4):
            rows = slice(256 * i, 256 * i + 256)
            term = nt(zb[:, 4096 + 2048 * k:6144 + 2048 * k], wv[rows, base:base + 2048])
            df_s[:, rows] = term if k == 0 else df_s[:, rows] + term
    part, gain_grad = rms_back(x1_s[...], r1, gffn[...], df_s[...])
    gffn_g[...] = gain_grad
    dx1 = g0 + part
    dx1_s[...] = dx1
    rt[1024:2048, :] = dx1.astype(BF16).T
    swap_rows(1)
    keep(8, 11)
    for g in groups:
        g.drain()
    for c in swaps:
        c.wait()
    for c in keeps:
        c.wait()


def forward_call(*args):
    def of(*s, t=F32):
        return jax.ShapeDtypeStruct(s, t)
    vm, hbm = pl.BlockSpec(memory_space=pltpu.VMEM), pl.BlockSpec(memory_space=pl.ANY)
    return pl.pallas_call(
        forward_kernel,
        out_shape=[of(4, 4, 2, 4, 8, COLS, t=BF16), of(1, 1024), of(1, 1024), of(1, 1536),
                   of(4, 1792), of(1, 1536), of(8, 128), of(128, COLS - FIRST, t=BF16), of(4, 16, 32, 128, t=BF16)]
        + [of(*s, t=t) for s, t in zip(SAVED, KINDS)],
        in_specs=[vm] * 21,
        out_specs=[hbm] + [vm] * 6 + [hbm] * 14,
        scratch_shapes=[pltpu.VMEM(s, t) for s, t in zip(SAVED, KINDS)] + [
            pltpu.VMEM((1024, COLS), BF16), pltpu.VMEM((128, 1024), F32), pltpu.VMEM((128, 2048), F32),
            pltpu.VMEM((1, 1024), F32), pltpu.VMEM((1, 1792), F32), pltpu.VMEM((1024, 128), F32), pltpu.VMEM((8, COLS), BF16),
            pltpu.VMEM((8, 128), F32), pltpu.SemaphoreType.DMA((10,)), pltpu.SemaphoreType.DMA,
            pltpu.SemaphoreType.DMA((12,)), pltpu.SemaphoreType.DMA((2, 4, 3, 3, 6)), pltpu.SemaphoreType.DMA((2, 4, 3, 7)),
            pltpu.SemaphoreType.DMA((8,)), pltpu.SemaphoreType.DMA((8,)),
        ],
        compiler_params=pltpu.CompilerParams(collective_id=0, has_side_effects=True, vmem_limit_bytes=60 << 20),
        name="forward",
    )(*args)


PIECES_A = (((0, 0, 1280, 256), (0, 1280, 128, 128)), ((0, 1408, 1280, 256), (0, 2688, 128, 128)),
            ((0, 2816, 1280, 256), (0, 4096, 128, 128)))
PIECES_B = (((1, 4224, 2048, 256), (3, 6272, 768, 256)), ((3, 7040, 1280, 256), (2, 8320, 1280, 256), (2, 9600, 128, 128)),
            ((2, 9728, 2688, 384),))


def backward_kernel(x_ref, gffn_g, gin, gmix, taps, skipx, rows_s, w, zb_sib_in, rt_sib_in, *refs):
    kept, (result, dx, out, head_out) = refs[:12], refs[12:16]
    proj, csum, conv, yfull, dec, soft, qr, misc, dx1_s, x1_s, zb, rt = refs[16:28]
    (wv, z, df_s, dm_s, do_s, dconv, ddt_s, gin_g, gmix_g, taps_g, cbias_g, small, head_g, grad_a, grad_b, zb_sib, za_sib,
     rt_sib, small_sib, wsem, keep_sem, x_send, x_recv, hnow, hbuf, h_send, h_recv, a_sems, b_sems) = refs[28:57]
    bufs_a, bufs_b = refs[57:93], refs[93:129]
    at = places()
    greet_start(at)

    def bring(k, src, dst):
        c = pltpu.make_async_copy(src, dst, keep_sem.at[k])
        c.start()
        return c
    sides = [bring(12, kept[11], rt), bring(13, rt_sib_in, rt_sib)]
    parts_a, parts_b = cut3(FIRST), cut3(COLS - FIRST, FIRST)
    columns = []
    for part, (c0, lo, hi) in enumerate(parts_b):
        cs = pl.ds(c0 - FIRST, lo + hi)
        columns.append((bring(14 + part, kept[10].at[:, cs], zb.at[:, cs]),
                        bring(17 + part, zb_sib_in.at[:, cs], zb_sib.at[:, cs])))
    keeps = [bring(k, kept[k], refs[16 + k]) for k in range(10)]
    rows_of_w = w.reshape(1024, COLS)
    load = pltpu.make_async_copy(rows_of_w.at[:, pl.ds(FIRST, 4096)], wv.at[:, pl.ds(0, 4096)], wsem.at[0])
    load.start()
    core = at[AC]
    rt = rt.reshape(4, 16, 2, 32, 128)
    swaps = {}

    def swap(k, src, dst):
        c = pltpu.make_async_remote_copy(src, dst, x_send.at[k], x_recv.at[k], device_id={AC: 1 - core}, device_id_type=MESH)
        c.start()
        swaps[k] = c

    def swap_columns(k, src, dst, part, first):
        c0, lo, hi = part
        cs = pl.ds(c0 - first, lo + hi)
        swap(k, src.at[:, cs], dst.at[:, cs])

    def products(pieces, grad, mine, other, first):
        for g, c0, n, width in pieces:
            left = jnp.concatenate([rt[g, :, core].reshape(512, 128), rt_sib[g].reshape(512, 128)], axis=1)

            def one(i, carry, c0=c0, width=width, left=left):
                cs = pl.ds(pl.multiple_of(c0 - first + i * width, 128), width)
                right = jnp.concatenate([mine[:, cs], other[:, cs]], axis=0)
                grad[:, :, :, :, cs] = nn(left, right).reshape(4, 4, 4, 8, width).astype(BF16)
                return carry
            lax.fori_loop(0, n // width, one, 0)

    sum_a = Reduce(at, parts_a, grad_a, 0, out, bufs_a, a_sems.at[0], a_sems.at[1])
    sum_b = Reduce(at, parts_b, grad_b, FIRST, out, bufs_b, b_sems.at[0], b_sems.at[1])
    for c in sides:
        c.wait()
    for part in range(3):
        for c in columns[part]:
            c.wait()
        products(PIECES_B[part], grad_b, zb, zb_sib, FIRST)
        if part == 0:
            greet_end()
        sum_b.start(0, part)

    axes, head_sent = (AX, AZ, AY), []

    def heads_go(k):
        a = axes[k]
        p = at[a]
        hbuf[k, p] = hnow[k]
        copies = []
        for d in (1, 2, 3):
            c = pltpu.make_async_remote_copy(hnow.at[k], hbuf.at[k, p], h_send.at[k, d - 1], h_recv.at[k, d - 1],
                                             device_id={a: lax.rem(p + d, 4)}, device_id_type=MESH)
            c.start()
            copies.append(c)
        head_sent.extend(copies)
        return copies

    def heads_come(k, copies):
        for c in copies:
            c.wait_recv()
        return ((hbuf[k, 0] + hbuf[k, 1]) + hbuf[k, 2]) + hbuf[k, 3]

    lane = lax.broadcasted_iota(jnp.int32, (128, 128), 1)
    sub = lax.broadcasted_iota(jnp.int32, (128, 128), 0)
    low_lanes = lane < 64
    def halves(v):
        return jnp.where(low_lanes, v, 0.0), jnp.where(low_lanes, 0.0, v)

    def stacked(v):
        lo, hi = halves(v)
        return jnp.concatenate([lo, hi], axis=0).astype(BF16)

    for c in keeps:
        c.wait()
    load.wait()
    blow = dx1_s[...].astype(BF16)

    def back_branch(i, carry):
        dm_s[:, cols_of(i, 512)] = nn(blow, wv[:, cols_of(i, 512)])
        return carry
    lax.fori_loop(0, 3, back_branch, 0)
    do_s[...] = nn(blow, wv[:, 1536:2048])
    for i in range(4):
        rows = slice(256 * i, 256 * i + 256)
        result[:, rows] = (x1_s[:, rows] + nt(zb[:, 2048:4096], wv[rows, 2048:4096])).astype(BF16)
    load = pltpu.make_async_copy(rows_of_w.at[:, pl.ds(0, FIRST)], wv, wsem.at[1])
    load.start()
    key_t, val, dt, step, inter, rmix, position, cosine, sine = [misc[k] for k in range(9)]
    rmix = rmix[:, 0:1]
    first = (lane % 64) < 32

    def turn(v, sign):
        side = jnp.where(first, -pltpu.roll(v, 96, axis=1), pltpu.roll(v, 32, axis=1))
        return v * cosine + sign * side * sine

    def dup(v, j):
        other = pltpu.roll(v, 64, axis=1)
        return jnp.where(low_lanes, v, other) if j == 0 else jnp.where(low_lanes, other, v)
    keys = [dup(key_t, j) for j in (0, 1)]
    vals = [dup(val, j) for j in (0, 1)]
    dks, dvs = [], []
    for t in range(4):
        cs = slice(128 * t, 128 * t + 128)
        do2 = stacked(do_s[:, cs])
        dp = nt(do2, vals[t // 2].astype(BF16))
        ds, ws = [], []
        for e in (0, 1):
            w = soft[2 * t + e]
            d = dp[128 * e:128 * e + 128]
            ds.append((w * (d - jnp.sum(d * w, axis=1, keepdims=True)) * 0.125).astype(BF16))
            ws.append(w.astype(BF16))
        dq = nn(jnp.concatenate(ds, axis=1), stacked(keys[t // 2]))
        z[:, 3328 + 128 * t:3456 + 128 * t] = turn(dq, -1.0).astype(BF16)
        dks.append(tn(jnp.concatenate(ds, axis=0), stacked(qr[:, cs])))
        dvs.append(tn(jnp.concatenate(ws, axis=0), do2))

    def fold(parts):
        a, b = parts[0] + parts[1], parts[2] + parts[3]
        return jnp.where(low_lanes, a + pltpu.roll(a, 64, axis=1), b + pltpu.roll(b, 64, axis=1))
    z[:, 3840:3968] = turn(fold(dks), -1.0).astype(BF16)
    z[:, 3968:4096] = fold(dvs).astype(BF16)

    dt_t = dt.T
    rate = -jnp.exp(rows_s[1:2, :])
    b_mat = conv[:, 1536:1664]
    c_mat = conv[:, 1664:1792]
    dots = jnp.zeros((128, 1), F32)
    for t in range(12):
        cs = slice(128 * t, 128 * t + 128)
        gate = proj[:, cs]
        gy = yfull[:, cs] * (gate * sigmoid(gate))
        dm = dm_s[:, cs]
        gmix_g[:, cs] = jnp.sum(dm * gy * rmix, axis=0, keepdims=True)
        dots = dots + jnp.sum(gy * dm * gmix[:, cs], axis=1, keepdims=True)
    pull = rmix * rmix * rmix * dots * (1.0 / 1536)
    ddt_s[...] = jnp.zeros((128, 128), F32)
    dlevel = jnp.zeros((128, 128), F32)
    dskip = jnp.zeros((1, 128), F32)
    lane_row = lane[0:1, :]
    dinter = jnp.zeros((128, 128), F32)
    for t in range(12):
        cs = slice(128 * t, 128 * t + 128)
        gate = proj[:, cs]
        s = sigmoid(gate)
        gs = gate * s
        y = yfull[:, cs]
        dgy = rmix * (gmix[:, cs] * dm_s[:, cs]) - y * gs * pull
        z[:, cs] = (dgy * y * (s + gs * (1.0 - s))).astype(BF16)
        dy = dgy * gs
        xs = conv[:, cs]
        skipped = jnp.sum(dy * xs, axis=0, keepdims=True)
        for e in (0, 1):
            in_head = (lane_row < 64) if e == 0 else (lane_row >= 64)
            dskip = dskip + jnp.where(lane_row == 2 * t + e,
                                      jnp.sum(jnp.where(in_head, skipped, 0.0), axis=1, keepdims=True), 0.0)
        dy2 = stacked(dy)
        dmix = nt(dy2, xs.astype(BF16))
        mixes = []
        for e in (0, 1):
            n = 2 * t + e
            dt_row = dt_t[n:n + 1, :]
            decay = dec[n]
            mixed = decay * inter
            dm = dmix[128 * e:128 * e + 128]
            mixes.append((mixed * dt_row).astype(BF16))
            dd = dm * dt_row
            dinter = dinter + dd * decay
            ddt_s[n:n + 1, :] = jnp.sum(dm * mixed, axis=0, keepdims=True)
            dlevel = dlevel + jnp.where(lane == n, jnp.sum(dd * mixed, axis=1, keepdims=True), 0.0)
        dconv[:, cs] = tn(jnp.concatenate(mixes, axis=0), dy2) + skipx[:, cs] * dy
    sum_b.middle(0)
    dconv[:, 1536:1664] = tn(dinter, c_mat, HIGH)
    dconv[:, 1664:1792] = nn(dinter, b_mat, HIGH)
    ddt = ddt_s[...].T
    dlevel = dlevel - ddt * dt
    upper = (sub <= lane).astype(F32)
    drate = nn(upper, dlevel, HIGH)
    dstep = jnp.where(lane < 24, (ddt + drate * rate) * sigmoid(step), 0.0)
    z[:, 4096:4224] = dstep.astype(BF16)
    head_g[...] = jnp.zeros((8, 128), F32)
    head_g[2:3, :] = dskip
    head_g[0:1, :] = jnp.sum(dstep, axis=0, keepdims=True)
    head_g[1:2, :] = jnp.sum(drate * dt * rate, axis=0, keepdims=True)

    def unconvolve(i, carry):
        cs = cols_of(i, 128)
        total = csum[:, cs]
        s = sigmoid(total)
        d = dconv[:, cs] * (s + total * s * (1.0 - s))
        p = proj[:, cols_of(i, 128, 1536)]
        cbias_g[:, cs] = jnp.sum(d, axis=0, keepdims=True)
        taps_g[3:4, cs] = jnp.sum(d * p, axis=0, keepdims=True)
        back = d * taps[3:4, cs]
        for j in (1, 2, 3):
            masked = jnp.where(position >= float(j), d, 0.0)
            taps_g[3 - j:4 - j, cs] = jnp.sum(masked * pltpu.roll(p, j, axis=0), axis=0, keepdims=True)
            back = back + pltpu.roll(masked, 128 - j, axis=0) * taps[3 - j:4 - j, cs]
        z[:, cols_of(i, 128, 1536)] = back.astype(BF16)
        return carry
    lax.fori_loop(0, 14, unconvolve, 0)

    for part in range(3):
        swap_columns(4 + part, z, za_sib, parts_a[part], 0)
    swap(8, head_g, hnow.at[3])
    for part in range(2):
        swaps[4 + part].wait_recv()
        products(PIECES_A[part], grad_a, z, za_sib, 0)
        sum_a.start(0, part)
    swaps[8].wait_recv()
    hnow[0] = head_g[...] + hnow[3]
    moving = heads_go(0)
    load.wait()
    for i in range(4):
        rows = slice(256 * i, 256 * i + 256)
        df_s[:, rows] = nt(z[:, 0:FIRST], wv[rows, 0:FIRST])
    x = x_ref[...].astype(F32)
    part, gain_grad = rms_back(x, row_scale(x), gin[...], df_s[...])
    gin_g[...] = gain_grad
    dx[...] = dx1_s[...] + part

    small_rows = small.reshape(1024, 128)
    small_rows[...] = jnp.zeros((1024, 128), F32)
    for r in range(4):
        total = unspread_row(taps_g, AT_TAPS, 14, 1792, r)
        if r == 0:
            for src, (start, n, width) in zip((gin_g, gffn_g, gmix_g, cbias_g), SMALLS):
                total = total + unspread_row(src, start, n, width)
        small_rows[pl.ds(r, 128, stride=8), :] = total


    swap(7, small.at[:, 1 - core], small_sib)
    swaps[6].wait_recv()
    products(PIECES_A[2], grad_a, z, za_sib, 0)
    swaps[7].wait_recv()
    tile = grad_a.at[:, :, :, :, pl.ds(4096, 128)]
    extra = small[:, core] + small_sib[...]
    tile[...] = (tile[...].astype(F32) + extra.reshape(4, 4, 4, 8, 128)).astype(BF16)
    sum_a.start(0, 2)
    sum_b.finish(0)
    hnow[1] = heads_come(0, moving)
    moving = heads_go(1)
    sum_a.middle(0)
    sum_b.middle(1)
    sum_a.finish(0)
    hnow[2] = heads_come(1, moving)
    moving = heads_go(2)
    sum_b.finish(1)
    sum_a.middle(1)
    sum_a.finish(1)
    sum_b.last()
    head_out[...] = heads_come(2, moving)
    sum_a.last()
    sum_a.drain()
    sum_b.drain()
    for c in list(swaps.values()) + head_sent:
        c.wait_send()


def shapes_of(phase, cols):
    return (4,) * (2 - phase) + (8, cols)


def buffers(parts):
    return [pltpu.VMEM(shapes_of(phase, n), BF16) for c0, lo, hi in parts for phase in range(3)
            for n in ((lo, hi, lo + hi, lo + hi) if phase < 2 else (lo + hi, lo + hi, lo + hi, 128))]


def backward_call(*args):
    def of(*s, t=F32):
        return jax.ShapeDtypeStruct(s, t)
    vm, hbm = pl.BlockSpec(memory_space=pltpu.VMEM), pl.BlockSpec(memory_space=pl.ANY)
    second = COLS - FIRST
    return pl.pallas_call(
        backward_kernel,
        out_shape=[of(128, 1024, t=BF16), of(128, 1024), of(8, COLS), of(8, 128)],
        in_specs=[vm] * 7 + [hbm] * 15,
        out_specs=[vm] * 4,
        scratch_shapes=[pltpu.VMEM(s, t) for s, t in zip(SAVED, KINDS)] + [
            pltpu.VMEM((1024, FIRST), BF16), pltpu.VMEM((128, FIRST), BF16), pltpu.VMEM((128, 1024), F32),
            pltpu.VMEM((128, 1536), F32), pltpu.VMEM((128, 512), F32), pltpu.VMEM((128, 1792), F32), pltpu.VMEM((128, 128), F32), pltpu.VMEM((1, 1024), F32), pltpu.VMEM((1, 1536), F32),
            pltpu.VMEM((4, 1792), F32), pltpu.VMEM((1, 1792), F32), pltpu.VMEM((16, 2, 32, 128), F32),
            pltpu.VMEM((8, 128), F32), pltpu.VMEM((4, 4, 4, 8, FIRST), BF16), pltpu.VMEM((4, 4, 4, 8, second), BF16),
            pltpu.VMEM((128, second), BF16), pltpu.VMEM((128, FIRST), BF16), pltpu.VMEM((4, 16, 32, 128), BF16),
            pltpu.VMEM((16, 32, 128), F32), pltpu.SemaphoreType.DMA((2,)), pltpu.SemaphoreType.DMA((20,)),
            pltpu.SemaphoreType.DMA((9,)), pltpu.SemaphoreType.DMA((9,)),
            pltpu.VMEM((4, 8, 128), F32), pltpu.VMEM((3, 4, 8, 128), F32),
            pltpu.SemaphoreType.DMA((3, 3)), pltpu.SemaphoreType.DMA((3, 3)),
            pltpu.SemaphoreType.DMA((2, 3, 3, 6)), pltpu.SemaphoreType.DMA((2, 3, 3, 6)),
        ] + buffers(cut3(FIRST)) + buffers(cut3(second, FIRST)),
        compiler_params=pltpu.CompilerParams(collective_id=1, has_side_effects=True, vmem_limit_bytes=62 << 20),
        name="backward",
    )(*args)


SPLIT = ("gate", "inner", "query", "keyval", "mix", "attn", "gateup", "down")


def split_kernel(grads, head, result_in, dx_in, *outs):
    outs[17][...] = result_in[...]
    outs[18][...] = dx_in[...]
    for src, dst in GATEUP:
        outs[6][:, src:src + 1024] = grads[:, dst:dst + 1024]
    for name, dst in zip(SPLIT, outs[:8]):
        if name == "gateup":
            continue
        start, n = OFF[name]
        dst[...] = grads[:, start:start + n]
    step, gin, gffn, gmix, cbias, taps, bias, decay, skip = outs[8:17]
    tile = grads[:, 4096:4224]
    step[...] = tile[:, 0:24]
    gin[...] = tile[0:1, AT_IN:AT_IN + 8]
    gffn[...] = tile[0:1, AT_FFN:AT_FFN + 8]
    gmix[...] = tile[0:1, AT_MIX:AT_MIX + 12]
    cbias[...] = tile[0:1, AT_BIAS:AT_BIAS + 14]
    taps[...] = tile[0:4, AT_TAPS:AT_TAPS + 14]
    for r, dst in enumerate((bias, decay, skip)):
        dst[...] = head[r:r + 1, 0:24]


def split_call(grads, head, result, dx):
    def of(*s):
        return jax.ShapeDtypeStruct(s, F32)
    vm = pl.BlockSpec(memory_space=pltpu.VMEM)
    return pl.pallas_call(
        split_kernel,
        out_shape=[of(8, OFF[k][1]) for k in SPLIT] + [of(8, 24), of(1, 8), of(1, 8), of(1, 12), of(1, 14), of(4, 14),
                                                       of(1, 24), of(1, 24), of(1, 24),
                                                       jax.ShapeDtypeStruct((128, 1024), BF16), of(128, 1024)],
        in_specs=[vm] * 4,
        out_specs=[vm] * 19,
        name="split",
    )(grads, head, result, dx)


def body(tokens, seq_lengths, seq_owner, input_norm, gate_proj, inner_proj, step_proj, conv_weight, conv_bias, step_bias,
         decay_log, skip_gain, mixer_norm, mixer_out, query_proj, keyval_proj, attn_out, ffn_norm, gateup_proj, down_proj,
         out_grad):
    made = forward_call(gate_proj[0], inner_proj[0], step_proj[0], conv_weight[0], conv_bias, mixer_norm, mixer_out[0].T,
                        query_proj[0], keyval_proj[0], attn_out[0].T, input_norm, ffn_norm, gateup_proj[0], down_proj[0].T,
                        tokens, out_grad, seq_lengths.reshape(1, 256), seq_owner.reshape(1, 256), step_bias, decay_log,
                        skip_gain)
    result, dx, grads, heads = backward_call(tokens, *made[1:7], made[0], made[7], made[8], *made[9:])
    (gate, inner, query, keyval, mix, attn, gateup, down, step, gin, gffn, gmix, cbias, taps, bias, decay, skip, result,
     dx) = split_call(grads, heads, result, dx)
    return (result, dx, gin, gate[None], inner[None], step[None], taps[None], cbias, bias, decay, skip, gmix, mix.T[None],
            query[None], keyval[None], attn.T[None], gffn, gateup[None], down.T[None])


def solution(mesh):
    split = Mesh(mesh.devices.reshape(4, 4, 2, mesh.shape["fsdp"]), DP_FSDP)
    rows, flat = P(DP_FSDP, None), P(None, DP_FSDP)
    weight, turned = P(None, DP_FSDP, None), P(None, None, DP_FSDP)
    in_specs = (rows, P(), P(), flat, weight, weight, weight, turned, flat, P(), P(), P(), flat, turned, weight, weight,
                turned, flat, weight, turned, rows)
    out_specs = (rows, rows, flat, weight, weight, weight, turned, flat, P(), P(), P(), flat, turned, weight, weight,
                 turned, flat, weight, turned)
    return jax.shard_map(body, mesh=split, in_specs=in_specs, out_specs=out_specs, check_vma=False)
```

```python
import functools
import math

import jax
import jax.numpy as jnp
from jax import lax
from jax.experimental import pallas as pl
from jax.experimental.pallas import tpu as pltpu
from jax.sharding import Mesh
from jax.sharding import PartitionSpec as P

EPSILON = 1e-05
ROPE_BASE = 100000000000.0
DP_FSDP = ("dp_0", "dp_1", "dp_2", "fsdp")
OFF = dict(gate=(0, 1536), inner=(1536, 1792), query=(3328, 512), keyval=(3840, 256), step=(4096, 128),
           mix=(4224, 1536), attn=(5760, 512), down=(6272, 2048), gateup=(8320, 4096))
COLS = 12416
GATEUP = ((0, 8320), (2048, 9344), (1024, 10368), (3072, 11392))
FIRST = 4224
F32, BF16 = jnp.float32, jnp.bfloat16
HIGH = lax.Precision.HIGHEST
AT_IN, AT_FFN, AT_MIX, AT_BIAS, AT_TAPS = 24, 32, 40, 52, 66
SMALLS = ((AT_IN, 8, 1024), (AT_FFN, 8, 1024), (AT_MIX, 12, 1536), (AT_BIAS, 14, 1792))
INVERSE = {8: 8192, 12: 5462, 14: 4682}


AX, AZ, AC, AY = "dp_0", "dp_1", "dp_2", "fsdp"
ORDERS = ((AX, AY, AZ), (AY, AZ, AX), (AZ, AX, AY))
MESH = pl.DeviceIdType.MESH
WHOLE = slice(None)


def places():
    return {a: lax.axis_index(a) for a in (AX, AZ, AC, AY)}


def greet_start(at):
    barrier = pltpu.get_barrier_semaphore()
    for a in (AX, AZ, AY):
        for d in (1, 2, 3):
            pl.semaphore_signal(barrier, inc=1, device_id={a: lax.rem(at[a] + d, 4)}, device_id_type=MESH)
    pl.semaphore_signal(barrier, inc=1, device_id={AC: 1 - at[AC]}, device_id_type=MESH)


def greet_end():
    pl.semaphore_wait(pltpu.get_barrier_semaphore(), 10)


def cut3(cols, start=0):
    tiles = cols // 128
    sizes = [tiles // 3 + (1 if k < tiles % 3 else 0) for k in range(3)]
    parts, at = [], start
    for n in sizes:
        lo = (n + 1) // 2 * 128
        parts.append((at, lo, n * 128 - lo))
        at += n * 128
    return parts


class Gather:
    def __init__(self, at, parts, shard, out, send, recv, sib_send, sib_recv):
        self.at, self.parts, self.shard, self.out = at, parts, shard, out
        self.sems, self.sib_sems = (send, recv), (sib_send, sib_recv)
        self.sent, self.sib, self.state = [], [], {}

    def block(self, sel, c0, n):
        return self.out.at[sel[AX], sel[AZ], self.at[AC], sel[AY], :, pl.ds(c0, n)]

    def to_sibling(self, part, k, sel, c0, n):
        ref = self.block(sel, c0, n)
        send, recv = self.sib_sems
        c = pltpu.make_async_remote_copy(ref, ref, send.at[part, k], recv.at[part, k],
                                         device_id={AC: 1 - self.at[AC]}, device_id_type=MESH)
        c.start()
        self.sib.append(c)

    def start(self, phase):
        send, recv = self.sems
        state = []
        for part, (c0, lo, hi) in enumerate(self.parts):
            order = ORDERS[part]
            a = order[phase]
            p = self.at[a]
            nxt, prv, opp = lax.rem(p + 1, 4), lax.rem(p + 3, 4), lax.rem(p + 2, 4)
            base = {b: self.at[b] for b in (AX, AZ, AY)}
            for b in order[:phase]:
                base[b] = WHOLE

            def mk(kind, q, cc, n, to, part=part, a=a, base=base):
                dst = self.block({**base, a: q}, cc, n)
                src = self.shard.at[:, pl.ds(cc, n)] if (phase == 0 and kind < 4) else dst
                return pltpu.make_async_remote_copy(src, dst, send.at[part, phase, kind], recv.at[part, phase, kind],
                                                    device_id={a: to}, device_id_type=MESH)
            if phase == 0:
                copies = [mk(k, p, c0, lo + hi, to) for k, to in enumerate((nxt, prv, opp))]
                for c in copies:
                    c.start()
                self.sent += copies
                state.append(copies)
                continue
            copies = [mk(0, p, c0, lo, nxt), mk(1, p, c0 + lo, hi, prv), mk(2, p, c0 + lo, hi, nxt), mk(3, p, c0, lo, prv)]
            for c in copies:
                c.start()
            self.sent += copies
            if phase == 2:
                self.to_sibling(part, 0, base, c0, lo + hi)
            state.append((copies, mk, nxt, prv, opp, base, a, c0, lo, hi))
        self.state[phase] = state

    def forward(self, phase):
        self.fwd = []
        for part, (copies, mk, nxt, prv, opp, base, a, c0, lo, hi) in enumerate(self.state[phase]):
            copies[0].wait_recv()
            fr = mk(4, prv, c0, lo, nxt)
            fr.start()
            copies[1].wait_recv()
            fl = mk(5, nxt, c0 + lo, hi, prv)
            fl.start()
            if phase == 2:
                self.to_sibling(part, 1, {**base, a: prv}, c0, lo)
                self.to_sibling(part, 2, {**base, a: nxt}, c0 + lo, hi)
            self.fwd.append((fr, fl))
            self.sent += [fr, fl]

    def sides(self, phase):
        for part, (copies, mk, nxt, prv, opp, base, a, c0, lo, hi) in enumerate(self.state[phase]):
            copies[2].wait_recv()
            if phase == 2:
                self.to_sibling(part, 3, {**base, a: prv}, c0 + lo, hi)
            copies[3].wait_recv()
            if phase == 2:
                self.to_sibling(part, 4, {**base, a: nxt}, c0, lo)

    def finish(self, phase):
        if phase == 0:
            for copies in self.state[0]:
                for c in copies:
                    c.wait_recv()
            return
        for part, (copies, mk, nxt, prv, opp, base, a, c0, lo, hi) in enumerate(self.state[phase]):
            fr, fl = self.fwd[part]
            fr.wait_recv()
            if phase == 2:
                self.to_sibling(part, 5, {**base, a: opp}, c0, lo)
            fl.wait_recv()
            if phase == 2:
                self.to_sibling(part, 6, {**base, a: opp}, c0 + lo, hi)

    def shared(self):
        for c in self.sib:
            c.wait_recv()

    def drain(self):
        for c in self.sent + self.sib:
            c.wait_send()


class Reduce:
    def __init__(self, at, parts, grad, first, out, bufs, send, recv):
        self.at, self.parts, self.grad, self.first, self.out, self.bufs = at, parts, grad, first, out, bufs
        self.sems, self.sent, self.state = (send, recv), [], {0: [], 1: [], 2: []}

    def start(self, phase, part):
        send, recv = self.sems
        c0, lo, hi = self.parts[part]
        order = ORDERS[part][::-1]
        a = order[phase]
        p = self.at[a]
        nxt, prv, opp = lax.rem(p + 1, 4), lax.rem(p + 3, 4), lax.rem(p + 2, 4)
        base = {b: self.at[b] for b in (AX, AZ, AY)}
        for b in order[phase + 1:]:
            base[b] = WHOLE
        el, er, fr, fl = self.bufs[(part * 3 + phase) * 4:(part * 3 + phase) * 4 + 4]

        def ref(q, cc, n):
            sel = {**base, a: q}
            return self.grad.at[sel[AX], sel[AZ], sel[AY], :, pl.ds(cc - self.first, n)]

        def mk(kind, q, cc, n, dst, to):
            return pltpu.make_async_remote_copy(ref(q, cc, n), dst, send.at[part, phase, kind],
                                                recv.at[part, phase, kind], device_id={a: to}, device_id_type=MESH)
        if phase == 2:
            now = [mk(k, q, c0, lo + hi, dst, q) for k, (q, dst) in enumerate(((nxt, el), (prv, er), (opp, fr)))]
            for c in now:
                c.start()
            self.sent += now
            self.state[2].append((now, ref(p, c0, lo + hi), (el, er, fr)))
            return
        lead = (WHOLE,) * (3 - phase)
        fr_lo, fr_hi = fr.at[lead + (pl.ds(0, lo),)], fr.at[lead + (pl.ds(lo, hi),)]
        fl_lo, fl_hi = fl.at[lead + (pl.ds(0, lo),)], fl.at[lead + (pl.ds(lo, hi),)]
        now = [mk(0, opp, c0, lo, el, prv), mk(1, opp, c0 + lo, hi, er, nxt), mk(2, prv, c0 + lo, hi, fr_hi, prv),
               mk(3, nxt, c0, lo, fl_lo, nxt)]
        for c in now:
            c.start()
        later = [mk(4, prv, c0, lo, fr_lo, prv), mk(5, nxt, c0 + lo, hi, fl_hi, nxt)]
        self.sent += now + later
        self.state[phase].append((now, later, ref(prv, c0, lo), ref(nxt, c0 + lo, hi), ref(p, c0, lo + hi), el, er, fr, fl))

    def each(self, phase, fn):
        def one(k, carry):
            fn(((k // 4, k % 4) if phase == 0 else (k,)) + (WHOLE, WHOLE))
            return carry
        lax.fori_loop(0, 16 if phase == 0 else 4, one, 0)

    def middle(self, phase):
        for now, later, left, right, own, el, er, fr, fl in self.state[phase]:
            for c, onward, target, come in ((now[0], later[0], left, el), (now[1], later[1], right, er)):
                c.wait_recv()

                def add(ix, target=target, come=come):
                    target[ix] = target[ix] + come[ix]
                self.each(phase, add)
                onward.start()

    def last(self):
        for (c0, lo, hi), (now, own, come) in zip(self.parts, self.state[2]):
            for c in now:
                c.wait_recv()
            total = own[...].astype(F32)
            for ref in come:
                total = total + ref[...].astype(F32)
            self.out[:, pl.ds(c0, lo + hi)] = total

    def finish(self, phase):
        for part, (now, later, left, right, own, el, er, fr, fl) in enumerate(self.state[phase]):
            for c in (now[2], now[3], later[0], later[1]):
                c.wait_recv()

            def total(ix, own=own, fl=fl, fr=fr):
                v = own[ix].astype(F32) + fl[ix].astype(F32) + fr[ix].astype(F32)
                own[ix] = v.astype(BF16)
            self.each(phase, total)
            self.start(phase + 1, part)

    def drain(self):
        for c in self.sent:
            c.wait_send()


def assemble(pieces, shard, tile):
    gate, inner, step, taps, cbias, mixer, mix, query, keyval, attn, gin, gffn, gateup, down = pieces
    for src, dst in GATEUP:
        shard[:, dst:dst + 1024] = gateup[:, src:src + 1024]
    for ref, (c0, n) in ((gate, OFF["gate"]), (inner, OFF["inner"]), (query, OFF["query"]), (keyval, OFF["keyval"]),
                         (mix, OFF["mix"]), (attn, OFF["attn"]), (down, OFF["down"])):
        shard[:, c0:c0 + n] = ref[...]
    tile[...] = jnp.zeros((8, 128), F32)
    tile[:, 0:24] = step[...].astype(F32)
    tile[0:1, AT_IN:AT_IN + 8] = gin[...].astype(F32)
    tile[0:1, AT_FFN:AT_FFN + 8] = gffn[...].astype(F32)
    tile[0:1, AT_MIX:AT_MIX + 12] = mixer[...].astype(F32)
    tile[0:1, AT_BIAS:AT_BIAS + 14] = cbias[...].astype(F32)
    tile[0:4, AT_TAPS:AT_TAPS + 14] = taps[...].astype(F32)
    shard[:, 4096:4224] = tile[...].astype(BF16)


def nn(a, b, precision=None):
    return lax.dot_general(a, b, (((1,), (0,)), ((), ())), preferred_element_type=F32, precision=precision)


def nt(a, b, precision=None):
    return lax.dot_general(a, b, (((1,), (1,)), ((), ())), preferred_element_type=F32, precision=precision)


def tn(a, b, precision=None):
    return lax.dot_general(a, b, (((0,), (0,)), ((), ())), preferred_element_type=F32, precision=precision)


def sigmoid(v):
    return 1.0 / (1.0 + jnp.exp(-v))


def cols_of(i, n, start=0):
    return pl.ds(pl.multiple_of(start + i * n, 128), n)


def rms_back(values, scale, gain, grad):
    inner = grad * gain
    mean = jnp.mean(values * inner, axis=-1, keepdims=True)
    return scale * inner - values * (scale * scale * scale * mean), jnp.sum(grad * values * scale, axis=0, keepdims=True)


def row_scale(values):
    return lax.rsqrt(jnp.mean(values * values, axis=-1, keepdims=True) + EPSILON)


def selectors(i, start, n):
    d = lax.broadcasted_iota(jnp.int32, (128, 128), 1) + 128 * i
    row = lax.broadcasted_iota(jnp.int32, (128, 128), 0)
    owner = lax.shift_right_logical(d * INVERSE[n], 16)
    return row == owner, row == start + d - n * owner


def spread_row(table, start, n, width, dst, row=0):
    for i in range(width // 128):
        owned, lane = selectors(i, start, n)
        v = nn(table, lane.astype(F32).astype(BF16))
        dst[row:row + 1, 128 * i:128 * i + 128] = jnp.sum(jnp.where(owned, v, 0.0), axis=0, keepdims=True)


def unspread_row(src, start, n, width, row=0):
    total = jnp.zeros((128, 128), F32)
    for i in range(width // 128):
        owned, lane = selectors(i, start, n)
        held = jnp.where(owned, src[row:row + 1, 128 * i:128 * i + 128], 0.0)
        total = total + nt(held.astype(BF16), lane.astype(F32).astype(BF16))
    return total


GROUPS = ((0, FIRST), (FIRST, 4096), (8320, 2048), (10368, 2048))
SAVED = ((128, FIRST), (128, 1792), (128, 1792), (128, 1536), (8, 128), (8, 128, 128), (128, 512), (10, 128, 128),
         (128, 1024), (128, 1024), (128, COLS - FIRST), (4096, 128))
KINDS = (F32,) * 10 + (BF16,) * 2
MADE_AGAIN = (2, 4)


def forward_kernel(*refs):
    pieces, (x_ref, og_ref, lengths, owners, sbias_ref, dlog_ref, skip_ref) = refs[:14], refs[14:21]
    w, gffn_g, gin, gmix, taps, skipx, rows_s, zb_sib, rt_sib = refs[21:30]
    kept, (proj, csum, conv, yfull, dec, soft, qr, misc, dx1_s, x1_s, zb, rt) = refs[30:42], refs[42:54]
    (wv, df_s, da_s, gffn, cbias, table, shard, tile, wsem, own_sem, keep_sem, sems, sib_sems, x_send, x_recv) = refs[54:]
    at = places()
    greet_start(at)
    assemble(pieces, shard, tile)
    greet_end()
    own = pltpu.make_async_copy(shard, w.at[at[AX], at[AZ], at[AC], at[AY]], own_sem)
    own.start()
    groups = [Gather(at, cut3(n, c0), shard, w, sems.at[0, k], sems.at[1, k], sib_sems.at[0, k], sib_sems.at[1, k])
              for k, (c0, n) in enumerate(GROUPS)]
    one, two, three, four = groups
    for g in groups:
        g.start(0)
    lane = lax.broadcasted_iota(jnp.int32, (128, 128), 1)
    sub = lax.broadcasted_iota(jnp.int32, (128, 128), 0)
    low_lanes = lane < 64

    me = ((at[AX] * 4 + at[AZ]) * 2 + at[AC]) * 4 + at[AY]
    owned = owners[...] == me
    held = jnp.where(owned, lengths[...], 0).astype(F32)
    before = lax.broadcasted_iota(jnp.int32, (256, 256), 0) <= lax.broadcasted_iota(jnp.int32, (256, 256), 1)
    ends = nn(jnp.broadcast_to(held, (8, 256)).astype(BF16), before.astype(F32).astype(BF16))[0:1, :]
    slot = lax.broadcasted_iota(jnp.int32, (128, 256), 0).astype(F32)
    closed = jnp.broadcast_to(owned.astype(F32), (128, 256)) * (jnp.broadcast_to(ends, (128, 256)) <= slot).astype(F32)
    segment = jnp.sum(closed, axis=1, keepdims=True)
    begins = jnp.max(closed * ends, axis=1, keepdims=True)
    used = jnp.max(ends, axis=1, keepdims=True)
    slots = sub.astype(F32)
    position = jnp.broadcast_to(slots[:, 0:1] - begins, (128, 128))
    active = (slots[:, 0:1] < used).astype(F32)
    segments = jnp.broadcast_to(segment, (128, 128))
    allowed = (segments == segments.T) & (sub >= lane)
    speeds = jnp.exp((lane % 32).astype(F32) * (-math.log(ROPE_BASE) * 2.0 / 64))
    angles = position * speeds
    cosine, sine = jnp.cos(angles), jnp.sin(angles)

    rows_s[...] = jnp.zeros((8, 128), F32)
    rows_s[0:1, 0:24] = sbias_ref[...].astype(F32)
    rows_s[1:2, 0:24] = dlog_ref[...].astype(F32)
    rows_s[2:3, 0:24] = skip_ref[...].astype(F32)
    sbias, dlog = rows_s[0:1, :], rows_s[1:2, :]
    heads_low = rows_s[...].astype(BF16)
    for i in range(12):
        of_head = (sub == 2 * i + lax.shift_right_logical(lane, 6)).astype(F32).astype(BF16)
        skipx[:, 128 * i:128 * i + 128] = nn(heads_low, of_head)[2:3, :]

    def halves(v):
        return jnp.where(low_lanes, v, 0.0), jnp.where(low_lanes, 0.0, v)

    def stacked(v):
        lo, hi = halves(v)
        return jnp.concatenate([lo, hi], axis=0).astype(BF16)

    own.wait()
    for g in groups:
        g.finish(0)
        g.start(1)
    for g in groups:
        g.forward(1)
    one.sides(1)
    one.finish(1)
    one.start(2)
    one.forward(2)
    two.sides(1)
    two.finish(1)
    two.start(2)
    one.sides(2)
    one.finish(2)
    two.forward(2)
    for g in (three, four):
        g.sides(1)
        g.finish(1)
        g.start(2)
    one.shared()
    rows_of_w = w.reshape(1024, COLS)

    def load(k, c0, n):
        c = pltpu.make_async_copy(rows_of_w.at[:, pl.ds(c0, n)], wv.at[:, pl.ds(c0, n)], wsem.at[k])
        c.start()
        return c
    swaps = []
    rt5 = rt.reshape(4, 16, 2, 32, 128)

    def swap(k, src, dst):
        c = pltpu.make_async_remote_copy(src, dst, x_send.at[k], x_recv.at[k], device_id={AC: 1 - at[AC]},
                                         device_id_type=MESH)
        c.start()
        swaps.append(c)

    def swap_rows(g):
        swap(g, rt5.at[g, :, 1 - at[AC]], rt_sib.at[g])

    def swap_columns(k, c0):
        swap(k, zb.at[:, pl.ds(c0, 2048)], zb_sib.at[:, pl.ds(c0, 2048)])
    load(0, 0, FIRST).wait()
    table[...] = wv[:, 4096:4224].astype(F32)
    tables = [table[pl.ds(r, 128, stride=8), :].astype(BF16) for r in range(4)]
    for dst, (start, n, width) in zip((gin, gffn, gmix, cbias), SMALLS):
        spread_row(tables[0], start, n, width, dst)
    for r in range(4):
        spread_row(tables[r], AT_TAPS, 14, 1792, taps, r)

    x = x_ref[...].astype(F32)
    h = (x * row_scale(x) * gin[...]).astype(BF16)
    rt[0:1024, :] = h.T
    g0 = og_ref[...].astype(F32) * active
    glow = g0.astype(BF16)
    rt[3072:4096, :] = glow.T
    swap_rows(0)
    swap_rows(3)
    z_h = h

    def project(i, carry):
        proj[:, cols_of(i, 384)] = nn(z_h, wv[:, cols_of(i, 384)])
        return carry
    lax.fori_loop(0, 11, project, 0)

    def convolve(i, carry):
        cs = cols_of(i, 128)
        p = proj[:, cols_of(i, 128, 1536)]
        total = p * taps[3:4, cs]
        for j in (1, 2, 3):
            moved = jnp.where(position >= float(j), pltpu.roll(p, j, axis=0), 0.0)
            total = total + moved * taps[3 - j:4 - j, cs]
        total = total + cbias[:, cs]
        csum[:, cs] = total
        conv[:, cs] = total * sigmoid(total)
        return carry
    lax.fori_loop(0, 14, convolve, 0)

    keeps = []

    def keep(*which):
        for k in which:
            c = pltpu.make_async_copy(refs[42 + k], kept[k], keep_sem.at[k])
            c.start()
            keeps.append(c)
    keep(0, 1)

    step = proj[:, 4096:4224] + sbias
    dt = jnp.maximum(step, 0.0) + jnp.log(1.0 + jnp.exp(-jnp.abs(step)))
    rate = -jnp.exp(dlog)
    lower = (sub >= lane).astype(F32)
    level = nn(lower, dt * rate, HIGH)
    dt_t = dt.T
    level_t = level.T
    b_mat = conv[:, 1536:1664]
    c_mat = conv[:, 1664:1792]
    inter = nt(c_mat, b_mat, HIGH)

    square = jnp.zeros((128, 1), F32)
    for t in range(6):
        cs = slice(128 * t, 128 * t + 128)
        mixes = []
        for n in (2 * t, 2 * t + 1):
            spread = jnp.where(allowed, level[:, n:n + 1] - level_t[n:n + 1, :], -1e30)
            decay = jnp.exp(spread)
            mixes.append((decay * inter * dt_t[n:n + 1, :]).astype(BF16))
        xs = conv[:, cs]
        y = nn(jnp.concatenate(mixes, axis=1), stacked(xs)) + skipx[:, cs] * xs
        yfull[:, cs] = y
        gate = proj[:, cs]
        gy = y * (gate * sigmoid(gate))
        square = square + jnp.sum(gy * gy, axis=1, keepdims=True)
    two.sides(2)
    two.finish(2)
    three.forward(2)
    for t in range(6, 12):
        cs = slice(128 * t, 128 * t + 128)
        mixes = []
        for n in (2 * t, 2 * t + 1):
            spread = jnp.where(allowed, level[:, n:n + 1] - level_t[n:n + 1, :], -1e30)
            decay = jnp.exp(spread)
            mixes.append((decay * inter * dt_t[n:n + 1, :]).astype(BF16))
        xs = conv[:, cs]
        y = nn(jnp.concatenate(mixes, axis=1), stacked(xs)) + skipx[:, cs] * xs
        yfull[:, cs] = y
        gate = proj[:, cs]
        gy = y * (gate * sigmoid(gate))
        square = square + jnp.sum(gy * gy, axis=1, keepdims=True)
    rmix = lax.rsqrt(square * (1.0 / 1536) + EPSILON)

    def mixer_norm(i, carry):
        cs = cols_of(i, 128)
        gate = proj[:, cs]
        gy = yfull[:, cs] * (gate * sigmoid(gate))
        zb[:, cols_of(i, 128)] = (gy * rmix * gmix[:, cs]).astype(BF16)
        return carry
    lax.fori_loop(0, 12, mixer_norm, 0)

    four.forward(2)
    keep(3)

    first = (lane % 64) < 32

    def turn(v, sign):
        side = jnp.where(first, -pltpu.roll(v, 96, axis=1), pltpu.roll(v, 32, axis=1))
        return v * cosine + sign * side * sine

    def dup(v, j):
        other = pltpu.roll(v, 64, axis=1)
        return jnp.where(low_lanes, v, other) if j == 0 else jnp.where(low_lanes, other, v)
    key_t = turn(proj[:, 3840:3968], 1.0).astype(BF16).astype(F32)
    val = proj[:, 3968:4096].astype(BF16).astype(F32)
    keys = [dup(key_t, j) for j in (0, 1)]
    vals = [dup(val, j) for j in (0, 1)]
    for t in range(4):
        cs = slice(128 * t, 128 * t + 128)
        q = turn(proj[:, 3328 + 128 * t:3456 + 128 * t], 1.0).astype(BF16).astype(F32)
        qr[:, cs] = q
        scores = nt(stacked(q), keys[t // 2].astype(BF16)) * 0.125
        weights = []
        for e in (0, 1):
            s = jnp.where(allowed, scores[128 * e:128 * e + 128], -1e30)
            w = jnp.exp(s - jnp.max(s, axis=1, keepdims=True))
            w = w / jnp.sum(w, axis=1, keepdims=True)
            soft[2 * t + e] = w
            weights.append(w.astype(BF16))
        zb[:, 1536 + 128 * t:1664 + 128 * t] = nn(jnp.concatenate(weights, axis=1), stacked(vals[t // 2])).astype(BF16)

    for k, v in enumerate((key_t, val, dt, step, inter, jnp.broadcast_to(rmix, (128, 128)), position, cosine, sine, level)):
        misc[k] = v
    keep(5, 6, 7)
    swap_columns(4, 0)
    two.shared()
    loads = [load(1, 4224, 4096)]
    three.sides(2)
    four.sides(2)
    loads[0].wait()
    for i in range(4):
        rows = slice(256 * i, 256 * i + 256)
        x1_s[:, rows] = x_ref[:, rows].astype(F32) + nt(zb[:, 0:2048], wv[rows, 4224:6272])
    x1 = x1_s[...]
    r1 = row_scale(x1)
    f = (x1 * r1 * gffn[...]).astype(BF16)
    rt[2048:3072, :] = f.T
    swap_rows(2)
    three.finish(2)

    def back_down(i, carry):
        da_s[:, cols_of(i, 512)] = nn(glow, wv[:, cols_of(i, 512, 6272)])
        return carry
    lax.fori_loop(0, 4, back_down, 0)

    four.finish(2)

    for k, g in enumerate((three, four)):
        base = 8320 + 2048 * k
        g.shared()
        pieces_of = [[load(2 + 4 * k + 2 * e + o, base + 512 * e + 1024 * o, 512) for o in (0, 1)] for e in (0, 1)]
        for i in range(4):
            if i % 2 == 0:
                for c in pieces_of[i // 2]:
                    c.wait()
            gate = nn(f, wv[:, base + 256 * i:base + 256 * i + 256])
            up = nn(f, wv[:, base + 1024 + 256 * i:base + 1280 + 256 * i])
            da = da_s[:, 1024 * k + 256 * i:1024 * k + 256 * i + 256]
            s = sigmoid(gate)
            gs = gate * s
            at_a, at_g = 2048 + 1024 * k + 256 * i, 4096 + 2048 * k + 256 * i
            zb[:, at_a:at_a + 256] = (gs * up).astype(BF16)
            zb[:, at_g:at_g + 256] = (da * up * (s + gs * (1.0 - s))).astype(BF16)
            zb[:, at_g + 1024:at_g + 1280] = (da * gs).astype(BF16)
        swap_columns(5 + k, 4096 + 2048 * k)
        if k == 1:
            swap_columns(7, 2048)
            keep(9, 10)
        for i in range(4):
            rows = slice(256 * i, 256 * i + 256)
            term = nt(zb[:, 4096 + 2048 * k:6144 + 2048 * k], wv[rows, base:base + 2048])
            df_s[:, rows] = term if k == 0 else df_s[:, rows] + term
    part, gain_grad = rms_back(x1_s[...], r1, gffn[...], df_s[...])
    gffn_g[...] = gain_grad
    dx1 = g0 + part
    dx1_s[...] = dx1
    rt[1024:2048, :] = dx1.astype(BF16).T
    swap_rows(1)
    keep(8, 11)
    for g in groups:
        g.drain()
    for c in swaps:
        c.wait()
    for c in keeps:
        c.wait()


def forward_call(*args):
    def of(*s, t=F32):
        return jax.ShapeDtypeStruct(s, t)
    vm, hbm = pl.BlockSpec(memory_space=pltpu.VMEM), pl.BlockSpec(memory_space=pl.ANY)
    return pl.pallas_call(
        forward_kernel,
        out_shape=[of(4, 4, 2, 4, 8, COLS, t=BF16), of(1, 1024), of(1, 1024), of(1, 1536),
                   of(4, 1792), of(1, 1536), of(8, 128), of(128, COLS - FIRST, t=BF16), of(4, 16, 32, 128, t=BF16)]
        + [of(*((8, 128) if k in MADE_AGAIN else s), t=t) for k, (s, t) in enumerate(zip(SAVED, KINDS))],
        in_specs=[vm] * 21,
        out_specs=[hbm] + [vm] * 6 + [hbm] * 14,
        scratch_shapes=[pltpu.VMEM(s, t) for s, t in zip(SAVED, KINDS)] + [
            pltpu.VMEM((1024, COLS), BF16), pltpu.VMEM((128, 1024), F32), pltpu.VMEM((128, 2048), F32),
            pltpu.VMEM((1, 1024), F32), pltpu.VMEM((1, 1792), F32), pltpu.VMEM((1024, 128), F32), pltpu.VMEM((8, COLS), BF16),
            pltpu.VMEM((8, 128), F32), pltpu.SemaphoreType.DMA((10,)), pltpu.SemaphoreType.DMA,
            pltpu.SemaphoreType.DMA((12,)), pltpu.SemaphoreType.DMA((2, 4, 3, 3, 6)), pltpu.SemaphoreType.DMA((2, 4, 3, 7)),
            pltpu.SemaphoreType.DMA((8,)), pltpu.SemaphoreType.DMA((8,)),
        ],
        compiler_params=pltpu.CompilerParams(collective_id=0, has_side_effects=True, vmem_limit_bytes=60 << 20),
        name="forward",
    )(*args)


PIECES_A = (((0, 0, 1280, 256), (0, 1280, 128, 128)), ((0, 1408, 1280, 256), (0, 2688, 128, 128)),
            ((0, 2816, 1280, 256), (0, 4096, 128, 128)))
PIECES_B = (((1, 4224, 2048, 256), (3, 6272, 768, 256)), ((3, 7040, 1280, 256), (2, 8320, 1280, 256), (2, 9600, 128, 128)),
            ((2, 9728, 2688, 384),))


def backward_kernel(x_ref, gffn_g, gin, gmix, taps, skipx, rows_s, w, zb_sib_in, rt_sib_in, *refs):
    kept, (result, dx, out, head_out) = refs[:12], refs[12:16]
    proj, csum, conv, yfull, dec, soft, qr, misc, dx1_s, x1_s, zb, rt = refs[16:28]
    (wv, z, df_s, dm_s, do_s, dconv, ddt_s, gin_g, gmix_g, taps_g, cbias_g, small, head_g, grad_a, grad_b, zb_sib, za_sib,
     rt_sib, small_sib, wsem, keep_sem, x_send, x_recv, hnow, hbuf, h_send, h_recv, a_sems, b_sems) = refs[28:57]
    bufs_a, bufs_b = refs[57:93], refs[93:129]
    at = places()
    greet_start(at)

    def bring(k, src, dst):
        c = pltpu.make_async_copy(src, dst, keep_sem.at[k])
        c.start()
        return c
    sides = [bring(12, kept[11], rt), bring(13, rt_sib_in, rt_sib)]
    parts_a, parts_b = cut3(FIRST), cut3(COLS - FIRST, FIRST)
    columns = []
    for part, (c0, lo, hi) in enumerate(parts_b):
        cs = pl.ds(c0 - FIRST, lo + hi)
        columns.append((bring(14 + part, kept[10].at[:, cs], zb.at[:, cs]),
                        bring(17 + part, zb_sib_in.at[:, cs], zb_sib.at[:, cs])))
    keeps = [bring(k, kept[k], refs[16 + k]) for k in range(10) if k not in MADE_AGAIN]
    rows_of_w = w.reshape(1024, COLS)
    load = pltpu.make_async_copy(rows_of_w.at[:, pl.ds(FIRST, 4096)], wv.at[:, pl.ds(0, 4096)], wsem.at[0])
    load.start()
    core = at[AC]
    rt = rt.reshape(4, 16, 2, 32, 128)
    swaps = {}

    def swap(k, src, dst):
        c = pltpu.make_async_remote_copy(src, dst, x_send.at[k], x_recv.at[k], device_id={AC: 1 - core}, device_id_type=MESH)
        c.start()
        swaps[k] = c

    def swap_columns(k, src, dst, part, first):
        c0, lo, hi = part
        cs = pl.ds(c0 - first, lo + hi)
        swap(k, src.at[:, cs], dst.at[:, cs])

    def products(pieces, grad, mine, other, first):
        for g, c0, n, width in pieces:
            left = jnp.concatenate([rt[g, :, core].reshape(512, 128), rt_sib[g].reshape(512, 128)], axis=1)

            def one(i, carry, c0=c0, width=width, left=left):
                cs = pl.ds(pl.multiple_of(c0 - first + i * width, 128), width)
                right = jnp.concatenate([mine[:, cs], other[:, cs]], axis=0)
                grad[:, :, :, :, cs] = nn(left, right).reshape(4, 4, 4, 8, width).astype(BF16)
                return carry
            lax.fori_loop(0, n // width, one, 0)

    sum_a = Reduce(at, parts_a, grad_a, 0, out, bufs_a, a_sems.at[0], a_sems.at[1])
    sum_b = Reduce(at, parts_b, grad_b, FIRST, out, bufs_b, b_sems.at[0], b_sems.at[1])
    for c in sides:
        c.wait()
    for part in range(3):
        for c in columns[part]:
            c.wait()
        products(PIECES_B[part], grad_b, zb, zb_sib, FIRST)
        if part == 0:
            greet_end()
        sum_b.start(0, part)

    axes, head_sent = (AX, AZ, AY), []

    def heads_go(k):
        a = axes[k]
        p = at[a]
        hbuf[k, p] = hnow[k]
        copies = []
        for d in (1, 2, 3):
            c = pltpu.make_async_remote_copy(hnow.at[k], hbuf.at[k, p], h_send.at[k, d - 1], h_recv.at[k, d - 1],
                                             device_id={a: lax.rem(p + d, 4)}, device_id_type=MESH)
            c.start()
            copies.append(c)
        head_sent.extend(copies)
        return copies

    def heads_come(k, copies):
        for c in copies:
            c.wait_recv()
        return ((hbuf[k, 0] + hbuf[k, 1]) + hbuf[k, 2]) + hbuf[k, 3]

    lane = lax.broadcasted_iota(jnp.int32, (128, 128), 1)
    sub = lax.broadcasted_iota(jnp.int32, (128, 128), 0)
    low_lanes = lane < 64
    def halves(v):
        return jnp.where(low_lanes, v, 0.0), jnp.where(low_lanes, 0.0, v)

    def stacked(v):
        lo, hi = halves(v)
        return jnp.concatenate([lo, hi], axis=0).astype(BF16)

    for c in keeps:
        c.wait()
    load.wait()
    blow = dx1_s[...].astype(BF16)

    def back_branch(i, carry):
        dm_s[:, cols_of(i, 512)] = nn(blow, wv[:, cols_of(i, 512)])
        return carry
    lax.fori_loop(0, 3, back_branch, 0)
    do_s[...] = nn(blow, wv[:, 1536:2048])
    for i in range(4):
        rows = slice(256 * i, 256 * i + 256)
        result[:, rows] = (x1_s[:, rows] + nt(zb[:, 2048:4096], wv[rows, 2048:4096])).astype(BF16)
    load = pltpu.make_async_copy(rows_of_w.at[:, pl.ds(0, FIRST)], wv, wsem.at[1])
    load.start()
    key_t, val, dt, step, inter, rmix, position, cosine, sine, level = [misc[k] for k in range(10)]
    rmix = rmix[:, 0:1]
    level_t = level.T
    allowed = (sub >= lane) & (lane.astype(F32) >= sub.astype(F32) - position)

    def convolved(i, carry):
        cs = cols_of(i, 128)
        total = csum[:, cs]
        conv[:, cs] = total * sigmoid(total)
        return carry
    lax.fori_loop(0, 14, convolved, 0)
    first = (lane % 64) < 32

    def turn(v, sign):
        side = jnp.where(first, -pltpu.roll(v, 96, axis=1), pltpu.roll(v, 32, axis=1))
        return v * cosine + sign * side * sine

    def dup(v, j):
        other = pltpu.roll(v, 64, axis=1)
        return jnp.where(low_lanes, v, other) if j == 0 else jnp.where(low_lanes, other, v)
    keys = [dup(key_t, j) for j in (0, 1)]
    vals = [dup(val, j) for j in (0, 1)]
    dks, dvs = [], []
    for t in range(4):
        cs = slice(128 * t, 128 * t + 128)
        do2 = stacked(do_s[:, cs])
        dp = nt(do2, vals[t // 2].astype(BF16))
        ds, ws = [], []
        for e in (0, 1):
            w = soft[2 * t + e]
            d = dp[128 * e:128 * e + 128]
            ds.append((w * (d - jnp.sum(d * w, axis=1, keepdims=True)) * 0.125).astype(BF16))
            ws.append(w.astype(BF16))
        dq = nn(jnp.concatenate(ds, axis=1), stacked(keys[t // 2]))
        z[:, 3328 + 128 * t:3456 + 128 * t] = turn(dq, -1.0).astype(BF16)
        dks.append(tn(jnp.concatenate(ds, axis=0), stacked(qr[:, cs])))
        dvs.append(tn(jnp.concatenate(ws, axis=0), do2))

    def fold(parts):
        a, b = parts[0] + parts[1], parts[2] + parts[3]
        return jnp.where(low_lanes, a + pltpu.roll(a, 64, axis=1), b + pltpu.roll(b, 64, axis=1))
    z[:, 3840:3968] = turn(fold(dks), -1.0).astype(BF16)
    z[:, 3968:4096] = fold(dvs).astype(BF16)

    dt_t = dt.T
    rate = -jnp.exp(rows_s[1:2, :])
    b_mat = conv[:, 1536:1664]
    c_mat = conv[:, 1664:1792]
    dots = jnp.zeros((128, 1), F32)
    for t in range(12):
        cs = slice(128 * t, 128 * t + 128)
        gate = proj[:, cs]
        gy = yfull[:, cs] * (gate * sigmoid(gate))
        dm = dm_s[:, cs]
        gmix_g[:, cs] = jnp.sum(dm * gy * rmix, axis=0, keepdims=True)
        dots = dots + jnp.sum(gy * dm * gmix[:, cs], axis=1, keepdims=True)
    pull = rmix * rmix * rmix * dots * (1.0 / 1536)
    ddt_s[...] = jnp.zeros((128, 128), F32)
    dlevel = jnp.zeros((128, 128), F32)
    dskip = jnp.zeros((1, 128), F32)
    lane_row = lane[0:1, :]
    dinter = jnp.zeros((128, 128), F32)
    for t in range(12):
        cs = slice(128 * t, 128 * t + 128)
        gate = proj[:, cs]
        s = sigmoid(gate)
        gs = gate * s
        y = yfull[:, cs]
        dgy = rmix * (gmix[:, cs] * dm_s[:, cs]) - y * gs * pull
        z[:, cs] = (dgy * y * (s + gs * (1.0 - s))).astype(BF16)
        dy = dgy * gs
        xs = conv[:, cs]
        skipped = jnp.sum(dy * xs, axis=0, keepdims=True)
        for e in (0, 1):
            in_head = (lane_row < 64) if e == 0 else (lane_row >= 64)
            dskip = dskip + jnp.where(lane_row == 2 * t + e,
                                      jnp.sum(jnp.where(in_head, skipped, 0.0), axis=1, keepdims=True), 0.0)
        dy2 = stacked(dy)
        dmix = nt(dy2, xs.astype(BF16))
        mixes = []
        for e in (0, 1):
            n = 2 * t + e
            dt_row = dt_t[n:n + 1, :]
            decay = jnp.exp(jnp.where(allowed, level[:, n:n + 1] - level_t[n:n + 1, :], -1e30))
            mixed = decay * inter
            dm = dmix[128 * e:128 * e + 128]
            mixes.append((mixed * dt_row).astype(BF16))
            dd = dm * dt_row
            dinter = dinter + dd * decay
            ddt_s[n:n + 1, :] = jnp.sum(dm * mixed, axis=0, keepdims=True)
            dlevel = dlevel + jnp.where(lane == n, jnp.sum(dd * mixed, axis=1, keepdims=True), 0.0)
        dconv[:, cs] = tn(jnp.concatenate(mixes, axis=0), dy2) + skipx[:, cs] * dy
    sum_b.middle(0)
    dconv[:, 1536:1664] = tn(dinter, c_mat, HIGH)
    dconv[:, 1664:1792] = nn(dinter, b_mat, HIGH)
    ddt = ddt_s[...].T
    dlevel = dlevel - ddt * dt
    upper = (sub <= lane).astype(F32)
    drate = nn(upper, dlevel, HIGH)
    dstep = jnp.where(lane < 24, (ddt + drate * rate) * sigmoid(step), 0.0)
    z[:, 4096:4224] = dstep.astype(BF16)
    head_g[...] = jnp.zeros((8, 128), F32)
    head_g[2:3, :] = dskip
    head_g[0:1, :] = jnp.sum(dstep, axis=0, keepdims=True)
    head_g[1:2, :] = jnp.sum(drate * dt * rate, axis=0, keepdims=True)

    def unconvolve(i, carry):
        cs = cols_of(i, 128)
        total = csum[:, cs]
        s = sigmoid(total)
        d = dconv[:, cs] * (s + total * s * (1.0 - s))
        p = proj[:, cols_of(i, 128, 1536)]
        cbias_g[:, cs] = jnp.sum(d, axis=0, keepdims=True)
        taps_g[3:4, cs] = jnp.sum(d * p, axis=0, keepdims=True)
        back = d * taps[3:4, cs]
        for j in (1, 2, 3):
            masked = jnp.where(position >= float(j), d, 0.0)
            taps_g[3 - j:4 - j, cs] = jnp.sum(masked * pltpu.roll(p, j, axis=0), axis=0, keepdims=True)
            back = back + pltpu.roll(masked, 128 - j, axis=0) * taps[3 - j:4 - j, cs]
        z[:, cols_of(i, 128, 1536)] = back.astype(BF16)
        return carry
    lax.fori_loop(0, 14, unconvolve, 0)

    for part in range(3):
        swap_columns(4 + part, z, za_sib, parts_a[part], 0)
    swap(8, head_g, hnow.at[3])
    for part in range(2):
        swaps[4 + part].wait_recv()
        products(PIECES_A[part], grad_a, z, za_sib, 0)
        sum_a.start(0, part)
    swaps[8].wait_recv()
    hnow[0] = head_g[...] + hnow[3]
    moving = heads_go(0)
    load.wait()
    for i in range(4):
        rows = slice(256 * i, 256 * i + 256)
        df_s[:, rows] = nt(z[:, 0:FIRST], wv[rows, 0:FIRST])
    x = x_ref[...].astype(F32)
    part, gain_grad = rms_back(x, row_scale(x), gin[...], df_s[...])
    gin_g[...] = gain_grad
    dx[...] = dx1_s[...] + part

    small_rows = small.reshape(1024, 128)
    small_rows[...] = jnp.zeros((1024, 128), F32)
    for r in range(4):
        total = unspread_row(taps_g, AT_TAPS, 14, 1792, r)
        if r == 0:
            for src, (start, n, width) in zip((gin_g, gffn_g, gmix_g, cbias_g), SMALLS):
                total = total + unspread_row(src, start, n, width)
        small_rows[pl.ds(r, 128, stride=8), :] = total


    swap(7, small.at[:, 1 - core], small_sib)
    swaps[6].wait_recv()
    products(PIECES_A[2], grad_a, z, za_sib, 0)
    swaps[7].wait_recv()
    tile = grad_a.at[:, :, :, :, pl.ds(4096, 128)]
    extra = small[:, core] + small_sib[...]
    tile[...] = (tile[...].astype(F32) + extra.reshape(4, 4, 4, 8, 128)).astype(BF16)
    sum_a.start(0, 2)
    sum_b.finish(0)
    hnow[1] = heads_come(0, moving)
    moving = heads_go(1)
    sum_a.middle(0)
    sum_b.middle(1)
    sum_a.finish(0)
    hnow[2] = heads_come(1, moving)
    moving = heads_go(2)
    sum_b.finish(1)
    sum_a.middle(1)
    sum_a.finish(1)
    sum_b.last()
    head_out[...] = heads_come(2, moving)
    sum_a.last()
    sum_a.drain()
    sum_b.drain()
    for c in list(swaps.values()) + head_sent:
        c.wait_send()


def shapes_of(phase, cols):
    return (4,) * (2 - phase) + (8, cols)


def buffers(parts):
    return [pltpu.VMEM(shapes_of(phase, n), BF16) for c0, lo, hi in parts for phase in range(3)
            for n in ((lo, hi, lo + hi, lo + hi) if phase < 2 else (lo + hi, lo + hi, lo + hi, 128))]


def backward_call(*args):
    def of(*s, t=F32):
        return jax.ShapeDtypeStruct(s, t)
    vm, hbm = pl.BlockSpec(memory_space=pltpu.VMEM), pl.BlockSpec(memory_space=pl.ANY)
    second = COLS - FIRST
    return pl.pallas_call(
        backward_kernel,
        out_shape=[of(128, 1024, t=BF16), of(128, 1024), of(8, COLS), of(8, 128)],
        in_specs=[vm] * 7 + [hbm] * 15,
        out_specs=[vm] * 4,
        scratch_shapes=[pltpu.VMEM(s, t) for s, t in zip(SAVED, KINDS)] + [
            pltpu.VMEM((1024, FIRST), BF16), pltpu.VMEM((128, FIRST), BF16), pltpu.VMEM((128, 1024), F32),
            pltpu.VMEM((128, 1536), F32), pltpu.VMEM((128, 512), F32), pltpu.VMEM((128, 1792), F32), pltpu.VMEM((128, 128), F32), pltpu.VMEM((1, 1024), F32), pltpu.VMEM((1, 1536), F32),
            pltpu.VMEM((4, 1792), F32), pltpu.VMEM((1, 1792), F32), pltpu.VMEM((16, 2, 32, 128), F32),
            pltpu.VMEM((8, 128), F32), pltpu.VMEM((4, 4, 4, 8, FIRST), BF16), pltpu.VMEM((4, 4, 4, 8, second), BF16),
            pltpu.VMEM((128, second), BF16), pltpu.VMEM((128, FIRST), BF16), pltpu.VMEM((4, 16, 32, 128), BF16),
            pltpu.VMEM((16, 32, 128), F32), pltpu.SemaphoreType.DMA((2,)), pltpu.SemaphoreType.DMA((20,)),
            pltpu.SemaphoreType.DMA((9,)), pltpu.SemaphoreType.DMA((9,)),
            pltpu.VMEM((4, 8, 128), F32), pltpu.VMEM((3, 4, 8, 128), F32),
            pltpu.SemaphoreType.DMA((3, 3)), pltpu.SemaphoreType.DMA((3, 3)),
            pltpu.SemaphoreType.DMA((2, 3, 3, 6)), pltpu.SemaphoreType.DMA((2, 3, 3, 6)),
        ] + buffers(cut3(FIRST)) + buffers(cut3(second, FIRST)),
        compiler_params=pltpu.CompilerParams(collective_id=1, has_side_effects=True, vmem_limit_bytes=62 << 20),
        name="backward",
    )(*args)


SPLIT = ("gate", "inner", "query", "keyval", "mix", "attn", "gateup", "down")


def split_kernel(grads, head, result_in, dx_in, *outs):
    outs[17][...] = result_in[...]
    outs[18][...] = dx_in[...]
    for src, dst in GATEUP:
        outs[6][:, src:src + 1024] = grads[:, dst:dst + 1024]
    for name, dst in zip(SPLIT, outs[:8]):
        if name == "gateup":
            continue
        start, n = OFF[name]
        dst[...] = grads[:, start:start + n]
    step, gin, gffn, gmix, cbias, taps, bias, decay, skip = outs[8:17]
    tile = grads[:, 4096:4224]
    step[...] = tile[:, 0:24]
    gin[...] = tile[0:1, AT_IN:AT_IN + 8]
    gffn[...] = tile[0:1, AT_FFN:AT_FFN + 8]
    gmix[...] = tile[0:1, AT_MIX:AT_MIX + 12]
    cbias[...] = tile[0:1, AT_BIAS:AT_BIAS + 14]
    taps[...] = tile[0:4, AT_TAPS:AT_TAPS + 14]
    for r, dst in enumerate((bias, decay, skip)):
        dst[...] = head[r:r + 1, 0:24]


def split_call(grads, head, result, dx):
    def of(*s):
        return jax.ShapeDtypeStruct(s, F32)
    vm = pl.BlockSpec(memory_space=pltpu.VMEM)
    return pl.pallas_call(
        split_kernel,
        out_shape=[of(8, OFF[k][1]) for k in SPLIT] + [of(8, 24), of(1, 8), of(1, 8), of(1, 12), of(1, 14), of(4, 14),
                                                       of(1, 24), of(1, 24), of(1, 24),
                                                       jax.ShapeDtypeStruct((128, 1024), BF16), of(128, 1024)],
        in_specs=[vm] * 4,
        out_specs=[vm] * 19,
        name="split",
    )(grads, head, result, dx)


def body(tokens, seq_lengths, seq_owner, input_norm, gate_proj, inner_proj, step_proj, conv_weight, conv_bias, step_bias,
         decay_log, skip_gain, mixer_norm, mixer_out, query_proj, keyval_proj, attn_out, ffn_norm, gateup_proj, down_proj,
         out_grad):
    made = forward_call(gate_proj[0], inner_proj[0], step_proj[0], conv_weight[0], conv_bias, mixer_norm, mixer_out[0].T,
                        query_proj[0], keyval_proj[0], attn_out[0].T, input_norm, ffn_norm, gateup_proj[0], down_proj[0].T,
                        tokens, out_grad, seq_lengths.reshape(1, 256), seq_owner.reshape(1, 256), step_bias, decay_log,
                        skip_gain)
    result, dx, grads, heads = backward_call(tokens, *made[1:7], made[0], made[7], made[8], *made[9:])
    (gate, inner, query, keyval, mix, attn, gateup, down, step, gin, gffn, gmix, cbias, taps, bias, decay, skip, result,
     dx) = split_call(grads, heads, result, dx)
    return (result, dx, gin, gate[None], inner[None], step[None], taps[None], cbias, bias, decay, skip, gmix, mix.T[None],
            query[None], keyval[None], attn.T[None], gffn, gateup[None], down.T[None])


def solution(mesh):
    split = Mesh(mesh.devices.reshape(4, 4, 2, mesh.shape["fsdp"]), DP_FSDP)
    rows, flat = P(DP_FSDP, None), P(None, DP_FSDP)
    weight, turned = P(None, DP_FSDP, None), P(None, None, DP_FSDP)
    in_specs = (rows, P(), P(), flat, weight, weight, weight, turned, flat, P(), P(), P(), flat, turned, weight, weight,
                turned, flat, weight, turned, rows)
    out_specs = (rows, rows, flat, weight, weight, weight, turned, flat, P(), P(), P(), flat, turned, weight, weight,
                 turned, flat, weight, turned)
    return jax.shard_map(body, mesh=split, in_specs=in_specs, out_specs=out_specs, check_vma=False)
```
